32 devices in a mesh: img: 8 (over y, x, core), seq: 4 (over z).
Axes of the slice: x: 2, y: 2, z: 4, core: 2. Of those that a mesh axis runs over, the one named last changes fastest.
Arguments:
- tokens: bfloat16 [8192, 1152], P(('img', 'seq')), may hold values from -6 to 6
- cotangent: bfloat16 [8192, 1152], P(('img', 'seq')), may hold values from -6 to 6
- image_lengths: int32 [8, 2], P('img'), may hold values from 1 to 729, 1024 in all within a row
- qkv_weight: bfloat16 [2, 1152, 3456], P(None, ('img', 'seq')), may hold values from -0.1875 to 0.1875
- out_weight: bfloat16 [2, 1152, 1152], P(None, ('img', 'seq')), may hold values from -3 to 3
- up_weight: bfloat16 [2, 1152, 4304], P(None, ('img', 'seq')), may hold values from -0.1875 to 0.1875
- down_weight: bfloat16 [2, 1152, 4304], P(None, ('img', 'seq')), may hold values from -0.09375 to 0.09375
- up_bias: bfloat16 [2, 4304], replicated, may hold values from -3 to 3
- norm_scale: bfloat16 [2, 1152, 2], P(None, ('img', 'seq')), may hold values from 0.5 to 1.5
- shifts: bfloat16 [2, 1152, 6], P(None, ('img', 'seq')), may hold values from -3 to 3
Outputs:
- output: float32 [8192, 1152], P(('img', 'seq'))
- tokens_grad: float32 [8192, 1152], P(('img', 'seq'))
- qkv_grad: float32 [2, 1152, 3456], P(None, ('img', 'seq'))
- out_grad: float32 [2, 1152, 1152], P(None, ('img', 'seq'))
- up_grad: float32 [2, 1152, 4304], P(None, ('img', 'seq'))
- down_grad: float32 [2, 1152, 4304], P(None, ('img', 'seq'))
- up_bias_grad: float32 [2, 4304], replicated
- norm_scale_grad: float32 [2, 1152, 2], P(None, ('img', 'seq'))
- shifts_grad: float32 [2, 1152, 6], P(None, ('img', 'seq'))
The draws below stay inside these ranges and needn't reach their ends.
Inputs may be any that keep to these rules, and one draw needn't show every extreme that they name: `image_lengths`: row g lists the lengths of the 2 images packed in order into the 1024 rows of group g; each row sums to 1024, and no image has more than 729 tokens.
All inputs are finite; a program needn't handle non-finite values.
Results may differ from the reference program's by a relative error of at most 0.012.
Values may be sent and summed in bfloat16 or wider, within the bound.
No kernel may reach another device: no remote copies, remote signals or barrier semaphores. Data moves between devices by JAX's collectives and lax.ppermute only.
A program may use at most 448 MiB of HBM per device.

```python
import math
import jax
import jax.numpy as jnp
import numpy as np
from jax import lax

D = 1152
HEADS = 16
FF = 4304
LAYERS = 2
IMG_AVG = 512
IMG_MAX = 729
GROUP_ROWS = 1024
IMGS = 2
GROUPS = 8
TOKENS = 8192


def steps_of(key, extent, shards, low, largest):
    factor_of = 1.0
    for position, parts in shards:
        draws = jax.random.uniform(jax.random.fold_in(jax.random.fold_in(key, 6), position), (parts,), jnp.float32, low / len(shards), largest / len(shards))
        factor_of = factor_of * jnp.repeat(jnp.exp(draws), extent[position] // parts).reshape((-1,) + (1,) * (len(extent) - 1 - position))
    return factor_of


def length_profile(count, total, reach, lean):
    portions = [(1 << 20) // math.isqrt(standing ** lean) + 1 for standing in range(2, count + 1)]
    spare, counts = total - reach - (count - 1), [1] * (count - 1)
    while spare > 0:
        candidates = [i for i in range(count - 1) if counts[i] < reach]
        mass, budget = sum([portions[i] for i in candidates]), spare
        for i in candidates:
            more = min(reach - counts[i], max(1, budget * portions[i] // mass), spare)
            counts[i] = counts[i] + more
            spare = spare - more
    return np.array([reach] + counts)


def uneven(rng, amount, total, most, slope):
    if amount == 2:
        one = jax.random.randint(rng, (), max(1, total - most), min(most, total - 1) + 1)
        return jnp.stack([one, total - one])
    tallies = jnp.asarray(length_profile(amount, total, most, slope), jnp.int32)
    twos = (amount - 1) // 2
    donor, sink = tallies[1:1 + 2 * twos:2], tallies[2:2 + 2 * twos:2]
    margin = jnp.minimum(donor - 1, most - sink)
    moved = jax.random.randint(jax.random.fold_in(rng, 1), (twos,), 0, 1 << 20) % (margin + 1)
    tallies = tallies.at[1:1 + 2 * twos:2].set(donor - moved).at[2:2 + 2 * twos:2].set(sink + moved)
    return tallies[jax.random.permutation(jax.random.fold_in(rng, 2), amount)]


def scatter_about(own_key, extent, spread, limit, pieces=(), kind=jnp.bfloat16):
    values = spread * jax.random.normal(own_key, extent, jnp.float32)
    if pieces:
        values = values * steps_of(own_key, extent, pieces, -0.22, 0.18)
    return jnp.clip(values, -limit, limit).astype(kind)


def setup_inputs(seed: int = 0) -> dict:
    key_list = jax.random.split(jax.random.key(seed), 11)
    return {
        "tokens": scatter_about(key_list[0], (TOKENS, D), 1.0, 6.0, ((0, 32),)),
        "cotangent": scatter_about(key_list[1], (TOKENS, D), 1.0, 6.0, ((0, 32),)),
        "image_lengths": jax.vmap(lambda own: uneven(own, IMGS, GROUP_ROWS, IMG_MAX, 1))(jax.random.split(key_list[2], GROUPS)).reshape((GROUPS, IMGS)).astype(jnp.int32),
        "qkv_weight": scatter_about(key_list[3], (LAYERS, D, 3 * D), D ** -0.5, 0.1875, ((1, 32),)),
        "out_weight": scatter_about(key_list[4], (LAYERS, D, D), (2 * D // IMG_AVG) ** -0.5, 3.0, ((1, 32),)),
        "up_weight": scatter_about(key_list[5], (LAYERS, D, FF), D ** -0.5, 0.1875, ((1, 32),)),
        "down_weight": scatter_about(key_list[6], (LAYERS, D, FF), FF ** -0.5, 0.09375, ((1, 32),)),
        "up_bias": scatter_about(key_list[7], (LAYERS, FF), 0.5, 3.0),
        "norm_scale": jnp.clip(1.0 + 0.1 * jax.random.normal(key_list[8], (LAYERS, D, 2), jnp.float32), 0.5, 1.5).astype(jnp.bfloat16),
        "shifts": scatter_about(key_list[9], (LAYERS, D, 6), 0.5, 3.0, ((1, 32),)),
    }


@jax.custom_vjp
def low(v):
    return lax.optimization_barrier(v.astype(jnp.bfloat16)).astype(jnp.float32)

@jax.custom_vjp
def low_back(v):
    return v

def low_keep(v):
    return (low(v), None)

def low_pass(kept, grad):
    return (grad,)

def back_keep(v):
    return (v, None)

def back_low(kept, grad):
    return (low(grad),)
low.defvjp(low_keep, low_pass)
low_back.defvjp(back_keep, back_low)
EPSILON = 1e-06
NEGATIVE = -1e+30

def normalize(inputs, gain, offset):
    centred = inputs - lax.optimization_barrier(jnp.mean(inputs, axis=-1, keepdims=True))
    variance = lax.optimization_barrier(jnp.mean(centred * centred, axis=-1, keepdims=True))
    return centred * lax.rsqrt(variance + EPSILON) * gain + offset

def matmul(left, right):
    return jnp.dot(left, right, precision=lax.Precision.HIGHEST, preferred_element_type=jnp.float32)

def image_ids(image_lengths):
    finish = jnp.cumsum(image_lengths, axis=1).astype(jnp.int32)
    positions = jnp.arange(GROUP_ROWS, dtype=jnp.int32)
    return lax.optimization_barrier(jnp.sum((positions[None, :, None] >= finish[:, None, :]).astype(jnp.int32), axis=2))

def group_attention(queries, key_rows, value_rows, group_ids):
    row_count = queries.shape[0]
    head_dim = D // HEADS
    query_heads = queries.reshape(row_count, HEADS, head_dim)
    key_heads = key_rows.reshape(row_count, HEADS, head_dim)
    value_heads = value_rows.reshape(row_count, HEADS, head_dim)
    scores = jnp.einsum('qhd,khd->hqk', query_heads, key_heads, precision=lax.Precision.HIGHEST) * head_dim ** (-0.5)
    scores = low_back(scores)
    same = (group_ids[:, None] == group_ids[None, :])[None]
    probs = low(jax.nn.softmax(jnp.where(same, scores, NEGATIVE), axis=-1))
    attended = jnp.einsum('hqk,khd->qhd', probs, value_heads, precision=lax.Precision.HIGHEST)
    return attended.reshape(row_count, D)
checked_attention = jax.checkpoint(group_attention)

def attend_group(packed):
    return checked_attention(packed[0], packed[1], packed[2], packed[3])

def forward(tokens, qkv_weight, out_weight, up_weight, down_weight, up_bias, norm_scale, shifts, group_ids):
    current = tokens
    for layer_index in range(LAYERS):
        gains = norm_scale[layer_index]
        offsets = shifts[layer_index]
        attn_in = low(normalize(current, gains[:, 0], offsets[:, 0]))
        qkv_bias = jnp.concatenate([offsets[:, 1], jnp.zeros((D,), jnp.float32), offsets[:, 2]])
        mixed = low(low_back(matmul(attn_in, qkv_weight[layer_index]) + qkv_bias))
        shaped = mixed.reshape(GROUPS, GROUP_ROWS, 3 * D)
        attended = lax.map(attend_group, (shaped[:, :, :D], shaped[:, :, D:2 * D], shaped[:, :, 2 * D:], group_ids))
        attended = low(low_back(attended.reshape(TOKENS, D)))
        after_attn = current + low_back(matmul(attended, out_weight[layer_index]) + offsets[:, 3])
        mlp_in = low(normalize(after_attn, gains[:, 1], offsets[:, 4]))
        hidden = low_back(matmul(mlp_in, up_weight[layer_index]) + up_bias[layer_index])
        activated = low(jax.nn.gelu(hidden, approximate=True))
        current = after_attn + low_back(matmul(activated, down_weight[layer_index].T) + offsets[:, 5])
    return current

def reference(tokens, cotangent, image_lengths, qkv_weight, out_weight, up_weight, down_weight, up_bias, norm_scale, shifts):
    group_ids = image_ids(image_lengths)

    def run(*params):
        return forward(*params, group_ids)
    inputs = tuple((argument.astype(jnp.float32) for argument in (tokens, qkv_weight, out_weight, up_weight, down_weight, up_bias, norm_scale, shifts)))
    output, pullback = jax.vjp(run, *inputs)
    grads = pullback(cotangent.astype(jnp.float32))
    return (output, grads[0], grads[1], grads[2], grads[3], grads[4], grads[5], grads[6], grads[7])
```

```python
import functools
import math

import jax
import jax.numpy as jnp
from jax import lax
from jax.experimental import pallas as pl
from jax.experimental.pallas import tpu as pltpu
from jax.sharding import Mesh
from jax.sharding import PartitionSpec as P

HEADS = 16
RANKS = 4
EPSILON = 1e-06
NEGATIVE = -1e30
AXES = ("hi", "x", "c", "seq")
SWAP = ((0, 1), (1, 0))
bf16, f32 = jnp.bfloat16, jnp.float32


def attend_kernel(heads, dim, offset, qid_ref, kid_ref, q_ref, kv_ref, o_ref):
    factor = dim**-0.5 * math.log2(math.e)
    same = qid_ref[...] == kid_ref[...]
    width = heads * dim
    outs = []
    for h in range(heads):
        lo, hi = h * dim, (h + 1) * dim
        q = q_ref[:, lo:hi]
        k = kv_ref[:, offset + lo : offset + hi]
        v = kv_ref[:, offset + width + lo : offset + width + hi]
        s = lax.dot_general(q, k, (((1,), (1,)), ((), ())), preferred_element_type=f32)
        s = jnp.where(same, s, NEGATIVE)
        top = jnp.max(s, axis=1, keepdims=True)
        p = jnp.exp2((s - top) * factor)
        total = jnp.sum(p, axis=1, keepdims=True)
        o = jnp.dot(p.astype(bf16), v, preferred_element_type=f32)
        outs.append(o / total)
    o_ref[...] = jnp.concatenate(outs, axis=1).astype(o_ref.dtype)


def attend(qkv, kv, offset, query_ids, key_ids, heads, dim):
    rows, keys, width = qkv.shape[0], kv.shape[0], heads * dim
    block = min(rows, 512 * 1024 // keys)
    return pl.pallas_call(
        functools.partial(attend_kernel, heads, dim, offset),
        grid=(rows // block,),
        in_specs=[
            pl.BlockSpec((block, 1), lambda i: (i, 0)),
            pl.BlockSpec((1, keys), lambda i: (0, 0)),
            pl.BlockSpec((block, qkv.shape[1]), lambda i: (i, 0)),
            pl.BlockSpec(kv.shape, lambda i: (0, 0)),
        ],
        out_specs=pl.BlockSpec((block, width), lambda i: (i, 0)),
        out_shape=jax.ShapeDtypeStruct((rows, width), bf16),
        compiler_params=pltpu.CompilerParams(vmem_limit_bytes=48 * 2**20),
        cost_estimate=pl.CostEstimate(
            flops=4 * rows * keys * width,
            bytes_accessed=8 * rows * width,
            transcendentals=heads * rows * keys,
        ),
    )(query_ids[:, None], key_ids[None, :], qkv, kv)


def attend_back_kernel(
    heads, dim, offset, qid_ref, kid_ref, q_ref, kv_ref, do_ref, dq_ref, dkv_ref, dk_sum, dv_sum
):
    scale = dim**-0.5
    factor = scale * math.log2(math.e)
    step = pl.program_id(0)

    @pl.when(step == 0)
    def _():
        dk_sum[...] = jnp.zeros_like(dk_sum)
        dv_sum[...] = jnp.zeros_like(dv_sum)

    same = kid_ref[...] == qid_ref[...]
    width = heads * dim
    dqs = []
    for h in range(heads):
        lo, hi = h * dim, (h + 1) * dim
        q = q_ref[:, lo:hi]
        do = do_ref[:, lo:hi]
        k = kv_ref[:, offset + lo : offset + hi]
        v = kv_ref[:, offset + width + lo : offset + width + hi]
        s = lax.dot_general(k, q, (((1,), (1,)), ((), ())), preferred_element_type=f32)
        s = jnp.where(same, s, NEGATIVE)
        top = jnp.max(s, axis=0, keepdims=True)
        p = jnp.exp2((s - top) * factor)
        p = p * (1.0 / jnp.sum(p, axis=0, keepdims=True))
        dp = lax.dot_general(v, do, (((1,), (1,)), ((), ())), preferred_element_type=f32)
        delta = jnp.sum(p * dp, axis=0, keepdims=True)
        ds = (p * (dp - delta)).astype(bf16)
        dv_sum[h] += jnp.dot(p.astype(bf16), do, preferred_element_type=f32)
        dk_sum[h] += jnp.dot(ds, q, preferred_element_type=f32)
        dq = lax.dot_general(ds, k, (((0,), (0,)), ((), ())), preferred_element_type=f32)
        dqs.append(dq * scale)
    dq_ref[...] = jnp.concatenate(dqs, axis=1).astype(dq_ref.dtype)

    @pl.when(step == pl.num_programs(0) - 1)
    def _():
        parts = [dk_sum[h] * scale for h in range(heads)] + [dv_sum[h] for h in range(heads)]
        dkv_ref[...] = jnp.concatenate(parts, axis=1).astype(dkv_ref.dtype)


def attend_back(qkv, kv, offset, query_ids, key_ids, grad, heads, dim):
    rows, keys, width = qkv.shape[0], kv.shape[0], heads * dim
    block = min(rows, 512 * 1024 // keys)
    return pl.pallas_call(
        functools.partial(attend_back_kernel, heads, dim, offset),
        grid=(rows // block,),
        in_specs=[
            pl.BlockSpec((1, block), lambda i: (0, i)),
            pl.BlockSpec((keys, 1), lambda i: (0, 0)),
            pl.BlockSpec((block, qkv.shape[1]), lambda i: (i, 0)),
            pl.BlockSpec(kv.shape, lambda i: (0, 0)),
            pl.BlockSpec((block, width), lambda i: (i, 0)),
        ],
        out_specs=[
            pl.BlockSpec((block, width), lambda i: (i, 0)),
            pl.BlockSpec((keys, 2 * width), lambda i: (0, 0)),
        ],
        out_shape=[
            jax.ShapeDtypeStruct((rows, width), bf16),
            jax.ShapeDtypeStruct((keys, 2 * width), bf16),
        ],
        scratch_shapes=[pltpu.VMEM((heads, keys, dim), f32)] * 2,
        compiler_params=pltpu.CompilerParams(vmem_limit_bytes=56 * 2**20),
        cost_estimate=pl.CostEstimate(
            flops=10 * rows * keys * width,
            bytes_accessed=20 * rows * width,
            transcendentals=heads * rows * keys,
        ),
    )(query_ids[None, :], key_ids[:, None], qkv, kv, grad)


def dot(left, right, kind=f32):
    return jnp.dot(left, right, preferred_element_type=f32).astype(kind)


def dot_last(left, right, kind=f32):
    dims = (((1,), (1,)), ((), ()))
    return lax.dot_general(left, right, dims, preferred_element_type=f32).astype(kind)


def dot_rows(left, right, kind=f32):
    dims = (((0,), (0,)), ((), ()))
    return lax.dot_general(left, right, dims, preferred_element_type=f32).astype(kind)


def pick(array, index, axis=0):
    return lax.dynamic_index_in_dim(array, index, axis, keepdims=False)


def standardize(v):
    centred = v - jnp.mean(v, axis=-1, keepdims=True)
    scale = lax.rsqrt(jnp.mean(centred * centred, axis=-1, keepdims=True) + EPSILON)
    return centred * scale, scale


def norm(v, gain, offset):
    return standardize(v)[0] * gain + offset


def norm_back(v, gain, t):
    n, scale = standardize(v)
    w = t * gain
    mean_w = jnp.mean(w, axis=-1, keepdims=True)
    mean_wn = jnp.mean(w * n, axis=-1, keepdims=True)
    grad = scale * (w - mean_w - n * mean_wn)
    return grad, jnp.sum(t * n, axis=0), jnp.sum(t, axis=0)


def gelu_tanh(v):
    return jax.nn.gelu(v, approximate=True)


def swap_x(v):
    return lax.ppermute(v, "x", SWAP)


def swap_c(v):
    return lax.ppermute(v, "c", SWAP)


def x_order(own, other):
    first = lax.axis_index("x") == 0
    return jnp.where(first, own, other), jnp.where(first, other, own)


def exchange(blocks):
    xi, ci = lax.axis_index("x"), lax.axis_index("c")
    blocks = blocks.reshape((2, 2) + blocks.shape[1:])
    mine = pick(blocks, xi)
    theirs = swap_x(pick(blocks, 1 - xi))
    ahead, behind = x_order(mine, theirs)
    both = jnp.stack([ahead, behind])
    kept = pick(both, ci, 1)
    come = swap_c(pick(both, 1 - ci, 1))
    first = ci == 0
    out = jnp.stack([jnp.where(first, kept, come), jnp.where(first, come, kept)], axis=1)
    return out.reshape((RANKS,) + blocks.shape[2:])


def gather_rows(payload):
    size = lax.axis_size("hi")
    place = lax.axis_index("hi")
    full = lax.all_gather(payload, "seq", axis=0, tiled=True)[None]
    step = 1
    while step < size:
        come = lax.ppermute(full, "hi", [(i, i ^ step) for i in range(size)])
        low = (place & step) == 0
        full = jnp.concatenate([jnp.where(low, full, come), jnp.where(low, come, full)])
        step *= 2
    return full.reshape((-1,) + payload.shape[1:])


def scatter_rows(terms):
    size = lax.axis_size("hi")
    place = lax.axis_index("hi")
    step = size // 2
    while step:
        halves = terms.reshape((2, -1) + terms.shape[1:])
        bit = (place // step) % 2
        come = lax.ppermute(pick(halves, 1 - bit), "hi", [(i, i ^ step) for i in range(size)])
        terms = (pick(halves, bit).astype(f32) + come.astype(f32)).astype(terms.dtype)
        step //= 2
    return lax.psum_scatter(terms, "seq", scatter_dimension=0, tiled=True)


def sum_everywhere(v):
    for axis in AXES[::-1]:
        size = lax.axis_size(axis)
        step = 1
        while step < size:
            v = v + lax.ppermute(v, axis, [(i, i ^ step) for i in range(size)])
            step *= 2
    return v


def body(
    tokens,
    cotangent,
    image_lengths,
    qkv_weight,
    out_weight,
    up_weight,
    down_weight,
    up_bias,
    norm_scale,
    shifts,
):
    rows, width = tokens.shape
    layers, held = qkv_weight.shape[0], qkv_weight.shape[1]
    blocks, seqs = lax.axis_size("hi"), lax.axis_size("seq")
    ways = seqs // RANKS
    shards = blocks * seqs
    chunk = seqs * held
    heads = HEADS // RANKS
    dim = width // HEADS
    part = width // RANKS
    ff = up_weight.shape[2]
    ff_part = ff // RANKS
    ff_pad = -(-ff_part // 128) * 128
    assert ff_pad % shards == 0
    xi, ci = lax.axis_index("x"), lax.axis_index("c")
    rank = 2 * xi + ci

    def mixed_order(v):
        lead = v.shape[:-1]
        v = v.reshape(lead + (blocks, RANKS, seqs, held))
        return jnp.swapaxes(v, -3, -2).reshape(lead + (width,))

    def plain_order(v):
        lead = v.shape[:-1]
        v = v.reshape(lead + (blocks, seqs, RANKS, held))
        return jnp.swapaxes(v, -3, -2).reshape(lead + (width,))

    def mine(v):
        return pick(v.reshape(blocks, seqs, RANKS, held), rank, 2).reshape(part)

    there = []
    for b in range(blocks):
        for r in range(RANKS):
            for s in range(seqs):
                target = (b * RANKS + s % RANKS) * seqs + r * ways + s // RANKS
                there.append(((b * RANKS + r) * seqs + s, target))
    back = [(target, source) for source, target in there]

    def rank_columns(piece):
        piece = piece.reshape(held, 3, blocks, RANKS, chunk)
        return piece.transpose(3, 0, 1, 2, 4).reshape(RANKS, held, 3 * part)

    def ff_columns(piece):
        piece = piece.reshape(held, RANKS, ff_part).transpose(1, 0, 2)
        return jnp.pad(piece, ((0, 0), (0, 0), (0, ff_pad - ff_part)))

    smalls = jnp.concatenate([norm_scale, shifts], axis=2)
    kinds = smalls.shape[2]
    small_size = layers * kinds * held
    small_row = smalls.transpose(0, 2, 1).reshape(1, 1, small_size)
    small_row = jnp.pad(small_row, ((0, 0), (0, 0), (0, 3 * part - small_size)))
    small_row = jnp.broadcast_to(small_row, (RANKS, 1, 3 * part))
    extra = 8
    assert RANKS * small_size <= extra * width

    gathered_attn, gathered_ff = [], []
    small_full = None
    for l in range(layers):
        sent = rank_columns(qkv_weight[l])
        if l == 0:
            sent = jnp.concatenate([sent, small_row], axis=1)
        came = exchange(sent)
        out_piece = mixed_order(out_weight[l]).reshape(held, RANKS, part).transpose(1, 0, 2)
        payload = jnp.concatenate([came[:, :held], out_piece], axis=2)
        payload = payload.reshape(RANKS * held, width)
        if l == 0:
            small_block = came[:, held, :small_size].reshape(RANKS * small_size)
            small_block = jnp.pad(small_block, (0, extra * width - RANKS * small_size))
            payload = jnp.concatenate([payload, small_block.reshape(extra, width)], axis=0)
        full = gather_rows(payload)
        if l == 0:
            full = full.reshape(shards, RANKS * held + extra, width)
            small_full = full[:, RANKS * held :].reshape(shards, extra * width)
            small_full = small_full[:, : RANKS * small_size]
            small_full = small_full.reshape(shards, RANKS, layers, kinds, held)
            small_full = small_full.transpose(2, 3, 0, 1, 4).reshape(layers, kinds, width)
            small_full = small_full.astype(f32)
            full = full[:, : RANKS * held].reshape(width, width)
        qkv_full = full[:, : 3 * part]
        out_full = full[:, 3 * part :].reshape(shards, RANKS, held, part)
        out_full = out_full.transpose(0, 2, 1, 3).reshape(part, width)
        gathered_attn.append((qkv_full, out_full))
        sent = jnp.concatenate([ff_columns(up_weight[l]), ff_columns(down_weight[l])], axis=2)
        payload = exchange(sent).reshape(RANKS * held, 2 * ff_pad)
        full = gather_rows(payload)
        gathered_ff.append((full[:, :ff_pad], full[:, ff_pad:]))
    up_shift = pick(up_bias.reshape(layers, RANKS, ff_part), rank, 1).astype(f32)
    up_shift = jnp.pad(up_shift, ((0, 0), (0, ff_pad - ff_part)))

    held_rows = 2 * rows
    lengths = lax.ppermute(image_lengths, AXES, there)
    finish = jnp.cumsum(lengths[0])
    base = jnp.arange(rows, dtype=jnp.int32)
    local = jnp.concatenate(
        [base + (2 * x + c) * rows for c in (ci, 1 - ci) for x in (0, 1)]
    )
    group = RANKS * rows
    query_pos = local + (lax.axis_index("seq") % ways) * group
    key_pos = jnp.concatenate([local + w * group for w in range(ways)])

    def ids_of(pos):
        return jnp.sum((pos[:, None] >= finish[None, :]).astype(jnp.int32), axis=1)

    query_ids, key_ids = ids_of(query_pos), ids_of(key_pos)
    seq_groups = [[j * ways + w for w in range(ways)] for j in range(seqs // ways)]

    def keys_of(qkv):
        if ways == 1:
            return qkv, part
        kv = lax.all_gather(
            qkv[:, part:], "seq", axis=0, tiled=True, axis_index_groups=seq_groups
        )
        return kv, 0

    def to_group(v):
        own = lax.ppermute(mixed_order(v), AXES, there)
        return jnp.concatenate(x_order(own, swap_x(own)), axis=0)

    def share(own):
        return jnp.concatenate([own, swap_c(own)], axis=0)

    def reduce_core(own, other):
        return (own + swap_c(other).astype(f32)).astype(bf16)

    def reduce_all(own, other):
        q = reduce_core(own, other)
        return q.astype(f32) + swap_x(q).astype(f32)

    def reduce_mine(own, other):
        q = reduce_core(own, other).reshape(2, rows, width)
        come = swap_x(pick(q, 1 - xi))
        return pick(q, xi).astype(f32) + come.astype(f32)

    def my_rows(v):
        return pick(v.reshape(2, rows, width), xi)

    current = to_group(tokens).astype(f32)
    saved = []
    output = None
    for l in range(layers):
        qkv_full, out_full = gathered_attn[l]
        up_full, down_full = gathered_ff[l]
        gain_one, gain_two, off_one, q_shift, v_shift, o_shift, off_two, d_shift = small_full[l]
        attn_in = share(norm(current, gain_one, off_one).astype(bf16))
        qkv_shift = jnp.concatenate([mine(q_shift), jnp.zeros((part,), f32), mine(v_shift)])
        qkv = (dot(attn_in, qkv_full) + qkv_shift).astype(bf16)
        kv, kv_offset = keys_of(qkv)
        attended = attend(qkv, kv, kv_offset, query_ids, key_ids, heads, dim)
        other = dot(attended[held_rows:], out_full, bf16)
        own = dot(attended[:held_rows], out_full)
        after_attn = current + (reduce_all(own, other) + o_shift)
        mlp_in = share(norm(after_attn, gain_two, off_two).astype(bf16))
        hidden = dot(mlp_in, up_full) + up_shift[l]
        activated = gelu_tanh(hidden).astype(bf16)
        other = dot_last(activated[held_rows:], down_full, bf16)
        own = dot_last(activated[:held_rows], down_full)
        saved.append((current, attn_in, qkv, kv, kv_offset, attended, after_attn, mlp_in, hidden, activated))
        if l < layers - 1:
            current = after_attn + (reduce_all(own, other) + d_shift)
        else:
            final = my_rows(after_attn) + (reduce_mine(own, other) + d_shift)
            output = lax.ppermute(final.astype(bf16), AXES, back)
            output = plain_order(output).astype(f32)

    grads = [None] * layers
    bias_rows = [None] * layers
    down_in = to_group(cotangent)
    grad_current = down_in.astype(f32)
    tokens_grad = None
    for l in reversed(range(layers)):
        (current, attn_in, qkv, kv, kv_offset, attended, after_attn, mlp_in, hidden, activated) = saved[l]
        qkv_full, out_full = gathered_attn[l]
        up_full, down_full = gathered_ff[l]
        gain_one, gain_two = small_full[l, 0], small_full[l, 1]
        down_in = share(down_in)
        grad_act = dot(down_in, down_full)
        hidden_grad = jax.vjp(gelu_tanh, hidden)[1](grad_act)[0].astype(bf16)
        other = dot_last(hidden_grad[held_rows:], up_full, bf16)
        own = dot_last(hidden_grad[:held_rows], up_full)
        d_sum = 0.5 * jnp.sum(down_in[:held_rows].astype(f32), axis=0)
        bias_sum = jnp.sum(hidden_grad.astype(f32), axis=0)
        resid, gain_two_sum, off_two_sum = norm_back(after_attn, gain_two, reduce_all(own, other))
        grad_current = grad_current + resid
        ff_terms = jnp.concatenate(
            [dot_rows(mlp_in, hidden_grad, bf16), dot_rows(down_in, activated, bf16)], axis=1
        ).reshape(shards, RANKS * held, 2 * ff_pad)
        piece = ff_pad // shards
        bias_row = jnp.pad(
            bias_sum.astype(bf16).reshape(shards, 1, piece),
            ((0, 0), (0, extra - 1), (0, 2 * ff_pad - piece)),
        )
        ff_terms = jnp.concatenate([ff_terms, bias_row], axis=1)
        ff_owned = scatter_rows(
            ff_terms.reshape(shards * (RANKS * held + extra), 2 * ff_pad)
        )
        bias_rows[l] = ff_owned[RANKS * held, :piece]
        ff_owned = exchange(ff_owned[: RANKS * held].reshape(RANKS, held, 2 * ff_pad))
        up_grad = ff_owned[:, :, :ff_part].transpose(1, 0, 2).reshape(held, ff)
        down_grad = ff_owned[:, :, ff_pad : ff_pad + ff_part].transpose(1, 0, 2).reshape(held, ff)

        out_own = grad_current.astype(bf16)
        o_sum = 0.5 * jnp.sum(out_own.astype(f32), axis=0)
        out_in = share(out_own)
        attended_grad = dot_last(out_in, out_full, bf16)
        q_grad, kv_grad = attend_back(
            qkv, kv, kv_offset, query_ids, key_ids, attended_grad, heads, dim
        )
        if ways > 1:
            kv_grad = lax.psum_scatter(
                kv_grad, "seq", scatter_dimension=0, tiled=True, axis_index_groups=seq_groups
            )
        qkv_grad = jnp.concatenate([q_grad, kv_grad], axis=1)
        other = dot_last(qkv_grad[held_rows:], qkv_full, bf16)
        own = dot_last(qkv_grad[:held_rows], qkv_full)
        column_sums = jnp.sum(qkv_grad.astype(f32), axis=0)

        def placed(v):
            spots = (jnp.arange(RANKS) == rank)[None, None, :, None]
            return jnp.where(spots, v.reshape(blocks, seqs, 1, held), 0.0).reshape(width)

        if l > 0:
            resid, gain_one_sum, off_one_sum = norm_back(current, gain_one, reduce_all(own, other))
            grad_current = grad_current + resid
            gain_one_sum, off_one_sum = 0.5 * gain_one_sum, 0.5 * off_one_sum
            down_in = grad_current.astype(bf16)
        else:
            resid, gain_one_sum, off_one_sum = norm_back(
                my_rows(current), gain_one, reduce_mine(own, other)
            )
            final = my_rows(grad_current) + resid
            tokens_grad = lax.ppermute(final.astype(bf16), AXES, back)
            tokens_grad = plain_order(tokens_grad).astype(f32)
        vectors = jnp.stack(
            [
                gain_one_sum,
                0.5 * gain_two_sum,
                off_one_sum,
                placed(column_sums[:part]),
                placed(column_sums[2 * part :]),
                o_sum,
                0.5 * off_two_sum,
                d_sum,
            ]
        )
        vectors = vectors.astype(bf16).reshape(kinds, shards, RANKS, held)
        vectors = vectors.transpose(1, 2, 0, 3).reshape(shards, 1, RANKS * kinds * held)
        vectors = jnp.pad(
            vectors, ((0, 0), (0, 0), (0, extra * width - RANKS * kinds * held))
        ).reshape(shards, extra, width)
        out_terms = dot_rows(attended, out_in, bf16).reshape(shards, held, RANKS, part)
        out_terms = out_terms.transpose(0, 2, 1, 3).reshape(shards, RANKS * held, part)
        qkv_terms = dot_rows(attn_in, qkv_grad, bf16).reshape(shards, RANKS * held, 3 * part)
        attn_terms = jnp.concatenate(
            [jnp.concatenate([qkv_terms, out_terms], axis=2), vectors], axis=1
        )
        owned = scatter_rows(attn_terms.reshape(shards * (RANKS * held + extra), width))
        out_grad = owned[: RANKS * held, 3 * part :].reshape(RANKS, held, part)
        out_grad = plain_order(out_grad.transpose(1, 0, 2).reshape(held, width))
        vector_row = owned[RANKS * held :].reshape(extra * width)[: RANKS * kinds * held]
        vector_row = vector_row.reshape(RANKS, 1, kinds * held)
        vector_row = jnp.pad(vector_row, ((0, 0), (0, 0), (0, 3 * part - kinds * held)))
        came = exchange(
            jnp.concatenate(
                [owned[: RANKS * held, : 3 * part].reshape(RANKS, held, 3 * part), vector_row],
                axis=1,
            )
        )
        qkv_out = came[:, :held].reshape(RANKS, held, 3, blocks, chunk)
        qkv_out = qkv_out.transpose(1, 2, 3, 0, 4).reshape(held, 3 * width)
        sums = jnp.sum(came[:, held, : kinds * held].astype(f32), axis=0).reshape(kinds, held)
        grads[l] = (
            qkv_out.astype(f32),
            out_grad.astype(f32),
            up_grad.astype(f32),
            down_grad.astype(f32),
            sums[:2].T,
            sums[2:].T,
        )

    bias = jnp.stack(bias_rows)
    place = jnp.arange(shards * RANKS) == lax.axis_index(AXES)
    bias = jnp.where(place[:, None, None], bias[None], jnp.zeros((), bf16))
    bias = sum_everywhere(bias.reshape(shards * RANKS, -1))
    bias = bias.reshape(blocks, RANKS, seqs, layers, -1).transpose(3, 1, 0, 2, 4)
    bias = bias.reshape(layers, RANKS, ff_pad)[:, :, :ff_part].reshape(layers, ff)
    stacked = [jnp.stack([grads[l][i] for l in range(layers)]) for i in range(6)]
    return (
        output,
        tokens_grad,
        stacked[0],
        stacked[1],
        stacked[2],
        stacked[3],
        bias.astype(f32),
        stacked[4],
        stacked[5],
    )


def solution(mesh):
    sizes = mesh.shape
    devices = mesh.devices.reshape(sizes["img"] // RANKS, 2, 2, sizes["seq"])
    fine = Mesh(devices, AXES)
    row = P(AXES, None)
    param = P(None, AXES, None)
    in_specs = (row, row, P(AXES[:3], None), param, param, param, param, P(), param, param)
    out_specs = (row, row, param, param, param, param, P(), param, param)
    return jax.shard_map(
        body, mesh=fine, in_specs=in_specs, out_specs=out_specs, check_vma=False
    )
```

```python
import functools
import math

import jax
import jax.numpy as jnp
from jax import lax
from jax.experimental import pallas as pl
from jax.experimental.pallas import tpu as pltpu
from jax.sharding import Mesh
from jax.sharding import PartitionSpec as P

HEADS = 16
RANKS = 4
CHUNKS = 1
EPSILON = 1e-06
NEGATIVE = -1e30
ROOT = math.sqrt(2.0 / math.pi)
AXES = ("hi", "x", "c", "seq")
SWAP = ((0, 1), (1, 0))
bf16, f32 = jnp.bfloat16, jnp.float32
VMEM = pl.BlockSpec(memory_space=pltpu.VMEM)


def mm(left, right):
    return jnp.dot(left, right, preferred_element_type=f32)


def mm_last(left, right):
    dims = (((1,), (1,)), ((), ()))
    return lax.dot_general(left, right, dims, preferred_element_type=f32)


def mm_first(left, right):
    dims = (((0,), (0,)), ((), ()))
    return lax.dot_general(left, right, dims, preferred_element_type=f32)


def shape(dims, kind):
    return jax.ShapeDtypeStruct(tuple(dims), kind)


def params(mib):
    return pltpu.CompilerParams(vmem_limit_bytes=mib * 2**20)


def cost(flops, moved, exps=0):
    share = 0.1
    return pl.CostEstimate(
        flops=int(share * flops), bytes_accessed=int(share * moved), transcendentals=int(share * exps)
    )


def const(dims):
    return pl.BlockSpec(tuple(dims), lambda i: (0,) * len(dims))


def split(half, block, width):
    n = half // block
    own = pl.BlockSpec((block, width), lambda i: (jnp.minimum(i, n - 1), 0))
    rec = pl.BlockSpec((block, width), lambda i: (jnp.maximum(i - n, 0), 0))
    strip = pl.BlockSpec((block, width), lambda i: (i, 0))
    return n, own, rec, strip


def either(own_work, rec_work):
    step, half = pl.program_id(0), pl.num_programs(0) // 2
    pl.when(step < half)(own_work)
    pl.when(step >= half)(rec_work)


def project_kernel(own_ref, rec_ref, w_ref, shift_ref, out_ref):
    width = out_ref.shape[1]

    def work(ref):
        out_ref[...] = (mm(ref[...], w_ref[:, :width]) + shift_ref[...]).astype(bf16)

    either(lambda: work(own_ref), lambda: work(rec_ref))


def project(own, rec, weight, shift):
    half, depth = own.shape
    width = shift.shape[0]
    n, own_spec, rec_spec, _ = split(half, min(half, 256), depth)
    return pl.pallas_call(
        project_kernel,
        grid=(2 * n,),
        in_specs=[own_spec, rec_spec, const(weight.shape), const((1, width))],
        out_specs=pl.BlockSpec((half // n, width), lambda i: (i, 0)),
        out_shape=shape((2 * half, width), bf16),
        compiler_params=params(24),
        cost_estimate=cost(4 * half * depth * width, 2 * depth * (2 * half + width)),
    )(own, rec, weight, shift[None])


def attend_kernel(heads, dim, offset, count, *refs):
    qid_ref, kid_ref, q_ref, wo_ref = refs[:4]
    kv_refs = refs[4 : 4 + count]
    o_ref, own_ref, rec_ref = refs[4 + count :]
    factor = dim**-0.5 * math.log2(math.e)
    width = heads * dim
    same = qid_ref[...] == kid_ref[...]
    outs = []
    for h in range(heads):
        lo = h * dim
        at = offset + width + lo
        q = q_ref[:, lo : lo + dim]
        k = jnp.concatenate([ref[:, offset + lo : offset + lo + dim] for ref in kv_refs])
        v = jnp.concatenate([ref[:, at : at + dim] for ref in kv_refs])
        s = jnp.where(same, mm_last(q, k), NEGATIVE)
        top = jnp.max(s, axis=1, keepdims=True)
        p = jnp.exp2((s - top) * factor)
        total = jnp.sum(p, axis=1, keepdims=True)
        outs.append(mm(p.astype(bf16), v) / total)
    o = jnp.concatenate(outs, axis=1).astype(bf16)
    o_ref[...] = o
    terms = mm(o, wo_ref[...])

    def own_work():
        own_ref[...] = terms

    def rec_work():
        rec_ref[...] = terms.astype(bf16)

    either(own_work, rec_work)


def attend(qkv, kvs, offset, query_ids, key_ids, out_full, heads, dim):
    rows, width, wide = qkv.shape[0], heads * dim, out_full.shape[1]
    keys = sum(kv.shape[0] for kv in kvs)
    n, own_spec, rec_spec, _ = split(rows // 2, min(rows // 2, 512 * 1024 // keys), wide)
    block = rows // (2 * n)
    return pl.pallas_call(
        functools.partial(attend_kernel, heads, dim, offset, len(kvs)),
        grid=(2 * n,),
        in_specs=[
            pl.BlockSpec((block, 1), lambda i: (i, 0)),
            const((1, keys)),
            pl.BlockSpec((block, qkv.shape[1]), lambda i: (i, 0)),
            const(out_full.shape),
        ]
        + [const(kv.shape) for kv in kvs],
        out_specs=[pl.BlockSpec((block, width), lambda i: (i, 0)), own_spec, rec_spec],
        out_shape=[
            shape((rows, width), bf16),
            shape((rows // 2, wide), f32),
            shape((rows // 2, wide), bf16),
        ],
        compiler_params=params(44),
        cost_estimate=cost(10 * rows * keys * width, 16 * rows * width, heads * rows * keys),
    )(query_ids[:, None], key_ids[None, :], qkv, out_full, *kvs)


def attend_back_kernel(heads, dim, offset, count, first, last, *refs):
    qid_ref, kid_ref, q_ref, wo_ref, own_ref, rec_ref = refs[:6]
    kv_refs = refs[6 : 6 + count]
    rest = refs[6 + count :]
    if not first:
        before_ref, rest = rest[0], rest[1:]
    dq_ref, dkv_ref, do_ref, acc_ref = rest
    step = pl.program_id(0)
    scale = dim**-0.5
    factor = scale * math.log2(math.e)
    width = heads * dim

    @pl.when(step == 0)
    def _():
        acc_ref[...] = jnp.zeros_like(acc_ref) if first else before_ref[...]

    def own_work():
        do_ref[...] = mm_last(own_ref[...], wo_ref[...]).astype(bf16)

    def rec_work():
        do_ref[...] = mm_last(rec_ref[...], wo_ref[...]).astype(bf16)

    either(own_work, rec_work)
    same = kid_ref[...] == qid_ref[...]
    dqs = []
    for h in range(heads):
        lo = h * dim
        at = offset + width + lo
        q = q_ref[:, lo : lo + dim]
        do = do_ref[:, lo : lo + dim]
        k = jnp.concatenate([ref[:, offset + lo : offset + lo + dim] for ref in kv_refs])
        v = jnp.concatenate([ref[:, at : at + dim] for ref in kv_refs])
        s = jnp.where(same, mm_last(k, q), NEGATIVE)
        top = jnp.max(s, axis=0, keepdims=True)
        p = jnp.exp2((s - top) * factor)
        p = p * (1.0 / jnp.sum(p, axis=0, keepdims=True))
        dp = mm_last(v, do)
        delta = jnp.sum(p * dp, axis=0, keepdims=True)
        ds = (p * (dp - delta)).astype(bf16)
        acc_ref[heads + h] += mm(p.astype(bf16), do)
        acc_ref[h] += mm(ds, q)
        dqs.append(mm_first(ds, k) * scale)
    dq_ref[...] = jnp.concatenate(dqs, axis=1).astype(bf16)

    @pl.when(step == pl.num_programs(0) - 1)
    def _():
        if last:
            parts = [acc_ref[h] * scale for h in range(heads)]
            parts += [acc_ref[heads + h] for h in range(heads)]
            dkv_ref[...] = jnp.concatenate(parts, axis=1).astype(bf16)
        else:
            dkv_ref[...] = acc_ref[...]


def attend_back(qkv, kvs, offset, query_ids, key_ids, out_full, own, rec, before, last, heads, dim):
    rows, width, wide = qkv.shape[0], heads * dim, out_full.shape[1]
    keys = sum(kv.shape[0] for kv in kvs)
    sums = (2 * heads, keys, dim)
    extra = [] if before is None else [before]
    n, own_spec, rec_spec, _ = split(rows // 2, min(rows // 2, 512 * 1024 // keys), wide)
    block = rows // (2 * n)
    done = shape((keys, 2 * width), bf16) if last else shape(sums, f32)
    return pl.pallas_call(
        functools.partial(attend_back_kernel, heads, dim, offset, len(kvs), before is None, last),
        grid=(2 * n,),
        in_specs=[
            pl.BlockSpec((1, block), lambda i: (0, i)),
            const((keys, 1)),
            pl.BlockSpec((block, qkv.shape[1]), lambda i: (i, 0)),
            const(out_full.shape),
            own_spec,
            rec_spec,
        ]
        + [const(v.shape) for v in list(kvs) + extra],
        out_specs=[pl.BlockSpec((block, width), lambda i: (i, 0)), const(done.shape)],
        out_shape=[shape((rows, width), bf16), done],
        scratch_shapes=[pltpu.VMEM((block, width), bf16), pltpu.VMEM(sums, f32)],
        compiler_params=params(52),
        cost_estimate=cost(24 * rows * keys * width, 30 * rows * width, heads * rows * keys),
    )(query_ids[None, :], key_ids[:, None], qkv, out_full, own, rec, *kvs, *extra)


def join_kernel(dq_ref, dkv_ref, w_ref, dqkv_ref, own_ref, rec_ref, sum_ref):
    @pl.when(pl.program_id(0) == 0)
    def _():
        sum_ref[...] = jnp.zeros_like(sum_ref)

    dqkv = jnp.concatenate([dq_ref[...], dkv_ref[...]], axis=1)
    dqkv_ref[...] = dqkv
    sum_ref[...] += jnp.sum(dqkv.astype(f32), axis=0, keepdims=True)
    terms = mm_last(dqkv, w_ref[:, : dqkv.shape[1]])

    def own_work():
        own_ref[...] = terms

    def rec_work():
        rec_ref[...] = terms.astype(bf16)

    either(own_work, rec_work)


def join(dq, dkv, chunk, weight):
    rows, width, wide = dq.shape[0], dq.shape[1] + dkv.shape[1], weight.shape[0]
    n, own_spec, rec_spec, _ = split(rows // 2, min(rows // 2, 256), wide)
    block, at = rows // (2 * n), 2 * n * chunk
    return pl.pallas_call(
        join_kernel,
        grid=(2 * n,),
        in_specs=[
            pl.BlockSpec((block, dq.shape[1]), lambda i: (i, 0)),
            pl.BlockSpec((block, dkv.shape[1]), lambda i: (at + i, 0)),
            const(weight.shape),
        ],
        out_specs=[pl.BlockSpec((block, width), lambda i: (i, 0)), own_spec, rec_spec, const((1, width))],
        out_shape=[
            shape((rows, width), bf16),
            shape((rows // 2, wide), f32),
            shape((rows // 2, wide), bf16),
            shape((1, width), f32),
        ],
        compiler_params=params(24),
        cost_estimate=cost(2 * rows * width * wide, 4 * wide * (rows + width)),
    )(dq, dkv, weight)


def hidden_kernel(own_ref, rec_ref, up_ref, down_ref, shift_ref, slope_ref, act_ref, po_ref, pr_ref):
    def work(ref, out_ref):
        e = mm(ref[...], up_ref[...]) + shift_ref[...]
        square = e * e
        h = 0.5 * jnp.tanh(e * (square * (ROOT * 0.044715) + ROOT)) + 0.5
        g = e * h
        slope = h + g * (1.0 - h) * (square * (6 * ROOT * 0.044715) + 2 * ROOT)
        g = g.astype(bf16)
        act_ref[...] = g
        slope_ref[...] = slope.astype(bf16)
        out_ref[...] = mm_last(g, down_ref[...]).astype(out_ref.dtype)

    either(lambda: work(own_ref, po_ref), lambda: work(rec_ref, pr_ref))


def tile_of(size):
    return 384 if size % 384 == 0 else 128


def hidden(own, rec, up, down, shift):
    half, wide = own.shape
    ff = up.shape[1]
    n, own_spec, rec_spec, _ = split(half, min(half, 256), wide)
    strip = pl.BlockSpec((half // n, ff), lambda i: (i, 0))
    return pl.pallas_call(
        hidden_kernel,
        grid=(2 * n,),
        in_specs=[own_spec, rec_spec, const(up.shape), const(down.shape), const((1, ff))],
        out_specs=[strip, strip, own_spec, rec_spec],
        out_shape=[
            shape((2 * half, ff), bf16),
            shape((2 * half, ff), bf16),
            shape((half, wide), f32),
            shape((half, wide), bf16),
        ],
        compiler_params=params(30),
        cost_estimate=cost(8 * half * wide * ff, 4 * wide * ff + 20 * half * wide, 2 * half * ff),
    )(own, rec, up, down, shift[None])


def hidden_back_kernel(own_ref, rec_ref, slope_ref, up_ref, down_ref, de_ref, sum_ref, po_ref, pr_ref):
    @pl.when(pl.program_id(0) == 0)
    def _():
        sum_ref[...] = jnp.zeros_like(sum_ref)

    def work(ref, out_ref):
        de = (mm(ref[...], down_ref[...]) * slope_ref[...].astype(f32)).astype(bf16)
        de_ref[...] = de
        sum_ref[...] += jnp.sum(de.astype(f32), axis=0, keepdims=True)
        out_ref[...] = mm_last(de, up_ref[...]).astype(out_ref.dtype)

    either(lambda: work(own_ref, po_ref), lambda: work(rec_ref, pr_ref))


def hidden_back(own, rec, slope, up, down):
    half, wide = own.shape
    ff = up.shape[1]
    n, own_spec, rec_spec, _ = split(half, min(half, 256), wide)
    strip = pl.BlockSpec((half // n, ff), lambda i: (i, 0))
    return pl.pallas_call(
        hidden_back_kernel,
        grid=(2 * n,),
        in_specs=[own_spec, rec_spec, strip, const(up.shape), const(down.shape)],
        out_specs=[strip, const((1, ff)), own_spec, rec_spec],
        out_shape=[
            shape((2 * half, ff), bf16),
            shape((1, ff), f32),
            shape((half, wide), f32),
            shape((half, wide), bf16),
        ],
        compiler_params=params(30),
        cost_estimate=cost(8 * half * wide * ff, 4 * wide * ff + 16 * half * wide),
    )(own, rec, slope, up, down)


def outer_kernel(lefts, rights, beside, bit_ref, *refs):
    left_refs, right_refs = refs[:lefts], refs[lefts : lefts + rights]
    rest = refs[lefts + rights :]
    if beside:
        beside_ref, rest = rest[0], rest[1:]
    mine_ref, theirs_ref = rest
    turned = right_refs[0].shape[0]
    cuts = [ref.shape[0] for ref in left_refs]
    total, at = None, 0
    for ref, size in zip(left_refs, cuts):
        low = at % turned
        right = right_refs[at // turned]
        part = mm_first(ref[...], right[low : low + size, :])
        total = part if total is None else total + part
        at += size
    out = total.astype(bf16)
    if beside:
        out = jnp.concatenate([out, beside_ref[...]], axis=1)
    half = out.shape[0] // 2

    @pl.when(bit_ref[0] == 0)
    def _():
        mine_ref[...], theirs_ref[...] = out[:half], out[half:]

    @pl.when(bit_ref[0] == 1)
    def _():
        mine_ref[...], theirs_ref[...] = out[half:], out[:half]


def outer(lefts, rights, bit, beside=None):
    depth, width = lefts[0].shape[1], rights[0].shape[1]
    rows = sum(v.shape[0] for v in lefts)
    extra = [] if beside is None else [beside]
    out = shape((depth // 2, width + sum(v.shape[1] for v in extra)), bf16)
    return pl.pallas_call(
        functools.partial(outer_kernel, len(lefts), len(rights), len(extra)),
        in_specs=[pl.BlockSpec(memory_space=pltpu.SMEM)]
        + [VMEM] * (len(lefts) + len(rights) + len(extra)),
        out_specs=[VMEM] * 2,
        out_shape=[out] * 2,
        compiler_params=params(30),
        cost_estimate=cost(2 * rows * depth * width, 2 * rows * (depth + width) + 2 * depth * width),
    )(bit, *lefts, *rights, *extra)


def outer_out_kernel(count, o_ref, *refs):
    out_ref = refs[count]
    total, at = None, 0
    for ref in refs[:count]:
        part = mm_first(o_ref[at : at + ref.shape[0], :], ref[...])
        total = part if total is None else total + part
        at += ref.shape[0]
    out_ref[...] = total.astype(bf16)


def outer_out(attended, rights):
    depth, width, rows = attended.shape[1], rights[0].shape[1], attended.shape[0]
    return pl.pallas_call(
        functools.partial(outer_out_kernel, len(rights)),
        in_specs=[VMEM] * (1 + len(rights)),
        out_specs=VMEM,
        out_shape=shape((depth, width), bf16),
        compiler_params=params(24),
        cost_estimate=cost(2 * rows * depth * width, 2 * rows * (depth + width) + 2 * depth * width),
    )(attended, *rights)


def spread(v):
    centred = v - jnp.mean(v, axis=-1, keepdims=True)
    scale = lax.rsqrt(jnp.mean(centred * centred, axis=-1, keepdims=True) + EPSILON)
    return centred * scale, scale


def norm_kernel(rows_of, v_ref, q_ref, come_ref, small_ref, next_ref, u_ref, m_ref):
    shift, gain, offset = rows_of
    u = v_ref[...] + (q_ref[...].astype(f32) + come_ref[...].astype(f32) + small_ref[shift : shift + 1, :])
    u_ref[...] = u
    n = spread(u)[0] * next_ref[gain : gain + 1, :] + next_ref[offset : offset + 1, :]
    m_ref[...] = n.astype(bf16)


def add_norm(v, q, come, small, following, rows_of):
    rows, width = v.shape
    block = pl.BlockSpec((min(rows, 256), width), lambda i: (i, 0))
    return pl.pallas_call(
        functools.partial(norm_kernel, rows_of),
        grid=(rows // min(rows, 256),),
        in_specs=[block] * 3 + [const(small.shape)] * 2,
        out_specs=[block] * 2,
        out_shape=[shape(v.shape, f32), shape(v.shape, bf16)],
        compiler_params=params(16),
        cost_estimate=cost(12 * v.size, 14 * v.size),
    )(v, q, come, small, following)


def norm_back_kernel(gain, v_ref, q_ref, come_ref, grad_ref, small_ref, out_ref, round_ref, sum_ref):
    @pl.when(pl.program_id(0) == 0)
    def _():
        sum_ref[...] = jnp.zeros_like(sum_ref)

    t = q_ref[...].astype(f32) + come_ref[...].astype(f32)
    n, scale = spread(v_ref[...])
    w = t * small_ref[gain : gain + 1, :]
    mean_w = jnp.mean(w, axis=-1, keepdims=True)
    mean_wn = jnp.mean(w * n, axis=-1, keepdims=True)
    out = grad_ref[...] + scale * (w - mean_w - n * mean_wn)
    out_ref[...] = out
    rounded = out.astype(bf16)
    round_ref[...] = rounded
    sum_ref[0:1, :] += jnp.sum(t * n, axis=0, keepdims=True)
    sum_ref[1:2, :] += jnp.sum(t, axis=0, keepdims=True)
    sum_ref[2:3, :] += jnp.sum(rounded.astype(f32), axis=0, keepdims=True)


def norm_back(v, q, come, grad, small, gain):
    rows, width = v.shape
    block = pl.BlockSpec((min(rows, 256), width), lambda i: (i, 0))
    return pl.pallas_call(
        functools.partial(norm_back_kernel, gain),
        grid=(rows // min(rows, 256),),
        in_specs=[block] * 4 + [const(small.shape)],
        out_specs=[block] * 2 + [const((8, width))],
        out_shape=[shape(v.shape, f32), shape(v.shape, bf16), shape((8, width), f32)],
        compiler_params=params(20),
        cost_estimate=cost(24 * v.size, 18 * v.size),
    )(v, q, come, grad, small)


def tie(values):
    return lax.optimization_barrier(values)


def pick(array, index, axis=0):
    return lax.dynamic_index_in_dim(array, index, axis, keepdims=False)


def swap_x(v):
    return lax.ppermute(v, "x", SWAP)


def swap_c(v):
    return lax.ppermute(v, "c", SWAP)


def in_order(axis, own, other):
    first = lax.axis_index(axis) == 0
    return jnp.where(first, own, other), jnp.where(first, other, own)


def exchange(blocks):
    xi, ci = lax.axis_index("x"), lax.axis_index("c")
    blocks = blocks.reshape((2, 2) + blocks.shape[1:])
    both = jnp.stack(in_order("x", pick(blocks, xi), swap_x(pick(blocks, 1 - xi))))
    out = in_order("c", pick(both, ci, 1), swap_c(pick(both, 1 - ci, 1)))
    return jnp.stack(out, axis=1).reshape((RANKS,) + blocks.shape[2:])


def flip(v, axis, step):
    size = lax.axis_size(axis)
    return lax.ppermute(v, axis, [(i, i ^ step) for i in range(size)])


def gather_rows(payload):
    return lax.all_gather(payload, ("hi", "seq"), axis=0, tiled=True)


def halve_rows(mine, theirs):
    step = lax.axis_size("hi") // 2
    place = lax.axis_index("hi")
    terms = (mine.astype(f32) + flip(theirs, "hi", step).astype(f32)).astype(bf16)
    step //= 2
    while step:
        halves = terms.reshape((2, -1) + terms.shape[1:])
        bit = (place // step) % 2
        come = flip(pick(halves, 1 - bit), "hi", step)
        terms = (pick(halves, bit).astype(f32) + come.astype(f32)).astype(bf16)
        step //= 2
    return terms


def scatter_rows(terms):
    return lax.psum_scatter(terms, "seq", scatter_dimension=0, tiled=True)


def sum_everywhere(v):
    for axis in AXES[::-1]:
        step = 1
        while step < lax.axis_size(axis):
            v = v + flip(v, axis, step)
            step *= 2
    return v


def body(
    tokens,
    cotangent,
    image_lengths,
    qkv_weight,
    out_weight,
    up_weight,
    down_weight,
    up_bias,
    norm_scale,
    shifts,
):
    rows, width = tokens.shape
    layers, held = qkv_weight.shape[0], qkv_weight.shape[1]
    blocks, seqs = lax.axis_size("hi"), lax.axis_size("seq")
    ways = seqs // RANKS
    shards = blocks * seqs
    chunk = seqs * held
    heads = HEADS // RANKS
    dim = width // HEADS
    part = width // RANKS
    ff = up_weight.shape[2]
    ff_part = ff // RANKS
    ff_pad = -(-ff_part // 128) * 128
    xi, ci = lax.axis_index("x"), lax.axis_index("c")
    rank = 2 * xi + ci

    spot = jnp.arange(width, dtype=jnp.int32)
    natural = ((spot // (RANKS * held * seqs) * RANKS + spot // held % RANKS) * seqs) * held
    natural = natural + spot // (RANKS * held) % seqs * held + spot % held
    turn_matrix = (spot[:, None] == natural[None, :]).astype(bf16)

    def mixed_order(v):
        return mm(v, turn_matrix).astype(bf16)

    def plain_order(v):
        return mm_last(v, turn_matrix)

    def mine(v):
        return pick(v.reshape(blocks, seqs, RANKS, held), rank, 2).reshape(part)

    def placed(v):
        v = v.reshape(blocks, seqs, 1, held)
        spots = (jnp.arange(RANKS) == rank)[None, None, :, None]
        return jnp.where(spots, v, 0.0).reshape(width)

    there = []
    for b in range(blocks):
        for r in range(RANKS):
            for s in range(seqs):
                target = (b * RANKS + s % RANKS) * seqs + r * ways + s // RANKS
                there.append(((b * RANKS + r) * seqs + s, target))
    back = [(target, source) for source, target in there]

    def rank_columns(piece):
        piece = piece.reshape(held, 3, blocks, RANKS, chunk)
        return piece.transpose(3, 0, 1, 2, 4).reshape(RANKS, held, 3 * part)

    def ff_columns(piece):
        piece = piece.reshape(held, RANKS, ff_part).transpose(1, 0, 2)
        return jnp.pad(piece, ((0, 0), (0, 0), (0, ff_pad - ff_part)))

    def out_rows(l):
        return mixed_order(out_weight[l]).reshape(held * RANKS, part)

    kinds = norm_scale.shape[2] + shifts.shape[2]
    smalls = jnp.concatenate([norm_scale, shifts], axis=2)
    smalls = smalls.transpose(1, 0, 2).reshape(1, held, layers * kinds)
    smalls = jnp.broadcast_to(smalls, (RANKS, held, layers * kinds))

    qkv_fulls, out_fulls, up_fulls, down_fulls = [], [], [], []
    came = exchange(jnp.concatenate([rank_columns(qkv_weight[0]), smalls], axis=2))
    came = came.reshape(RANKS * held, -1)
    payload = jnp.concatenate([came[:, : 3 * part], out_rows(0), came[:, 3 * part :]], axis=1)
    first = gather_rows(payload)
    small_full = first[:, width:].T.reshape(layers, kinds, width).astype(f32)
    qkv_fulls.append(first)
    out_fulls.append(first[:, 3 * part : width].reshape(part, width))
    later = [
        ff_columns(piece) for l in range(layers) for piece in (up_weight[l], down_weight[l])
    ] + [rank_columns(qkv_weight[l]) for l in range(1, layers)]
    arrived = lax.ppermute(tokens, AXES, there)
    later, arrived, _ = tie((jnp.concatenate(later, axis=2), arrived, payload))
    later = exchange(later).reshape(RANKS * held, -1)
    for l in range(layers):
        if l > 0:
            at = 2 * layers * ff_pad + (l - 1) * 3 * part
            payload = jnp.concatenate([later[:, at : at + 3 * part], out_rows(l)], axis=1)
            full = gather_rows(payload)
            qkv_fulls.append(full)
            out_fulls.append(full[:, 3 * part :].reshape(part, width))
        at = 2 * l * ff_pad
        full = gather_rows(later[:, at : at + 2 * ff_pad])
        up_fulls.append(full[:, :ff_pad])
        down_fulls.append(full[:, ff_pad:])
    up_shift = pick(up_bias.reshape(layers, RANKS, ff_part), rank, 1).astype(f32)
    up_shift = jnp.pad(up_shift, ((0, 0), (0, ff_pad - ff_part)))

    xs = [(0, 1)] if CHUNKS == 1 else [(0,), (1,)]
    span = 4 * rows // CHUNKS
    lengths = lax.ppermute(image_lengths, AXES, there)
    finish = jnp.cumsum(lengths[0])
    base = jnp.arange(rows, dtype=jnp.int32)
    local = [
        jnp.concatenate([base + (2 * x + c) * rows for c in (ci, 1 - ci) for x in chunk_xs])
        for chunk_xs in xs
    ]
    group = RANKS * rows
    turn = lax.axis_index("seq") % ways

    def ids_of(pos):
        return jnp.sum((pos[:, None] >= finish[None, :]).astype(jnp.int32), axis=1)

    query_ids = [ids_of(v + turn * group) for v in local]
    key_ids = ids_of(jnp.concatenate([v + w * group for v in local for w in range(ways)]))
    seq_groups = [[j * ways + w for w in range(ways)] for j in range(seqs // ways)]

    def keys_of(qkv):
        if ways == 1:
            return qkv, part
        kv = lax.all_gather(
            qkv[:, part:], "seq", axis=0, tiled=True, axis_index_groups=seq_groups
        )
        return kv, 0

    def chunks_of(v):
        own = mixed_order(v)
        pair = in_order("x", own, swap_x(own))
        return list(pair) if CHUNKS == 2 else [jnp.concatenate(pair)]

    def at_x(chunks, index):
        if CHUNKS == 2:
            return jnp.where(index == 0, chunks[0], chunks[1])
        return pick(chunks[0].reshape((2, rows) + chunks[0].shape[1:]), index)

    def core_sum(own, other):
        return (own + swap_c(other).astype(f32)).astype(bf16)

    def last_sum(qs):
        return at_x(qs, xi), swap_x(at_x(qs, 1 - xi))

    def to_rows(v):
        return plain_order(lax.ppermute(v.astype(bf16), AXES, back))

    GAIN1, GAIN2, OFF1, QB, VB, OB, OFF2, DB = range(8)
    starts = chunks_of(arrived)
    current = [v.astype(f32) for v in starts]
    normed = [
        (spread(v)[0] * small_full[0, GAIN1] + small_full[0, OFF1]).astype(bf16) for v in current
    ]
    saved = []
    output = None
    for l in range(layers):
        small = small_full[l]
        attn_in = [(v, swap_c(v)) for v in normed]
        shift = jnp.concatenate([mine(small[QB]), jnp.zeros((part,), f32), mine(small[VB])])
        qkv = [project(own, rec, qkv_fulls[l], shift) for own, rec in attn_in]
        kvs = [keys_of(v) for v in qkv]
        offset, kvs = kvs[0][1], [v[0] for v in kvs]
        attended, after, normed = [], [], []
        for j in range(CHUNKS):
            o, own, other = attend(
                qkv[j], kvs, offset, query_ids[j], key_ids, out_fulls[l], heads, dim
            )
            attended.append(o)
            q = core_sum(own, other)
            if l == layers - 1 and j == 0:
                q, cotangent = tie((q, cotangent))
                arrived = lax.ppermute(cotangent, AXES, there)
            come = swap_x(q)
            if l == layers - 1 and j == 0:
                come, arrived = tie((come, arrived))
            u, m = add_norm(current[j], q, come, small, small, (OB, GAIN2, OFF2))
            after.append(u)
            normed.append(m)
        mlp_in = [(v, swap_c(v)) for v in normed]
        if l == layers - 1:
            mlp_in, rounded = tie((mlp_in, chunks_of(arrived)))
        slopes, acts, qs, following, normed = [], [], [], [], []
        for j in range(CHUNKS):
            slope, act, own, other = hidden(*mlp_in[j], up_fulls[l], down_fulls[l], up_shift[l])
            slopes.append(slope)
            acts.append(act)
            q = core_sum(own, other)
            qs.append(q)
            if l < layers - 1:
                u, m = add_norm(
                    after[j], q, swap_x(q), small, small_full[l + 1], (DB, GAIN1, OFF1)
                )
                following.append(u)
                normed.append(m)
        saved.append((current, attn_in, qkv, kvs, attended, after, mlp_in, slopes, acts))
        current = following
        if l == layers - 1:
            q, come = last_sum(qs)
            final = at_x(after, xi) + (q.astype(f32) + come.astype(f32) + small[DB])
            output = to_rows(final)

    grads = [None] * layers
    vectors = [None] * layers
    biases = [None] * layers
    grad = [v.astype(f32) for v in rounded]
    d_sum = 0.5 * sum(jnp.sum(v, axis=0) for v in grad)
    tokens_grad = None
    top_bit = (lax.axis_index("hi") // (blocks // 2)).astype(jnp.int32)[None]

    waiting = None
    for l in reversed(range(layers)):
        (current, attn_in, qkv, kvs, attended, after, mlp_in, slopes, acts) = saved[l]
        small = small_full[l]
        down_in = [(v, swap_c(v)) for v in rounded]
        des, qs, bias = [], [], 0.0
        for j in range(CHUNKS):
            de, sums, own, other = hidden_back(*down_in[j], slopes[j], up_fulls[l], down_fulls[l])
            des.append(de)
            bias = bias + sums[0]
            qs.append(core_sum(own, other))
        biases[l] = bias
        qs, des, down_in = tie((qs, des, down_in))
        comes = [swap_x(q) for q in qs]
        down_terms = outer([v for pair in down_in for v in pair], acts, top_bit)
        up_terms = outer([v for pair in mlp_in for v in pair], des, top_bit)
        if waiting is None:
            comes, down_terms, up_terms = tie((comes, down_terms, up_terms))
        else:
            waiting = halve_rows(*waiting)
            comes, down_terms, up_terms, waiting = tie((comes, down_terms, up_terms, waiting))
            grads[l + 1][2] = scatter_rows(waiting)
        rounded, mid, sums = [], [], 0.0
        for j in range(CHUNKS):
            g, r, s = norm_back(after[j], qs[j], comes[j], grad[j], small, GAIN2)
            mid.append(g)
            rounded.append(r)
            sums = sums + 0.5 * s
        gain_two_sum, off_two_sum, o_sum = sums[0], sums[1], sums[2]
        out_in = [(v, swap_c(v)) for v in rounded]
        acc, dqs = None, []
        for j in range(CHUNKS):
            dq, acc = attend_back(
                qkv[j], kvs, 0 if ways > 1 else part, query_ids[j], key_ids, out_fulls[l],
                *out_in[j], acc, j == CHUNKS - 1, heads, dim,
            )
            dqs.append(dq)
        if ways > 1:
            acc = acc.reshape(CHUNKS, ways, span, 2 * part).swapaxes(0, 1)
            acc = lax.psum_scatter(
                acc.reshape(ways * CHUNKS * span, 2 * part),
                "seq",
                scatter_dimension=0,
                tiled=True,
                axis_index_groups=seq_groups,
            )
        dqkvs, qs, columns = [], [], 0.0
        for j in range(CHUNKS):
            dqkv, own, other, s = join(dqs[j], acc, j, qkv_fulls[l])
            dqkvs.append(dqkv)
            columns = columns + s[0]
            qs.append(core_sum(own, other))
        down_terms = halve_rows(*down_terms)
        qs, dqkvs, out_in, down_terms = tie((qs, dqkvs, out_in, down_terms))
        down_owned = scatter_rows(down_terms)
        if l > 0:
            comes = [swap_x(q) for q in qs]
        else:
            q, comes = last_sum(qs)
        out_terms = outer_out(
            jnp.concatenate(attended) if CHUNKS > 1 else attended[0],
            [v for pair in out_in for v in pair],
        ).reshape(width, part)
        waiting = outer([v for pair in attn_in for v in pair], dqkvs, top_bit, out_terms)
        up_terms = halve_rows(*up_terms)
        comes, waiting, up_terms = tie((comes, waiting, up_terms))
        up_owned = scatter_rows(up_terms)
        d_next = None
        if l > 0:
            grad, rounded, sums = [], [], 0.0
            for j in range(CHUNKS):
                g, r, s = norm_back(current[j], qs[j], comes[j], mid[j], small, GAIN1)
                grad.append(g)
                rounded.append(r)
                sums = sums + 0.5 * s
            d_next = sums[2]
        else:
            g, r, sums = norm_back(at_x(current, xi), q, comes, at_x(mid, xi), small, GAIN1)
            tokens_grad = to_rows(r)
        vectors[l] = jnp.stack(
            [
                sums[0],
                gain_two_sum,
                sums[1],
                placed(columns[:part]),
                placed(columns[2 * part :]),
                o_sum,
                off_two_sum,
                d_sum,
            ]
        )
        d_sum = d_next
        grads[l] = [up_owned, down_owned, None]

    waiting = halve_rows(*waiting)
    early = [v for l in range(layers) for v in grads[l][: 2 if l == 0 else 3]]
    early, waiting = tie((early, waiting))
    grads[0][2] = scatter_rows(waiting)
    for l in range(1, layers):
        grads[l][2] = early[3 * l + 1]
    early = [v[:, : 3 * part] if i > 2 and i % 3 == 1 else v for i, v in enumerate(early)]
    widths = [v.shape[1] for v in early]
    early = exchange(jnp.concatenate(early, axis=1).reshape(RANKS, held, -1))
    homes = iter(
        lax.slice_in_dim(early, sum(widths[:i]), sum(widths[: i + 1]), axis=2)
        for i in range(len(widths))
    )
    results = [[None] * layers for _ in range(4)]
    for l in range(layers):
        owned = grads[l][2]
        results[1][l] = plain_order(owned[:, 3 * part :].reshape(held, width))
        for i in (2, 3):
            results[i][l] = next(homes)[:, :, :ff_part].transpose(1, 0, 2).reshape(held, ff)
        owned = owned[:, : 3 * part].reshape(RANKS, held, 3 * part)
        qkv_grad = exchange(owned) if l == 0 else next(homes)
        qkv_grad = qkv_grad.reshape(RANKS, held, 3, blocks, chunk).transpose(1, 2, 3, 0, 4)
        results[0][l] = qkv_grad.reshape(held, 3 * width)
    results = [jnp.stack(v).astype(f32) for v in results]

    spots = (jnp.arange(RANKS) == rank)[None, :, None]
    bias = jnp.where(spots, jnp.stack(biases)[:, None, :], 0.0).reshape(layers * RANKS, ff_pad)
    wide = max(ff_pad, width)
    both = jnp.concatenate(
        [
            jnp.pad(jnp.concatenate(vectors), ((0, 0), (0, wide - width))),
            jnp.pad(bias, ((0, 0), (0, wide - ff_pad))),
        ]
    )
    both = sum_everywhere(both)
    vector = both[: layers * kinds, :width].reshape(layers, kinds, blocks, seqs, RANKS, held)
    for axis, index in ((2, "hi"), (2, "seq")):
        vector = pick(vector, lax.axis_index(index), axis)
    vector = pick(vector, rank, 2).swapaxes(1, 2)
    bias = both[layers * kinds :, :ff_part].reshape(layers, ff)
    return (
        output,
        tokens_grad,
        *results,
        bias,
        vector[:, :, :2],
        vector[:, :, 2:],
    )


def solution(mesh):
    sizes = mesh.shape
    devices = mesh.devices.reshape(sizes["img"] // RANKS, 2, 2, sizes["seq"])
    fine = Mesh(devices, AXES)
    row = P(AXES, None)
    param = P(None, AXES, None)
    in_specs = (row, row, P(AXES[:3], None), param, param, param, param, P(), param, param)
    out_specs = (row, row, param, param, param, param, P(), param, param)
    return jax.shard_map(
        body, mesh=fine, in_specs=in_specs, out_specs=out_specs, check_vma=False
    )
```

```python
import functools
import math

import jax
import jax.numpy as jnp
from jax import lax
from jax.experimental import pallas as pl
from jax.experimental.pallas import tpu as pltpu
from jax.sharding import Mesh
from jax.sharding import PartitionSpec as P

HEADS = 16
RANKS = 4
CHUNKS = 1
EPSILON = 1e-06
NEGATIVE = -1e30
ROOT = math.sqrt(2.0 / math.pi)
AXES = ("hi", "x", "c", "seq")
SWAP = ((0, 1), (1, 0))
bf16, f32 = jnp.bfloat16, jnp.float32
VMEM = pl.BlockSpec(memory_space=pltpu.VMEM)


def mm(left, right):
    return jnp.dot(left, right, preferred_element_type=f32)


def mm_last(left, right):
    dims = (((1,), (1,)), ((), ()))
    return lax.dot_general(left, right, dims, preferred_element_type=f32)


def mm_first(left, right):
    dims = (((0,), (0,)), ((), ()))
    return lax.dot_general(left, right, dims, preferred_element_type=f32)


def shape(dims, kind):
    return jax.ShapeDtypeStruct(tuple(dims), kind)


def params(mib):
    return pltpu.CompilerParams(vmem_limit_bytes=mib * 2**20)


def cost(flops, moved, exps=0):
    share = 0.1
    return pl.CostEstimate(
        flops=int(share * flops), bytes_accessed=int(share * moved), transcendentals=int(share * exps)
    )


def const(dims):
    return pl.BlockSpec(tuple(dims), lambda i: (0,) * len(dims))


def columns(weight):
    array, width, place = weight
    return pl.BlockSpec((array.shape[0], width), lambda i: (0, place))


def split(half, block, width):
    n = half // block
    own = pl.BlockSpec((block, width), lambda i: (jnp.minimum(i, n - 1), 0))
    rec = pl.BlockSpec((block, width), lambda i: (jnp.maximum(i - n, 0), 0))
    strip = pl.BlockSpec((block, width), lambda i: (i, 0))
    return n, own, rec, strip


def either(own_work, rec_work):
    step, half = pl.program_id(0), pl.num_programs(0) // 2
    pl.when(step < half)(own_work)
    pl.when(step >= half)(rec_work)


def project_kernel(own_ref, rec_ref, w_ref, shift_ref, out_ref):
    width = out_ref.shape[1]

    def work(ref):
        out_ref[...] = (mm(ref[...], w_ref[:, :width]) + shift_ref[...]).astype(bf16)

    either(lambda: work(own_ref), lambda: work(rec_ref))


def project(own, rec, weight, shift):
    half, depth = own.shape
    width = shift.shape[0]
    n, own_spec, rec_spec, _ = split(half, min(half, 256), depth)
    return pl.pallas_call(
        project_kernel,
        grid=(2 * n,),
        in_specs=[own_spec, rec_spec, columns(weight), const((1, width))],
        out_specs=pl.BlockSpec((half // n, width), lambda i: (i, 0)),
        out_shape=shape((2 * half, width), bf16),
        compiler_params=params(24),
        cost_estimate=cost(4 * half * depth * width, 2 * depth * (2 * half + width)),
    )(own, rec, weight[0], shift[None])


def attend_kernel(heads, dim, offset, count, *refs):
    qid_ref, kid_ref, q_ref, wo_ref = refs[:4]
    kv_refs = refs[4 : 4 + count]
    o_ref, total_ref, own_ref, rec_ref = refs[4 + count :]
    factor = dim**-0.5 * math.log2(math.e)
    width = heads * dim
    same = qid_ref[...] == kid_ref[...]

    def scores(h):
        lo = h * dim
        q = q_ref[:, lo : lo + dim]
        k = jnp.concatenate([ref[:, offset + lo : offset + lo + dim] for ref in kv_refs])
        return jnp.where(same, mm_last(q, k), NEGATIVE)

    keys = sum(ref.shape[0] for ref in kv_refs)
    ones = jnp.ones((keys, 8), bf16)
    outs, totals = [], []
    following = scores(0)
    for h in range(heads):
        at = offset + width + h * dim
        v = jnp.concatenate([ref[:, at : at + dim] for ref in kv_refs])
        s = following
        if h < heads - 1:
            following = scores(h + 1)
        top = jnp.max(s, axis=1, keepdims=True)
        p = jnp.exp2((s - top) * factor).astype(bf16)
        o = mm(p, jnp.concatenate([v, ones], axis=1))
        total = o[:, dim : dim + 1]
        outs.append(o[:, :dim] * (1.0 / total))
        totals.append(top * factor + jnp.log2(total))
    o_ref[...] = jnp.concatenate(outs, axis=1).astype(bf16)
    total_ref[...] = jnp.concatenate(totals + totals, axis=1)

    def own_work():
        own_ref[...] = mm(o_ref[...], wo_ref[...])

    def rec_work():
        rec_ref[...] = mm(o_ref[...], wo_ref[...]).astype(bf16)

    either(own_work, rec_work)


def attend(qkv, kvs, offset, query_ids, key_ids, out_full, heads, dim):
    rows, width, wide = qkv.shape[0], heads * dim, out_full.shape[1]
    keys = sum(kv.shape[0] for kv in kvs)
    n, own_spec, rec_spec, _ = split(rows // 2, min(rows // 2, 512 * 1024 // keys), wide)
    block = rows // (2 * n)
    return pl.pallas_call(
        functools.partial(attend_kernel, heads, dim, offset, len(kvs)),
        grid=(2 * n,),
        in_specs=[
            pl.BlockSpec((block, 1), lambda i: (i, 0)),
            const((1, keys)),
            pl.BlockSpec((block, qkv.shape[1]), lambda i: (i, 0)),
            const(out_full.shape),
        ]
        + [const(kv.shape) for kv in kvs],
        out_specs=[
            pl.BlockSpec((block, width), lambda i: (i, 0)),
            pl.BlockSpec((block, 2 * heads), lambda i: (i, 0)),
            own_spec,
            rec_spec,
        ],
        out_shape=[
            shape((rows, width), bf16),
            shape((rows, 2 * heads), f32),
            shape((rows // 2, wide), f32),
            shape((rows // 2, wide), bf16),
        ],
        compiler_params=params(44),
        cost_estimate=cost(10 * rows * keys * width, 16 * rows * width, heads * rows * keys),
    )(query_ids[:, None], key_ids[None, :], qkv, out_full, *kvs)


def attend_back_kernel(heads, dim, offset, count, first, last, *refs):
    qid_ref, kid_ref, q_ref, o_ref, total_ref, wo_ref, own_ref, rec_ref = refs[:8]
    kv_refs = refs[8 : 8 + count]
    rest = refs[8 + count :]
    if not first:
        before_ref, rest = rest[0], rest[1:]
    dq_ref, dkv_ref, do_ref, acc_ref = rest
    step = pl.program_id(0)
    scale = dim**-0.5
    factor = scale * math.log2(math.e)
    width = heads * dim

    @pl.when(step == 0)
    def _():
        acc_ref[...] = jnp.zeros_like(acc_ref) if first else before_ref[...]

    def own_work():
        do_ref[...] = mm_last(own_ref[...], wo_ref[...]).astype(bf16)

    def rec_work():
        do_ref[...] = mm_last(rec_ref[...], wo_ref[...]).astype(bf16)

    either(own_work, rec_work)
    same = kid_ref[...] == qid_ref[...]
    ones = jnp.ones((8, dim), bf16)
    dqs = []
    for h in range(heads):
        lo = h * dim
        at = offset + width + lo
        q = q_ref[:, lo : lo + dim]
        do = do_ref[:, lo : lo + dim]
        k = jnp.concatenate([ref[:, offset + lo : offset + lo + dim] for ref in kv_refs])
        v = jnp.concatenate([ref[:, at : at + dim] for ref in kv_refs])
        s = jnp.where(same, mm_last(k, q), NEGATIVE)
        p = jnp.exp2(s * factor - total_ref[h : h + 1, :])
        dp = mm_last(v, do)
        both = do.astype(f32) * o_ref[:, lo : lo + dim].astype(f32)
        high = both.astype(bf16)
        delta = mm_last(ones, high) + mm_last(ones, (both - high.astype(f32)).astype(bf16))
        ds = (p * (dp - delta[:1])).astype(bf16)
        acc_ref[heads + h] += mm(p.astype(bf16), do)
        acc_ref[h] += mm(ds, q)
        dqs.append(mm_first(ds, k) * scale)
    dq_ref[...] = jnp.concatenate(dqs, axis=1).astype(bf16)

    @pl.when(step == pl.num_programs(0) - 1)
    def _():
        if last:
            parts = [acc_ref[h] * scale for h in range(heads)]
            parts += [acc_ref[heads + h] for h in range(heads)]
            dkv_ref[...] = jnp.concatenate(parts, axis=1).astype(bf16)
        else:
            dkv_ref[...] = acc_ref[...]


def attend_back(
    qkv, kvs, offset, query_ids, key_ids, o, totals, out_full, own, rec, before, last, heads, dim
):
    rows, width, wide = qkv.shape[0], heads * dim, out_full.shape[1]
    keys = sum(kv.shape[0] for kv in kvs)
    sums = (2 * heads, keys, dim)
    extra = [] if before is None else [before]
    n, own_spec, rec_spec, _ = split(rows // 2, min(rows // 2, 512 * 1024 // keys), wide)
    block = rows // (2 * n)
    done = shape((keys, 2 * width), bf16) if last else shape(sums, f32)
    return pl.pallas_call(
        functools.partial(attend_back_kernel, heads, dim, offset, len(kvs), before is None, last),
        grid=(2 * n,),
        in_specs=[
            pl.BlockSpec((1, block), lambda i: (0, i)),
            const((keys, 1)),
            pl.BlockSpec((block, qkv.shape[1]), lambda i: (i, 0)),
            pl.BlockSpec((block, width), lambda i: (i, 0)),
            pl.BlockSpec((2 * heads, block), lambda i: (0, i)),
            const(out_full.shape),
            own_spec,
            rec_spec,
        ]
        + [const(v.shape) for v in list(kvs) + extra],
        out_specs=[pl.BlockSpec((block, width), lambda i: (i, 0)), const(done.shape)],
        out_shape=[shape((rows, width), bf16), done],
        scratch_shapes=[pltpu.VMEM((block, width), bf16), pltpu.VMEM(sums, f32)],
        compiler_params=params(52),
        cost_estimate=cost(24 * rows * keys * width, 30 * rows * width, heads * rows * keys),
    )(query_ids[None, :], key_ids[:, None], qkv, o, totals.T, out_full, own, rec, *kvs, *extra)


def join_kernel(dq_ref, dkv_ref, w_ref, dqkv_ref, own_ref, rec_ref, sum_ref):
    @pl.when(pl.program_id(0) == 0)
    def _():
        sum_ref[...] = jnp.zeros_like(sum_ref)

    dqkv = jnp.concatenate([dq_ref[...], dkv_ref[...]], axis=1)
    dqkv_ref[...] = dqkv
    sum_ref[...] += jnp.sum(dqkv.astype(f32), axis=0, keepdims=True)
    width = dqkv.shape[1]

    def own_work():
        own_ref[...] = mm_last(dqkv_ref[...], w_ref[:, :width])

    def rec_work():
        rec_ref[...] = mm_last(dqkv_ref[...], w_ref[:, :width]).astype(bf16)

    either(own_work, rec_work)


def join(dq, dkv, chunk, weight):
    rows, width, wide = dq.shape[0], dq.shape[1] + dkv.shape[1], weight[0].shape[0]
    n, own_spec, rec_spec, _ = split(rows // 2, min(rows // 2, 256), wide)
    block, at = rows // (2 * n), 2 * n * chunk
    return pl.pallas_call(
        join_kernel,
        grid=(2 * n,),
        in_specs=[
            pl.BlockSpec((block, dq.shape[1]), lambda i: (i, 0)),
            pl.BlockSpec((block, dkv.shape[1]), lambda i: (at + i, 0)),
            columns(weight),
        ],
        out_specs=[pl.BlockSpec((block, width), lambda i: (i, 0)), own_spec, rec_spec, const((1, width))],
        out_shape=[
            shape((rows, width), bf16),
            shape((rows // 2, wide), f32),
            shape((rows // 2, wide), bf16),
            shape((1, width), f32),
        ],
        compiler_params=params(24),
        cost_estimate=cost(2 * rows * width * wide, 4 * wide * (rows + width)),
    )(dq, dkv, weight[0])


def hidden_kernel(own_ref, rec_ref, up_ref, down_ref, shift_ref, slope_ref, act_ref, po_ref, pr_ref):
    def work(ref, out_ref):
        e = mm(ref[...], up_ref[...]) + shift_ref[...]
        square = e * e
        h = 0.5 * jnp.tanh(e * (square * (ROOT * 0.044715) + ROOT)) + 0.5
        g = e * h
        slope = h + g * (1.0 - h) * (square * (6 * ROOT * 0.044715) + 2 * ROOT)
        g = g.astype(bf16)
        act_ref[...] = g
        slope_ref[...] = slope.astype(bf16)
        out_ref[...] = mm_last(g, down_ref[...]).astype(out_ref.dtype)

    either(lambda: work(own_ref, po_ref), lambda: work(rec_ref, pr_ref))


def tile_of(size):
    return 384 if size % 384 == 0 else 128


def hidden(own, rec, up, down, shift):
    half, wide = own.shape
    ff = up[1]
    n, own_spec, rec_spec, _ = split(half, min(half, 256), wide)
    strip = pl.BlockSpec((half // n, ff), lambda i: (i, 0))
    return pl.pallas_call(
        hidden_kernel,
        grid=(2 * n,),
        in_specs=[own_spec, rec_spec, columns(up), columns(down), const((1, ff))],
        out_specs=[strip, strip, own_spec, rec_spec],
        out_shape=[
            shape((2 * half, ff), bf16),
            shape((2 * half, ff), bf16),
            shape((half, wide), f32),
            shape((half, wide), bf16),
        ],
        compiler_params=params(30),
        cost_estimate=cost(8 * half * wide * ff, 4 * wide * ff + 20 * half * wide, 2 * half * ff),
    )(own, rec, up[0], down[0], shift[None])


def hidden_back_kernel(own_ref, rec_ref, slope_ref, up_ref, down_ref, de_ref, sum_ref, po_ref, pr_ref):
    @pl.when(pl.program_id(0) == 0)
    def _():
        sum_ref[...] = jnp.zeros_like(sum_ref)

    def work(ref, out_ref):
        de = (mm(ref[...], down_ref[...]) * slope_ref[...].astype(f32)).astype(bf16)
        de_ref[...] = de
        sum_ref[...] += jnp.sum(de.astype(f32), axis=0, keepdims=True)
        out_ref[...] = mm_last(de, up_ref[...]).astype(out_ref.dtype)

    either(lambda: work(own_ref, po_ref), lambda: work(rec_ref, pr_ref))


def hidden_back(own, rec, slope, up, down):
    half, wide = own.shape
    ff = up[1]
    n, own_spec, rec_spec, _ = split(half, min(half, 256), wide)
    strip = pl.BlockSpec((half // n, ff), lambda i: (i, 0))
    return pl.pallas_call(
        hidden_back_kernel,
        grid=(2 * n,),
        in_specs=[own_spec, rec_spec, strip, columns(up), columns(down)],
        out_specs=[strip, const((1, ff)), own_spec, rec_spec],
        out_shape=[
            shape((2 * half, ff), bf16),
            shape((1, ff), f32),
            shape((half, wide), f32),
            shape((half, wide), bf16),
        ],
        compiler_params=params(30),
        cost_estimate=cost(8 * half * wide * ff, 4 * wide * ff + 16 * half * wide),
    )(own, rec, slope, up[0], down[0])


def outer_kernel(lefts, rights, beside, bit_ref, *refs):
    left_refs, right_refs = refs[:lefts], refs[lefts : lefts + rights]
    rest = refs[lefts + rights :]
    if beside:
        beside_ref, rest = rest[0], rest[1:]
    mine_ref, theirs_ref = rest
    turned = right_refs[0].shape[0]
    cuts = [ref.shape[0] for ref in left_refs]
    total, at = None, 0
    for ref, size in zip(left_refs, cuts):
        low = at % turned
        right = right_refs[at // turned]
        part = mm_first(ref[...], right[low : low + size, :])
        total = part if total is None else total + part
        at += size
    out = total.astype(bf16)
    if beside:
        out = jnp.concatenate([out, beside_ref[...]], axis=1)
    half = out.shape[0] // 2

    @pl.when(bit_ref[0] == 0)
    def _():
        mine_ref[...], theirs_ref[...] = out[:half], out[half:]

    @pl.when(bit_ref[0] == 1)
    def _():
        mine_ref[...], theirs_ref[...] = out[half:], out[:half]


def outer(lefts, rights, bit, beside=None):
    depth, width = lefts[0].shape[1], rights[0].shape[1]
    rows = sum(v.shape[0] for v in lefts)
    extra = [] if beside is None else [beside]
    out = shape((depth // 2, width + sum(v.shape[1] for v in extra)), bf16)
    return pl.pallas_call(
        functools.partial(outer_kernel, len(lefts), len(rights), len(extra)),
        in_specs=[pl.BlockSpec(memory_space=pltpu.SMEM)]
        + [VMEM] * (len(lefts) + len(rights) + len(extra)),
        out_specs=[VMEM] * 2,
        out_shape=[out] * 2,
        compiler_params=params(30),
        cost_estimate=cost(2 * rows * depth * width, 2 * rows * (depth + width) + 2 * depth * width),
    )(bit, *lefts, *rights, *extra)


def outer_out_kernel(count, o_ref, *refs):
    out_ref = refs[count]
    total, at = None, 0
    for ref in refs[:count]:
        part = mm_first(o_ref[at : at + ref.shape[0], :], ref[...])
        total = part if total is None else total + part
        at += ref.shape[0]
    out_ref[...] = total.astype(bf16)


def outer_out(attended, rights):
    depth, width, rows = attended.shape[1], rights[0].shape[1], attended.shape[0]
    return pl.pallas_call(
        functools.partial(outer_out_kernel, len(rights)),
        in_specs=[VMEM] * (1 + len(rights)),
        out_specs=VMEM,
        out_shape=shape((depth, width), bf16),
        compiler_params=params(24),
        cost_estimate=cost(2 * rows * depth * width, 2 * rows * (depth + width) + 2 * depth * width),
    )(attended, *rights)


def spread(v):
    centred = v - jnp.mean(v, axis=-1, keepdims=True)
    scale = lax.rsqrt(jnp.mean(centred * centred, axis=-1, keepdims=True) + EPSILON)
    return centred * scale, scale


def norm_kernel(rows_of, v_ref, q_ref, come_ref, small_ref, next_ref, u_ref, m_ref):
    shift, gain, offset = rows_of
    u = v_ref[...] + (q_ref[...].astype(f32) + come_ref[...].astype(f32) + small_ref[shift : shift + 1, :])
    u_ref[...] = u
    n = spread(u)[0] * next_ref[gain : gain + 1, :] + next_ref[offset : offset + 1, :]
    m_ref[...] = n.astype(bf16)


def add_norm(v, q, come, small, following, rows_of):
    rows, width = v.shape
    block = pl.BlockSpec((min(rows, 256), width), lambda i: (i, 0))
    return pl.pallas_call(
        functools.partial(norm_kernel, rows_of),
        grid=(rows // min(rows, 256),),
        in_specs=[block] * 3 + [const(small.shape)] * 2,
        out_specs=[block] * 2,
        out_shape=[shape(v.shape, f32), shape(v.shape, bf16)],
        compiler_params=params(16),
        cost_estimate=cost(12 * v.size, 14 * v.size),
    )(v, q, come, small, following)


def norm_back_kernel(gain, v_ref, q_ref, come_ref, grad_ref, small_ref, out_ref, round_ref, sum_ref):
    @pl.when(pl.program_id(0) == 0)
    def _():
        sum_ref[...] = jnp.zeros_like(sum_ref)

    t = q_ref[...].astype(f32) + come_ref[...].astype(f32)
    n, scale = spread(v_ref[...])
    w = t * small_ref[gain : gain + 1, :]
    mean_w = jnp.mean(w, axis=-1, keepdims=True)
    mean_wn = jnp.mean(w * n, axis=-1, keepdims=True)
    out = grad_ref[...] + scale * (w - mean_w - n * mean_wn)
    out_ref[...] = out
    rounded = out.astype(bf16)
    round_ref[...] = rounded
    sum_ref[0:1, :] += jnp.sum(t * n, axis=0, keepdims=True)
    sum_ref[1:2, :] += jnp.sum(t, axis=0, keepdims=True)
    sum_ref[2:3, :] += jnp.sum(rounded.astype(f32), axis=0, keepdims=True)


def norm_back(v, q, come, grad, small, gain):
    rows, width = v.shape
    block = pl.BlockSpec((min(rows, 256), width), lambda i: (i, 0))
    return pl.pallas_call(
        functools.partial(norm_back_kernel, gain),
        grid=(rows // min(rows, 256),),
        in_specs=[block] * 4 + [const(small.shape)],
        out_specs=[block] * 2 + [const((8, width))],
        out_shape=[shape(v.shape, f32), shape(v.shape, bf16), shape((8, width), f32)],
        compiler_params=params(20),
        cost_estimate=cost(24 * v.size, 18 * v.size),
    )(v, q, come, grad, small)


def tie(values):
    return lax.optimization_barrier(values)


def pick(array, index, axis=0):
    return lax.dynamic_index_in_dim(array, index, axis, keepdims=False)


def swap_x(v):
    return lax.ppermute(v, "x", SWAP)


def swap_c(v):
    return lax.ppermute(v, "c", SWAP)


def in_order(axis, own, other):
    first = lax.axis_index(axis) == 0
    return jnp.where(first, own, other), jnp.where(first, other, own)


def exchange(blocks):
    xi, ci = lax.axis_index("x"), lax.axis_index("c")
    blocks = blocks.reshape((2, 2) + blocks.shape[1:])
    both = jnp.stack(in_order("x", pick(blocks, xi), swap_x(pick(blocks, 1 - xi))))
    out = in_order("c", pick(both, ci, 1), swap_c(pick(both, 1 - ci, 1)))
    return jnp.stack(out, axis=1).reshape((RANKS,) + blocks.shape[2:])


def flip(v, axis, step):
    size = lax.axis_size(axis)
    return lax.ppermute(v, axis, [(i, i ^ step) for i in range(size)])


def gather_rows(payload):
    return lax.all_gather(payload, ("hi", "seq"), axis=0, tiled=True)


def halve_rows(mine, theirs):
    step = lax.axis_size("hi") // 2
    place = lax.axis_index("hi")
    terms = (mine.astype(f32) + flip(theirs, "hi", step).astype(f32)).astype(bf16)
    step //= 2
    while step:
        halves = terms.reshape((2, -1) + terms.shape[1:])
        bit = (place // step) % 2
        come = flip(pick(halves, 1 - bit), "hi", step)
        terms = (pick(halves, bit).astype(f32) + come.astype(f32)).astype(bf16)
        step //= 2
    return terms


def scatter_rows(terms):
    return lax.psum_scatter(terms, "seq", scatter_dimension=0, tiled=True)


def body(
    tokens,
    cotangent,
    image_lengths,
    qkv_weight,
    out_weight,
    up_weight,
    down_weight,
    up_bias,
    norm_scale,
    shifts,
):
    rows, width = tokens.shape
    layers, held = qkv_weight.shape[0], qkv_weight.shape[1]
    blocks, seqs = lax.axis_size("hi"), lax.axis_size("seq")
    ways = seqs // RANKS
    shards = blocks * seqs
    chunk = seqs * held
    heads = HEADS // RANKS
    dim = width // HEADS
    part = width // RANKS
    ff = up_weight.shape[2]
    ff_part = ff // RANKS
    ff_pad = -(-ff_part // 128) * 128
    xi, ci = lax.axis_index("x"), lax.axis_index("c")
    rank = 2 * xi + ci

    spot = jnp.arange(width, dtype=jnp.int32)
    natural = ((spot // (RANKS * held * seqs) * RANKS + spot // held % RANKS) * seqs) * held
    natural = natural + spot // (RANKS * held) % seqs * held + spot % held
    turn_matrix = (spot[:, None] == natural[None, :]).astype(bf16)

    def mixed_order(v):
        return mm(v, turn_matrix).astype(bf16)

    def plain_order(v):
        return mm_last(v, turn_matrix)

    def mine(v):
        return pick(v.reshape(blocks, seqs, RANKS, held), rank, 2).reshape(part)

    def placed(v):
        v = v.reshape(blocks, seqs, 1, held)
        spots = (jnp.arange(RANKS) == rank)[None, None, :, None]
        return jnp.where(spots, v, 0.0).reshape(width)

    there = []
    for b in range(blocks):
        for r in range(RANKS):
            for s in range(seqs):
                target = (b * RANKS + s % RANKS) * seqs + r * ways + s // RANKS
                there.append(((b * RANKS + r) * seqs + s, target))
    back = [(target, source) for source, target in there]

    def rank_columns(piece):
        piece = piece.reshape(held, 3, blocks, RANKS, chunk)
        return piece.transpose(3, 0, 1, 2, 4).reshape(RANKS, held, 3 * part)

    def ff_columns(piece):
        piece = piece.reshape(held, RANKS, ff_part).transpose(1, 0, 2)
        return jnp.pad(piece, ((0, 0), (0, 0), (0, ff_pad - ff_part)))

    def out_rows(l):
        return mixed_order(out_weight[l]).reshape(held * RANKS, part)

    kinds = norm_scale.shape[2] + shifts.shape[2]
    smalls = jnp.concatenate([norm_scale, shifts], axis=2)
    smalls = smalls.transpose(1, 0, 2).reshape(1, held, layers * kinds)
    smalls = jnp.broadcast_to(smalls, (RANKS, held, layers * kinds))

    qkv_fulls, out_fulls, up_fulls, down_fulls = [], [], [], []
    came = exchange(jnp.concatenate([rank_columns(qkv_weight[0]), smalls], axis=2))
    came = came.reshape(RANKS * held, -1)
    payload = jnp.concatenate([came[:, : 3 * part], out_rows(0), came[:, 3 * part :]], axis=1)
    first = gather_rows(payload)
    small_full = first[:, width:].T.reshape(layers, kinds, width).astype(f32)
    qkv_fulls.append((first, first.shape[1], 0))
    out_fulls.append(first[:, 3 * part : width].reshape(part, width))
    later = [
        ff_columns(piece) for l in range(layers) for piece in (up_weight[l], down_weight[l])
    ] + [rank_columns(qkv_weight[l]) for l in range(1, layers)]
    arrived = lax.ppermute(tokens, AXES, there)
    later, arrived, _ = tie((jnp.concatenate(later, axis=2), arrived, payload))
    later = exchange(later).reshape(RANKS * held, -1)
    for l in range(layers):
        if l > 0:
            at = 2 * layers * ff_pad + (l - 1) * 3 * part
            payload = jnp.concatenate([later[:, at : at + 3 * part], out_rows(l)], axis=1)
            full = gather_rows(payload)
            qkv_fulls.append((full, width, 0))
            out_fulls.append(full[:, 3 * part :].reshape(part, width))
        full = gather_rows(later[:, 2 * l * ff_pad : 2 * (l + 1) * ff_pad])
        up_fulls.append((full, ff_pad, 0))
        down_fulls.append((full, ff_pad, 1))
    up_shift = pick(up_bias.reshape(layers, RANKS, ff_part), rank, 1).astype(f32)
    up_shift = jnp.pad(up_shift, ((0, 0), (0, ff_pad - ff_part)))

    xs = [(0, 1)] if CHUNKS == 1 else [(0,), (1,)]
    span = 4 * rows // CHUNKS
    lengths = lax.ppermute(image_lengths, AXES, there)
    finish = jnp.cumsum(lengths[0])
    base = jnp.arange(rows, dtype=jnp.int32)
    local = [
        jnp.concatenate([base + (2 * x + c) * rows for c in (ci, 1 - ci) for x in chunk_xs])
        for chunk_xs in xs
    ]
    group = RANKS * rows
    turn = lax.axis_index("seq") % ways

    def ids_of(pos):
        return jnp.sum((pos[:, None] >= finish[None, :]).astype(jnp.int32), axis=1)

    query_ids = [ids_of(v + turn * group) for v in local]
    key_ids = ids_of(jnp.concatenate([v + w * group for v in local for w in range(ways)]))
    seq_groups = [[j * ways + w for w in range(ways)] for j in range(seqs // ways)]

    def keys_of(qkv):
        if ways == 1:
            return qkv, part
        kv = lax.all_gather(
            qkv[:, part:], "seq", axis=0, tiled=True, axis_index_groups=seq_groups
        )
        return kv, 0

    def chunks_of(v):
        own = mixed_order(v)
        pair = in_order("x", own, swap_x(own))
        return list(pair) if CHUNKS == 2 else [jnp.concatenate(pair)]

    def at_x(chunks, index):
        if CHUNKS == 2:
            return jnp.where(index == 0, chunks[0], chunks[1])
        return pick(chunks[0].reshape((2, rows) + chunks[0].shape[1:]), index)

    def core_sum(own, other):
        return (own + swap_c(other).astype(f32)).astype(bf16)

    def last_sum(qs):
        return at_x(qs, xi), swap_x(at_x(qs, 1 - xi))

    GAIN1, GAIN2, OFF1, QB, VB, OB, OFF2, DB = range(8)
    starts = chunks_of(arrived)
    current = [v.astype(f32) for v in starts]
    normed = [
        (spread(v)[0] * small_full[0, GAIN1] + small_full[0, OFF1]).astype(bf16) for v in current
    ]
    saved = []
    output = None
    for l in range(layers):
        small = small_full[l]
        attn_in = [(v, swap_c(v)) for v in normed]
        shift = jnp.concatenate([mine(small[QB]), jnp.zeros((part,), f32), mine(small[VB])])
        qkv = [project(own, rec, qkv_fulls[l], shift) for own, rec in attn_in]
        kvs = [keys_of(v) for v in qkv]
        offset, kvs = kvs[0][1], [v[0] for v in kvs]
        attended, totals, after, normed = [], [], [], []
        for j in range(CHUNKS):
            o, total, own, other = attend(
                qkv[j], kvs, offset, query_ids[j], key_ids, out_fulls[l], heads, dim
            )
            attended.append(o)
            totals.append(total)
            q = core_sum(own, other)
            if l == layers - 1 and j == 0:
                q, cotangent = tie((q, cotangent))
                arrived = lax.ppermute(cotangent, AXES, there)
            come = swap_x(q)
            if l == layers - 1 and j == 0:
                come, arrived = tie((come, arrived))
            u, m = add_norm(current[j], q, come, small, small, (OB, GAIN2, OFF2))
            after.append(u)
            normed.append(m)
        mlp_in = [(v, swap_c(v)) for v in normed]
        if l == layers - 1:
            rounded = chunks_of(arrived)
        slopes, acts, qs, following, normed = [], [], [], [], []
        for j in range(CHUNKS):
            slope, act, own, other = hidden(*mlp_in[j], up_fulls[l], down_fulls[l], up_shift[l])
            slopes.append(slope)
            acts.append(act)
            q = core_sum(own, other)
            qs.append(q)
            if l < layers - 1:
                u, m = add_norm(
                    after[j], q, swap_x(q), small, small_full[l + 1], (DB, GAIN1, OFF1)
                )
                following.append(u)
                normed.append(m)
        saved.append((current, attn_in, qkv, kvs, attended, totals, after, mlp_in, slopes, acts))
        current = following
        if l == layers - 1:
            output = (qs, after, small[DB])

    grads = [None] * layers
    vectors = [None] * layers
    biases = [None] * layers
    grad = [v.astype(f32) for v in rounded]
    d_sum = 0.5 * sum(jnp.sum(v, axis=0) for v in grad)
    tokens_grad = None
    top_bit = (lax.axis_index("hi") // (blocks // 2)).astype(jnp.int32)[None]

    def home_of(pieces):
        return exchange(jnp.concatenate(pieces, axis=1).reshape(RANKS, held, -1))


    waiting, homes = None, [None] * layers
    for l in reversed(range(layers)):
        (current, attn_in, qkv, kvs, attended, totals, after, mlp_in, slopes, acts) = saved[l]
        small = small_full[l]
        last_layer = waiting is None
        down_in = [(v, swap_c(v)) for v in rounded]
        down_terms = outer([v for pair in down_in for v in pair], acts, top_bit)
        down_in, down_terms = tie((down_in, down_terms))
        des, qs, bias = [], [], 0.0
        for j in range(CHUNKS):
            de, sums, own, other = hidden_back(*down_in[j], slopes[j], up_fulls[l], down_fulls[l])
            des.append(de)
            bias = bias + sums[0]
            qs.append(core_sum(own, other))
        biases[l] = bias
        if last_layer:
            qs, des = tie((qs, des))
        else:
            waiting = halve_rows(*waiting)
            qs, des, waiting = tie((qs, des, waiting))
            waiting = scatter_rows(waiting)
        comes = [swap_x(q) for q in qs]
        up_terms = outer([v for pair in mlp_in for v in pair], des, top_bit)
        down_terms = halve_rows(*down_terms)
        if last_layer:
            comes, down_terms, up_terms, output = tie((comes, down_terms, up_terms, output))
            q, come = last_sum(output[0])
            output = at_x(output[1], xi) + (q.astype(f32) + come.astype(f32) + output[2])
            output = output.astype(bf16)
        else:
            comes, down_terms, up_terms, grads[l + 1][2], output = tie(
                (comes, down_terms, up_terms, waiting, output)
            )
            output = lax.ppermute(output, AXES, back)
        down_owned = scatter_rows(down_terms)
        rounded, mid, sums = [], [], 0.0
        for j in range(CHUNKS):
            g, r, s = norm_back(after[j], qs[j], comes[j], grad[j], small, GAIN2)
            mid.append(g)
            rounded.append(r)
            sums = sums + 0.5 * s
        gain_two_sum, off_two_sum, o_sum = sums[0], sums[1], sums[2]
        out_in = [(v, swap_c(v)) for v in rounded]
        acc, dqs = None, []
        for j in range(CHUNKS):
            dq, acc = attend_back(
                qkv[j], kvs, 0 if ways > 1 else part, query_ids[j], key_ids, attended[j],
                totals[j], out_fulls[l], *out_in[j], acc, j == CHUNKS - 1, heads, dim,
            )
            dqs.append(dq)
        if ways > 1:
            acc = acc.reshape(CHUNKS, ways, span, 2 * part).swapaxes(0, 1)
            acc = lax.psum_scatter(
                acc.reshape(ways * CHUNKS * span, 2 * part),
                "seq",
                scatter_dimension=0,
                tiled=True,
                axis_index_groups=seq_groups,
            )
        if not last_layer:
            dqs, acc, output = tie((dqs, acc, output))
        dqkvs, qs, sums_qkv = [], [], 0.0
        for j in range(CHUNKS):
            dqkv, own, other, s = join(dqs[j], acc, j, qkv_fulls[l])
            dqkvs.append(dqkv)
            sums_qkv = sums_qkv + s[0]
            qs.append(core_sum(own, other))
        up_terms = halve_rows(*up_terms)
        if last_layer:
            qs, dqkvs, out_in, up_terms, down_owned, output = tie(
                (qs, dqkvs, out_in, up_terms, down_owned, output)
            )
        else:
            qs, dqkvs, out_in, up_terms, down_owned = tie(
                (qs, dqkvs, out_in, up_terms, down_owned)
            )
        up_owned = scatter_rows(up_terms)
        if l > 0:
            comes = [swap_x(q) for q in qs]
        else:
            q, comes = last_sum(qs)
        out_terms = outer_out(
            jnp.concatenate(attended) if CHUNKS > 1 else attended[0],
            [v for pair in out_in for v in pair],
        ).reshape(width, part)
        waiting = outer([v for pair in attn_in for v in pair], dqkvs, top_bit, out_terms)
        if not last_layer:
            homes[l + 1] = home_of([grads[l + 1][0], grads[l + 1][1], grads[l + 1][2][:, : 3 * part]])
            comes, homes[l + 1] = tie((comes, homes[l + 1]))
        comes, waiting, up_owned = tie((comes, waiting, up_owned))
        d_next = None
        if l > 0:
            grad, rounded, sums = [], [], 0.0
            for j in range(CHUNKS):
                g, r, s = norm_back(current[j], qs[j], comes[j], mid[j], small, GAIN1)
                grad.append(g)
                rounded.append(r)
                sums = sums + 0.5 * s
            d_next = sums[2]
        else:
            g, r, sums = norm_back(at_x(current, xi), q, comes, at_x(mid, xi), small, GAIN1)
            tokens_grad = r
        vectors[l] = jnp.stack(
            [
                sums[0],
                gain_two_sum,
                sums[1],
                placed(sums_qkv[:part]),
                placed(sums_qkv[2 * part :]),
                o_sum,
                off_two_sum,
                d_sum,
            ]
        )
        d_sum = d_next
        grads[l] = [up_owned, down_owned, None]

    spots = (jnp.arange(RANKS) == rank)[None, :, None]
    bias = jnp.where(spots, jnp.stack(biases)[:, None, :], 0.0).reshape(layers * RANKS, ff_pad)
    wide = max(ff_pad, width)
    both = jnp.concatenate(
        [
            jnp.pad(jnp.concatenate(vectors), ((0, 0), (0, wide - width))),
            jnp.pad(bias, ((0, 0), (0, wide - ff_pad))),
        ]
    )
    tokens_grad = lax.ppermute(tokens_grad, AXES, back)

    def sum_along(v, axis):
        step = 1
        while step < lax.axis_size(axis):
            v = v + flip(v, axis, step)
            step *= 2
        return v

    both = sum_along(sum_along(sum_along(both, "c"), "x"), "hi")
    mine_last, theirs_last = waiting
    mine_last, both, tokens_grad = tie((mine_last, both, tokens_grad))
    last = scatter_rows(halve_rows(mine_last, theirs_last))
    both = sum_along(both, "seq")
    grads[0][2] = last
    homes[0] = home_of([grads[0][0], grads[0][1], last[:, : 3 * part]])
    results = [[None] * layers for _ in range(4)]
    for l in range(layers):
        owned = grads[l][2]
        results[1][l] = plain_order(owned[:, 3 * part :].reshape(held, width))
        for i in (2, 3):
            home = homes[l][:, :, (i - 2) * ff_pad : (i - 2) * ff_pad + ff_part]
            results[i][l] = home.transpose(1, 0, 2).reshape(held, ff)
        qkv_grad = homes[l][:, :, 2 * ff_pad :]
        qkv_grad = qkv_grad.reshape(RANKS, held, 3, blocks, chunk).transpose(1, 2, 3, 0, 4)
        results[0][l] = qkv_grad.reshape(held, 3 * width)
    results = [jnp.stack(v).astype(f32) for v in results]

    vector = both[: layers * kinds, :width].reshape(layers, kinds, blocks, seqs, RANKS, held)
    for axis, index in ((2, "hi"), (2, "seq")):
        vector = pick(vector, lax.axis_index(index), axis)
    vector = pick(vector, rank, 2).swapaxes(1, 2)
    bias = both[layers * kinds :, :ff_part].reshape(layers, ff)
    return (
        plain_order(output),
        plain_order(tokens_grad),
        *results,
        bias,
        vector[:, :, :2],
        vector[:, :, 2:],
    )


def solution(mesh):
    sizes = mesh.shape
    devices = mesh.devices.reshape(sizes["img"] // RANKS, 2, 2, sizes["seq"])
    fine = Mesh(devices, AXES)
    row = P(AXES, None)
    param = P(None, AXES, None)
    in_specs = (row, row, P(AXES[:3], None), param, param, param, param, P(), param, param)
    out_specs = (row, row, param, param, param, param, P(), param, param)
    return jax.shard_map(
        body, mesh=fine, in_specs=in_specs, out_specs=out_specs, check_vma=False
    )
```

```python
import functools
import math

import jax
import jax.numpy as jnp
from jax import lax
from jax.experimental import pallas as pl
from jax.experimental.pallas import tpu as pltpu
from jax.sharding import Mesh
from jax.sharding import PartitionSpec as P

HEADS = 16
RANKS = 4
CHUNKS = 1
EPSILON = 1e-06
NEGATIVE = -1e30
ROOT = math.sqrt(2.0 / math.pi)
AXES = ("hi", "x", "c", "seq")
SWAP = ((0, 1), (1, 0))
bf16, f32 = jnp.bfloat16, jnp.float32
VMEM = pl.BlockSpec(memory_space=pltpu.VMEM)


def mm(left, right):
    return jnp.dot(left, right, preferred_element_type=f32)


def mm_last(left, right):
    dims = (((1,), (1,)), ((), ()))
    return lax.dot_general(left, right, dims, preferred_element_type=f32)


def mm_first(left, right):
    dims = (((0,), (0,)), ((), ()))
    return lax.dot_general(left, right, dims, preferred_element_type=f32)


def shape(dims, kind):
    return jax.ShapeDtypeStruct(tuple(dims), kind)


def params(mib):
    return pltpu.CompilerParams(vmem_limit_bytes=mib * 2**20)


def cost(flops, moved, exps=0):
    share = 0.1
    return pl.CostEstimate(
        flops=int(share * flops), bytes_accessed=int(share * moved), transcendentals=int(share * exps)
    )


def const(dims):
    return pl.BlockSpec(tuple(dims), lambda i: (0,) * len(dims))


def columns(weight):
    array, width, place = weight
    return pl.BlockSpec((array.shape[0], width), lambda i: (0, place))


def split(half, block, width):
    n = half // block
    own = pl.BlockSpec((block, width), lambda i: (jnp.minimum(i, n - 1), 0))
    rec = pl.BlockSpec((block, width), lambda i: (jnp.maximum(i - n, 0), 0))
    strip = pl.BlockSpec((block, width), lambda i: (i, 0))
    return n, own, rec, strip


def either(own_work, rec_work):
    step, half = pl.program_id(0), pl.num_programs(0) // 2
    pl.when(step < half)(own_work)
    pl.when(step >= half)(rec_work)


def project_kernel(own_ref, rec_ref, w_ref, shift_ref, out_ref):
    width = out_ref.shape[1]

    def work(ref):
        out_ref[...] = (mm(ref[...], w_ref[:, :width]) + shift_ref[...]).astype(bf16)

    either(lambda: work(own_ref), lambda: work(rec_ref))


def project(own, rec, weight, shift):
    half, depth = own.shape
    width = shift.shape[0]
    n, own_spec, rec_spec, _ = split(half, min(half, 256), depth)
    return pl.pallas_call(
        project_kernel,
        grid=(2 * n,),
        in_specs=[own_spec, rec_spec, columns(weight), const((1, width))],
        out_specs=pl.BlockSpec((half // n, width), lambda i: (i, 0)),
        out_shape=shape((2 * half, width), bf16),
        compiler_params=params(24),
        cost_estimate=cost(4 * half * depth * width, 2 * depth * (2 * half + width)),
    )(own, rec, weight[0], shift[None])


def attend_kernel(heads, dim, offset, count, *refs):
    qid_ref, kid_ref, q_ref, wo_ref = refs[:4]
    kv_refs = refs[4 : 4 + count]
    o_ref, total_ref, own_ref, rec_ref = refs[4 + count :]
    factor = dim**-0.5 * math.log2(math.e)
    width = heads * dim
    same = qid_ref[...] == kid_ref[...]

    def scores(h):
        lo = h * dim
        q = q_ref[:, lo : lo + dim]
        k = jnp.concatenate([ref[:, offset + lo : offset + lo + dim] for ref in kv_refs])
        return jnp.where(same, mm_last(q, k), NEGATIVE)

    keys = sum(ref.shape[0] for ref in kv_refs)
    ones = jnp.ones((keys, 8), bf16)
    outs, totals = [], []
    following = scores(0)
    for h in range(heads):
        at = offset + width + h * dim
        v = jnp.concatenate([ref[:, at : at + dim] for ref in kv_refs])
        s = following
        if h < heads - 1:
            following = scores(h + 1)
        top = jnp.max(s, axis=1, keepdims=True)
        p = jnp.exp2((s - top) * factor).astype(bf16)
        o = mm(p, jnp.concatenate([v, ones], axis=1))
        total = o[:, dim : dim + 1]
        outs.append(o[:, :dim] * (1.0 / total))
        totals.append(top * factor + jnp.log2(total))
    o_ref[...] = jnp.concatenate(outs, axis=1).astype(bf16)
    total_ref[...] = jnp.concatenate(totals + totals, axis=1)

    def own_work():
        own_ref[...] = mm(o_ref[...], wo_ref[...])

    def rec_work():
        rec_ref[...] = mm(o_ref[...], wo_ref[...]).astype(bf16)

    either(own_work, rec_work)


def attend(qkv, kvs, offset, query_ids, key_ids, out_full, heads, dim):
    rows, width, wide = qkv.shape[0], heads * dim, out_full.shape[1]
    keys = sum(kv.shape[0] for kv in kvs)
    n, own_spec, rec_spec, _ = split(rows // 2, min(rows // 2, 512 * 1024 // keys), wide)
    block = rows // (2 * n)
    return pl.pallas_call(
        functools.partial(attend_kernel, heads, dim, offset, len(kvs)),
        grid=(2 * n,),
        in_specs=[
            pl.BlockSpec((block, 1), lambda i: (i, 0)),
            const((1, keys)),
            pl.BlockSpec((block, qkv.shape[1]), lambda i: (i, 0)),
            const(out_full.shape),
        ]
        + [const(kv.shape) for kv in kvs],
        out_specs=[
            pl.BlockSpec((block, width), lambda i: (i, 0)),
            pl.BlockSpec((block, 2 * heads), lambda i: (i, 0)),
            own_spec,
            rec_spec,
        ],
        out_shape=[
            shape((rows, width), bf16),
            shape((rows, 2 * heads), f32),
            shape((rows // 2, wide), f32),
            shape((rows // 2, wide), bf16),
        ],
        compiler_params=params(44),
        cost_estimate=cost(10 * rows * keys * width, 16 * rows * width, heads * rows * keys),
    )(query_ids[:, None], key_ids[None, :], qkv, out_full, *kvs)


def attend_back_kernel(heads, dim, offset, count, first, last, *refs):
    qid_ref, kid_ref, q_ref, total_ref, wo_ref, own_ref, rec_ref = refs[:7]
    kv_refs = refs[7 : 7 + count]
    rest = refs[7 + count :]
    if not first:
        before_ref, rest = rest[0], rest[1:]
    dq_ref, dkv_ref, do_ref, acc_ref = rest
    step = pl.program_id(0)
    scale = dim**-0.5
    factor = scale * math.log2(math.e)
    width = heads * dim

    @pl.when(step == 0)
    def _():
        acc_ref[...] = jnp.zeros_like(acc_ref) if first else before_ref[...]

    def own_work():
        do_ref[...] = mm_last(own_ref[...], wo_ref[...]).astype(bf16)

    def rec_work():
        do_ref[...] = mm_last(rec_ref[...], wo_ref[...]).astype(bf16)

    either(own_work, rec_work)
    same = kid_ref[...] == qid_ref[...]
    dqs = []
    for h in range(heads):
        lo = h * dim
        at = offset + width + lo
        q = q_ref[:, lo : lo + dim]
        do = do_ref[:, lo : lo + dim]
        k = jnp.concatenate([ref[:, offset + lo : offset + lo + dim] for ref in kv_refs])
        v = jnp.concatenate([ref[:, at : at + dim] for ref in kv_refs])
        s = jnp.where(same, mm_last(k, q), NEGATIVE)
        p = jnp.exp2(s * factor - total_ref[h : h + 1, :])
        dp = mm_last(v, do)
        delta = jnp.sum(p * dp, axis=0, keepdims=True)
        ds = (p * (dp - delta)).astype(bf16)
        acc_ref[heads + h] += mm(p.astype(bf16), do)
        acc_ref[h] += mm(ds, q)
        dqs.append(mm_first(ds, k) * scale)
    dq_ref[...] = jnp.concatenate(dqs, axis=1).astype(bf16)

    @pl.when(step == pl.num_programs(0) - 1)
    def _():
        if last:
            parts = [acc_ref[h] * scale for h in range(heads)]
            parts += [acc_ref[heads + h] for h in range(heads)]
            dkv_ref[...] = jnp.concatenate(parts, axis=1).astype(bf16)
        else:
            dkv_ref[...] = acc_ref[...]


def attend_back(
    qkv, kvs, offset, query_ids, key_ids, totals, out_full, own, rec, before, last, heads, dim
):
    rows, width, wide = qkv.shape[0], heads * dim, out_full.shape[1]
    keys = sum(kv.shape[0] for kv in kvs)
    sums = (2 * heads, keys, dim)
    extra = [] if before is None else [before]
    n, own_spec, rec_spec, _ = split(rows // 2, min(rows // 2, 512 * 1024 // keys), wide)
    block = rows // (2 * n)
    done = shape((keys, 2 * width), bf16) if last else shape(sums, f32)
    return pl.pallas_call(
        functools.partial(attend_back_kernel, heads, dim, offset, len(kvs), before is None, last),
        grid=(2 * n,),
        in_specs=[
            pl.BlockSpec((1, block), lambda i: (0, i)),
            const((keys, 1)),
            pl.BlockSpec((block, qkv.shape[1]), lambda i: (i, 0)),
            pl.BlockSpec((2 * heads, block), lambda i: (0, i)),
            const(out_full.shape),
            own_spec,
            rec_spec,
        ]
        + [const(v.shape) for v in list(kvs) + extra],
        out_specs=[pl.BlockSpec((block, width), lambda i: (i, 0)), const(done.shape)],
        out_shape=[shape((rows, width), bf16), done],
        scratch_shapes=[pltpu.VMEM((block, width), bf16), pltpu.VMEM(sums, f32)],
        compiler_params=params(52),
        cost_estimate=cost(24 * rows * keys * width, 30 * rows * width, heads * rows * keys),
    )(query_ids[None, :], key_ids[:, None], qkv, totals.T, out_full, own, rec, *kvs, *extra)


def join_kernel(dq_ref, dkv_ref, w_ref, dqkv_ref, own_ref, rec_ref, sum_ref):
    @pl.when(pl.program_id(0) == 0)
    def _():
        sum_ref[...] = jnp.zeros_like(sum_ref)

    dqkv = jnp.concatenate([dq_ref[...], dkv_ref[...]], axis=1)
    dqkv_ref[...] = dqkv
    sum_ref[...] += jnp.sum(dqkv.astype(f32), axis=0, keepdims=True)
    width = dqkv.shape[1]

    def own_work():
        own_ref[...] = mm_last(dqkv_ref[...], w_ref[:, :width])

    def rec_work():
        rec_ref[...] = mm_last(dqkv_ref[...], w_ref[:, :width]).astype(bf16)

    either(own_work, rec_work)


def join(dq, dkv, chunk, weight):
    rows, width, wide = dq.shape[0], dq.shape[1] + dkv.shape[1], weight[0].shape[0]
    n, own_spec, rec_spec, _ = split(rows // 2, min(rows // 2, 256), wide)
    block, at = rows // (2 * n), 2 * n * chunk
    return pl.pallas_call(
        join_kernel,
        grid=(2 * n,),
        in_specs=[
            pl.BlockSpec((block, dq.shape[1]), lambda i: (i, 0)),
            pl.BlockSpec((block, dkv.shape[1]), lambda i: (at + i, 0)),
            columns(weight),
        ],
        out_specs=[pl.BlockSpec((block, width), lambda i: (i, 0)), own_spec, rec_spec, const((1, width))],
        out_shape=[
            shape((rows, width), bf16),
            shape((rows // 2, wide), f32),
            shape((rows // 2, wide), bf16),
            shape((1, width), f32),
        ],
        compiler_params=params(24),
        cost_estimate=cost(2 * rows * width * wide, 4 * wide * (rows + width)),
    )(dq, dkv, weight[0])


def hidden_kernel(own_ref, rec_ref, up_ref, down_ref, shift_ref, slope_ref, act_ref, po_ref, pr_ref):
    def work(ref, out_ref):
        e = mm(ref[...], up_ref[...]) + shift_ref[...]
        square = e * e
        h = 0.5 * jnp.tanh(e * (square * (ROOT * 0.044715) + ROOT)) + 0.5
        g = e * h
        slope = h + g * (1.0 - h) * (square * (6 * ROOT * 0.044715) + 2 * ROOT)
        g = g.astype(bf16)
        act_ref[...] = g
        slope_ref[...] = slope.astype(bf16)
        out_ref[...] = mm_last(g, down_ref[...]).astype(out_ref.dtype)

    either(lambda: work(own_ref, po_ref), lambda: work(rec_ref, pr_ref))


def tile_of(size):
    return 384 if size % 384 == 0 else 128


def hidden(own, rec, up, down, shift):
    half, wide = own.shape
    ff = up[1]
    n, own_spec, rec_spec, _ = split(half, min(half, 256), wide)
    strip = pl.BlockSpec((half // n, ff), lambda i: (i, 0))
    return pl.pallas_call(
        hidden_kernel,
        grid=(2 * n,),
        in_specs=[own_spec, rec_spec, columns(up), columns(down), const((1, ff))],
        out_specs=[strip, strip, own_spec, rec_spec],
        out_shape=[
            shape((2 * half, ff), bf16),
            shape((2 * half, ff), bf16),
            shape((half, wide), f32),
            shape((half, wide), bf16),
        ],
        compiler_params=params(30),
        cost_estimate=cost(8 * half * wide * ff, 4 * wide * ff + 20 * half * wide, 2 * half * ff),
    )(own, rec, up[0], down[0], shift[None])


def hidden_back_kernel(own_ref, rec_ref, slope_ref, up_ref, down_ref, de_ref, sum_ref, po_ref, pr_ref):
    @pl.when(pl.program_id(0) == 0)
    def _():
        sum_ref[...] = jnp.zeros_like(sum_ref)

    def work(ref, out_ref):
        de = (mm(ref[...], down_ref[...]) * slope_ref[...].astype(f32)).astype(bf16)
        de_ref[...] = de
        sum_ref[...] += jnp.sum(de.astype(f32), axis=0, keepdims=True)
        out_ref[...] = mm_last(de, up_ref[...]).astype(out_ref.dtype)

    either(lambda: work(own_ref, po_ref), lambda: work(rec_ref, pr_ref))


def hidden_back(own, rec, slope, up, down):
    half, wide = own.shape
    ff = up[1]
    n, own_spec, rec_spec, _ = split(half, min(half, 256), wide)
    strip = pl.BlockSpec((half // n, ff), lambda i: (i, 0))
    return pl.pallas_call(
        hidden_back_kernel,
        grid=(2 * n,),
        in_specs=[own_spec, rec_spec, strip, columns(up), columns(down)],
        out_specs=[strip, const((1, ff)), own_spec, rec_spec],
        out_shape=[
            shape((2 * half, ff), bf16),
            shape((1, ff), f32),
            shape((half, wide), f32),
            shape((half, wide), bf16),
        ],
        compiler_params=params(30),
        cost_estimate=cost(8 * half * wide * ff, 4 * wide * ff + 16 * half * wide),
    )(own, rec, slope, up[0], down[0])


def outer_kernel(lefts, rights, beside, bit_ref, *refs):
    left_refs, right_refs = refs[:lefts], refs[lefts : lefts + rights]
    rest = refs[lefts + rights :]
    if beside:
        beside_ref, rest = rest[0], rest[1:]
    mine_ref, theirs_ref = rest
    turned = right_refs[0].shape[0]
    cuts = [ref.shape[0] for ref in left_refs]
    total, at = None, 0
    for ref, size in zip(left_refs, cuts):
        low = at % turned
        right = right_refs[at // turned]
        part = mm_first(ref[...], right[low : low + size, :])
        total = part if total is None else total + part
        at += size
    out = total.astype(bf16)
    if beside:
        out = jnp.concatenate([out, beside_ref[...]], axis=1)
    half = out.shape[0] // 2

    @pl.when(bit_ref[0] == 0)
    def _():
        mine_ref[...], theirs_ref[...] = out[:half], out[half:]

    @pl.when(bit_ref[0] == 1)
    def _():
        mine_ref[...], theirs_ref[...] = out[half:], out[:half]


def outer(lefts, rights, bit, beside=None):
    depth, width = lefts[0].shape[1], rights[0].shape[1]
    rows = sum(v.shape[0] for v in lefts)
    extra = [] if beside is None else [beside]
    out = shape((depth // 2, width + sum(v.shape[1] for v in extra)), bf16)
    return pl.pallas_call(
        functools.partial(outer_kernel, len(lefts), len(rights), len(extra)),
        in_specs=[pl.BlockSpec(memory_space=pltpu.SMEM)]
        + [VMEM] * (len(lefts) + len(rights) + len(extra)),
        out_specs=[VMEM] * 2,
        out_shape=[out] * 2,
        compiler_params=params(30),
        cost_estimate=cost(2 * rows * depth * width, 2 * rows * (depth + width) + 2 * depth * width),
    )(bit, *lefts, *rights, *extra)


def outer_out_kernel(count, o_ref, *refs):
    out_ref = refs[count]
    total, at = None, 0
    for ref in refs[:count]:
        part = mm_first(o_ref[at : at + ref.shape[0], :], ref[...])
        total = part if total is None else total + part
        at += ref.shape[0]
    out_ref[...] = total.astype(bf16)


def outer_out(attended, rights):
    depth, width, rows = attended.shape[1], rights[0].shape[1], attended.shape[0]
    return pl.pallas_call(
        functools.partial(outer_out_kernel, len(rights)),
        in_specs=[VMEM] * (1 + len(rights)),
        out_specs=VMEM,
        out_shape=shape((depth, width), bf16),
        compiler_params=params(24),
        cost_estimate=cost(2 * rows * depth * width, 2 * rows * (depth + width) + 2 * depth * width),
    )(attended, *rights)


def spread(v):
    centred = v - jnp.mean(v, axis=-1, keepdims=True)
    scale = lax.rsqrt(jnp.mean(centred * centred, axis=-1, keepdims=True) + EPSILON)
    return centred * scale, scale


def norm_kernel(rows_of, v_ref, q_ref, come_ref, small_ref, next_ref, u_ref, m_ref):
    shift, gain, offset = rows_of
    u = v_ref[...] + (q_ref[...].astype(f32) + come_ref[...].astype(f32) + small_ref[shift : shift + 1, :])
    u_ref[...] = u
    n = spread(u)[0] * next_ref[gain : gain + 1, :] + next_ref[offset : offset + 1, :]
    m_ref[...] = n.astype(bf16)


def add_norm(v, q, come, small, following, rows_of):
    rows, width = v.shape
    block = pl.BlockSpec((min(rows, 256), width), lambda i: (i, 0))
    return pl.pallas_call(
        functools.partial(norm_kernel, rows_of),
        grid=(rows // min(rows, 256),),
        in_specs=[block] * 3 + [const(small.shape)] * 2,
        out_specs=[block] * 2,
        out_shape=[shape(v.shape, f32), shape(v.shape, bf16)],
        compiler_params=params(16),
        cost_estimate=cost(12 * v.size, 14 * v.size),
    )(v, q, come, small, following)


def norm_back_kernel(gain, v_ref, q_ref, come_ref, grad_ref, small_ref, out_ref, round_ref, sum_ref):
    @pl.when(pl.program_id(0) == 0)
    def _():
        sum_ref[...] = jnp.zeros_like(sum_ref)

    t = q_ref[...].astype(f32) + come_ref[...].astype(f32)
    n, scale = spread(v_ref[...])
    w = t * small_ref[gain : gain + 1, :]
    mean_w = jnp.mean(w, axis=-1, keepdims=True)
    mean_wn = jnp.mean(w * n, axis=-1, keepdims=True)
    out = grad_ref[...] + scale * (w - mean_w - n * mean_wn)
    out_ref[...] = out
    rounded = out.astype(bf16)
    round_ref[...] = rounded
    sum_ref[0:1, :] += jnp.sum(t * n, axis=0, keepdims=True)
    sum_ref[1:2, :] += jnp.sum(t, axis=0, keepdims=True)
    sum_ref[2:3, :] += jnp.sum(rounded.astype(f32), axis=0, keepdims=True)


def norm_back(v, q, come, grad, small, gain):
    rows, width = v.shape
    block = pl.BlockSpec((min(rows, 256), width), lambda i: (i, 0))
    return pl.pallas_call(
        functools.partial(norm_back_kernel, gain),
        grid=(rows // min(rows, 256),),
        in_specs=[block] * 4 + [const(small.shape)],
        out_specs=[block] * 2 + [const((8, width))],
        out_shape=[shape(v.shape, f32), shape(v.shape, bf16), shape((8, width), f32)],
        compiler_params=params(20),
        cost_estimate=cost(24 * v.size, 18 * v.size),
    )(v, q, come, grad, small)


def tie(values):
    return lax.optimization_barrier(values)


def pick(array, index, axis=0):
    return lax.dynamic_index_in_dim(array, index, axis, keepdims=False)


def swap_x(v):
    return lax.ppermute(v, "x", SWAP)


def swap_c(v):
    return lax.ppermute(v, "c", SWAP)


def in_order(axis, own, other):
    first = lax.axis_index(axis) == 0
    return jnp.where(first, own, other), jnp.where(first, other, own)


def exchange(blocks):
    xi, ci = lax.axis_index("x"), lax.axis_index("c")
    blocks = blocks.reshape((2, 2) + blocks.shape[1:])
    both = jnp.stack(in_order("x", pick(blocks, xi), swap_x(pick(blocks, 1 - xi))))
    out = in_order("c", pick(both, ci, 1), swap_c(pick(both, 1 - ci, 1)))
    return jnp.stack(out, axis=1).reshape((RANKS,) + blocks.shape[2:])


def flip(v, axis, step):
    size = lax.axis_size(axis)
    return lax.ppermute(v, axis, [(i, i ^ step) for i in range(size)])


def gather_rows(payload):
    return lax.all_gather(payload, ("hi", "seq"), axis=0, tiled=True)


def halve_rows(mine, theirs):
    step = lax.axis_size("hi") // 2
    place = lax.axis_index("hi")
    terms = (mine.astype(f32) + flip(theirs, "hi", step).astype(f32)).astype(bf16)
    step //= 2
    while step:
        halves = terms.reshape((2, -1) + terms.shape[1:])
        bit = (place // step) % 2
        come = flip(pick(halves, 1 - bit), "hi", step)
        terms = (pick(halves, bit).astype(f32) + come.astype(f32)).astype(bf16)
        step //= 2
    return terms


def scatter_rows(terms):
    return lax.psum_scatter(terms, "seq", scatter_dimension=0, tiled=True)


def body(
    tokens,
    cotangent,
    image_lengths,
    qkv_weight,
    out_weight,
    up_weight,
    down_weight,
    up_bias,
    norm_scale,
    shifts,
):
    rows, width = tokens.shape
    layers, held = qkv_weight.shape[0], qkv_weight.shape[1]
    blocks, seqs = lax.axis_size("hi"), lax.axis_size("seq")
    ways = seqs // RANKS
    shards = blocks * seqs
    chunk = seqs * held
    heads = HEADS // RANKS
    dim = width // HEADS
    part = width // RANKS
    ff = up_weight.shape[2]
    ff_part = ff // RANKS
    ff_pad = -(-ff_part // 128) * 128
    xi, ci = lax.axis_index("x"), lax.axis_index("c")
    rank = 2 * xi + ci

    spot = jnp.arange(width, dtype=jnp.int32)
    natural = ((spot // (RANKS * held * seqs) * RANKS + spot // held % RANKS) * seqs) * held
    natural = natural + spot // (RANKS * held) % seqs * held + spot % held
    turn_matrix = (spot[:, None] == natural[None, :]).astype(bf16)

    def mixed_order(v):
        return mm(v, turn_matrix).astype(bf16)

    def plain_order(v):
        return mm_last(v, turn_matrix)

    def mine(v):
        return pick(v.reshape(blocks, seqs, RANKS, held), rank, 2).reshape(part)

    def placed(v):
        v = v.reshape(blocks, seqs, 1, held)
        spots = (jnp.arange(RANKS) == rank)[None, None, :, None]
        return jnp.where(spots, v, 0.0).reshape(width)

    there, spots = [], (0, 3, 1, 2)
    for b in range(blocks):
        for r in range(RANKS):
            for s in range(seqs):
                target = (b * RANKS + s % RANKS) * seqs + spots[r] * ways + s // RANKS
                there.append(((b * RANKS + r) * seqs + s, target))
    back = [(target, source) for source, target in there]

    def rank_columns(piece):
        piece = piece.reshape(held, 3, blocks, RANKS, chunk)
        return piece.transpose(3, 0, 1, 2, 4).reshape(RANKS, held, 3 * part)

    def ff_columns(piece):
        piece = piece.reshape(held, RANKS, ff_part).transpose(1, 0, 2)
        return jnp.pad(piece, ((0, 0), (0, 0), (0, ff_pad - ff_part)))

    def out_rows(l):
        return mixed_order(out_weight[l]).reshape(held * RANKS, part)

    kinds = norm_scale.shape[2] + shifts.shape[2]
    smalls = jnp.concatenate([norm_scale, shifts], axis=2)
    smalls = smalls.transpose(1, 0, 2).reshape(1, held, layers * kinds)
    smalls = jnp.broadcast_to(smalls, (RANKS, held, layers * kinds))

    qkv_fulls, out_fulls, up_fulls, down_fulls = [], [], [], []
    came = exchange(jnp.concatenate([rank_columns(qkv_weight[0]), smalls], axis=2))
    came = came.reshape(RANKS * held, -1)
    payload = jnp.concatenate([came[:, : 3 * part], out_rows(0), came[:, 3 * part :]], axis=1)
    first = gather_rows(payload)
    later = [
        ff_columns(piece) for l in range(layers) for piece in (up_weight[l], down_weight[l])
    ] + [rank_columns(qkv_weight[l]) for l in range(1, layers)]
    arrived = lax.ppermute(tokens, AXES, there)
    later, arrived, _ = tie((jnp.concatenate(later, axis=2), arrived, payload))
    own = mixed_order(arrived)
    later = exchange(later).reshape(RANKS * held, -1)
    payloads = []
    for l in range(layers):
        if l > 0:
            at = 2 * layers * ff_pad + (l - 1) * 3 * part
            piece = jnp.concatenate([later[:, at : at + 3 * part], out_rows(l)], axis=1)
            payloads.append(piece)
        payloads.append(later[:, 2 * l * ff_pad : 2 * (l + 1) * ff_pad])
    payloads, first, starts = tie((payloads, first, in_order("x", own, swap_x(own))))
    gathered = iter([gather_rows(v) for v in payloads])
    unit = jnp.eye(layers * kinds, dtype=bf16)
    small_full = mm_last(unit, first[:, width:]).reshape(layers, kinds, width)
    qkv_fulls.append((first, first.shape[1], 0))
    out_fulls.append(first[:, 3 * part : width].reshape(part, width))
    for l in range(layers):
        if l > 0:
            full = next(gathered)
            qkv_fulls.append((full, width, 0))
            out_fulls.append(full[:, 3 * part :].reshape(part, width))
        full = next(gathered)
        up_fulls.append((full, ff_pad, 0))
        down_fulls.append((full, ff_pad, 1))
    up_shift = pick(up_bias.reshape(layers, RANKS, ff_part), rank, 1).astype(f32)
    up_shift = jnp.pad(up_shift, ((0, 0), (0, ff_pad - ff_part)))

    xs = [(0, 1)] if CHUNKS == 1 else [(0,), (1,)]
    span = 4 * rows // CHUNKS
    lengths = lax.ppermute(image_lengths, AXES, there)
    finish = jnp.cumsum(lengths[0])
    base = jnp.arange(rows, dtype=jnp.int32)
    local = [
        jnp.concatenate([base + (2 * x + c) * rows for c in (ci, 1 - ci) for x in chunk_xs])
        for chunk_xs in xs
    ]
    group = RANKS * rows
    turn = lax.axis_index("seq") % ways

    def ids_of(pos):
        return jnp.sum((pos[:, None] >= finish[None, :]).astype(jnp.int32), axis=1)

    query_ids = [ids_of(v + turn * group) for v in local]
    key_ids = ids_of(jnp.concatenate([v + w * group for v in local for w in range(ways)]))
    seq_groups = [[j * ways + w for w in range(ways)] for j in range(seqs // ways)]

    def keys_of(qkv):
        if ways == 1:
            return qkv, part
        kv = lax.all_gather(
            qkv[:, part:], "seq", axis=0, tiled=True, axis_index_groups=seq_groups
        )
        return kv, 0

    def chunks_of(v):
        own = mixed_order(v)
        pair = in_order("x", own, swap_x(own))
        return list(pair) if CHUNKS == 2 else [jnp.concatenate(pair)]

    def at_x(chunks, index):
        if CHUNKS == 2:
            return jnp.where(index == 0, chunks[0], chunks[1])
        return pick(chunks[0].reshape((2, rows) + chunks[0].shape[1:]), index)

    def core_sum(own, other):
        return (own + swap_c(other).astype(f32)).astype(bf16)

    def last_sum(qs):
        return at_x(qs, xi), swap_x(at_x(qs, 1 - xi))

    GAIN1, GAIN2, OFF1, QB, VB, OB, OFF2, DB = range(8)
    starts = list(starts) if CHUNKS == 2 else [jnp.concatenate(starts)]
    current = [v.astype(f32) for v in starts]
    normed = [
        (spread(v)[0] * small_full[0, GAIN1] + small_full[0, OFF1]).astype(bf16) for v in current
    ]
    saved = []
    output = None
    for l in range(layers):
        small = small_full[l]
        attn_in = [(v, swap_c(v)) for v in normed]
        shift = jnp.concatenate([mine(small[QB]), jnp.zeros((part,), f32), mine(small[VB])])
        qkv = [project(own, rec, qkv_fulls[l], shift) for own, rec in attn_in]
        kvs = [keys_of(v) for v in qkv]
        offset, kvs = kvs[0][1], [v[0] for v in kvs]
        attended, totals, after, normed = [], [], [], []
        for j in range(CHUNKS):
            o, total, own, other = attend(
                qkv[j], kvs, offset, query_ids[j], key_ids, out_fulls[l], heads, dim
            )
            attended.append(o)
            totals.append(total)
            q = core_sum(own, other)
            if l == layers - 1 and j == 0:
                q, cotangent = tie((q, cotangent))
                arrived = lax.ppermute(cotangent, AXES, there)
            come = swap_x(q)
            if l == layers - 1 and j == 0:
                come, arrived = tie((come, arrived))
            u, m = add_norm(current[j], q, come, small, small, (OB, GAIN2, OFF2))
            after.append(u)
            normed.append(m)
        mlp_in = [(v, swap_c(v)) for v in normed]
        if l == layers - 1:
            rounded = chunks_of(arrived)
        slopes, acts, qs, following, normed = [], [], [], [], []
        for j in range(CHUNKS):
            slope, act, own, other = hidden(*mlp_in[j], up_fulls[l], down_fulls[l], up_shift[l])
            slopes.append(slope)
            acts.append(act)
            q = core_sum(own, other)
            qs.append(q)
            if l < layers - 1:
                u, m = add_norm(
                    after[j], q, swap_x(q), small, small_full[l + 1], (DB, GAIN1, OFF1)
                )
                following.append(u)
                normed.append(m)
        saved.append((current, attn_in, qkv, kvs, attended, totals, after, mlp_in, slopes, acts))
        current = following
        if l == layers - 1:
            output = (qs, after, small[DB])

    grads = [None] * layers
    vectors = [None] * layers
    biases = [None] * layers
    grad = [v.astype(f32) for v in rounded]
    d_sum = 0.5 * sum(jnp.sum(v, axis=0) for v in grad)
    tokens_grad = None
    top_bit = (lax.axis_index("hi") // (blocks // 2)).astype(jnp.int32)[None]

    def home_of(pieces):
        return exchange(jnp.concatenate(pieces, axis=1).reshape(RANKS, held, -1))


    waiting, homes = None, {}
    for l in reversed(range(layers)):
        (current, attn_in, qkv, kvs, attended, totals, after, mlp_in, slopes, acts) = saved[l]
        small = small_full[l]
        last_layer = waiting is None
        down_in = [(v, swap_c(v)) for v in rounded]
        down_terms = outer([v for pair in down_in for v in pair], acts, top_bit)
        down_in, down_terms = tie((down_in, down_terms))
        des, qs, bias = [], [], 0.0
        for j in range(CHUNKS):
            de, sums, own, other = hidden_back(*down_in[j], slopes[j], up_fulls[l], down_fulls[l])
            des.append(de)
            bias = bias + sums[0]
            qs.append(core_sum(own, other))
        biases[l] = bias
        if last_layer:
            qs, des = tie((qs, des))
        else:
            waiting = halve_rows(*waiting)
            qs, des, waiting = tie((qs, des, waiting))
            waiting = scatter_rows(waiting)
        comes = [swap_x(q) for q in qs]
        up_terms = outer([v for pair in mlp_in for v in pair], des, top_bit)
        down_terms = halve_rows(*down_terms)
        if last_layer:
            comes, down_terms, up_terms, output = tie((comes, down_terms, up_terms, output))
            q, come = last_sum(output[0])
            output = at_x(output[1], xi) + (q.astype(f32) + come.astype(f32) + output[2])
            output = output.astype(bf16)
        else:
            comes, down_terms, up_terms, grads[l + 1][2], output = tie(
                (comes, down_terms, up_terms, waiting, output)
            )
            output = lax.ppermute(output, AXES, back)
        if l > 0:
            down_owned = scatter_rows(down_terms)
        rounded, mid, sums = [], [], 0.0
        for j in range(CHUNKS):
            g, r, s = norm_back(after[j], qs[j], comes[j], grad[j], small, GAIN2)
            mid.append(g)
            rounded.append(r)
            sums = sums + 0.5 * s
        gain_two_sum, off_two_sum, o_sum = sums[0], sums[1], sums[2]
        out_in = [(v, swap_c(v)) for v in rounded]
        acc, dqs = None, []
        for j in range(CHUNKS):
            dq, acc = attend_back(
                qkv[j], kvs, 0 if ways > 1 else part, query_ids[j], key_ids, totals[j],
                out_fulls[l], *out_in[j], acc, j == CHUNKS - 1, heads, dim,
            )
            dqs.append(dq)
        if ways > 1:
            acc = acc.reshape(CHUNKS, ways, span, 2 * part).swapaxes(0, 1)
            acc = lax.psum_scatter(
                acc.reshape(ways * CHUNKS * span, 2 * part),
                "seq",
                scatter_dimension=0,
                tiled=True,
                axis_index_groups=seq_groups,
            )
        if not last_layer:
            dqs, acc, output, down_terms = tie((dqs, acc, output, down_terms))
        dqkvs, qs, sums_qkv = [], [], 0.0
        for j in range(CHUNKS):
            dqkv, own, other, s = join(dqs[j], acc, j, qkv_fulls[l])
            dqkvs.append(dqkv)
            sums_qkv = sums_qkv + s[0]
            qs.append(core_sum(own, other))
        up_terms = halve_rows(*up_terms)
        if last_layer:
            qs, dqkvs, out_in, up_terms, down_owned, output = tie(
                (qs, dqkvs, out_in, up_terms, down_owned, output)
            )
        else:
            down_owned = scatter_rows(down_terms)
            qs, dqkvs, out_in, up_terms = tie((qs, dqkvs, out_in, up_terms))
        up_owned = scatter_rows(up_terms)
        if l > 0:
            comes = [swap_x(q) for q in qs]
        else:
            q, comes = last_sum(qs)
        out_terms = outer_out(
            jnp.concatenate(attended) if CHUNKS > 1 else attended[0],
            [v for pair in out_in for v in pair],
        ).reshape(width, part)
        waiting = outer([v for pair in attn_in for v in pair], dqkvs, top_bit, out_terms)
        if not last_layer:
            grads[l + 1], waiting = tie((grads[l + 1], waiting))
            homes[l + 1] = home_of([grads[l + 1][0], grads[l + 1][1], grads[l + 1][2][:, : 3 * part]])
        if l > 0:
            comes, waiting, up_owned = tie((comes, waiting, up_owned))
        else:
            comes, waiting, down_owned = tie((comes, waiting, down_owned))
        d_next = None
        if l > 0:
            grad, rounded, sums = [], [], 0.0
            for j in range(CHUNKS):
                g, r, s = norm_back(current[j], qs[j], comes[j], mid[j], small, GAIN1)
                grad.append(g)
                rounded.append(r)
                sums = sums + 0.5 * s
            d_next = sums[2]
        else:
            g, r, sums = norm_back(at_x(current, xi), q, comes, at_x(mid, xi), small, GAIN1)
            tokens_grad = r
        vectors[l] = jnp.stack(
            [
                sums[0],
                gain_two_sum,
                sums[1],
                placed(sums_qkv[:part]),
                placed(sums_qkv[2 * part :]),
                o_sum,
                off_two_sum,
                d_sum,
            ]
        )
        d_sum = d_next
        grads[l] = [up_owned, down_owned, None]

    spots = (jnp.arange(RANKS) == rank)[None, :, None]
    bias = jnp.where(spots, jnp.stack(biases)[:, None, :], 0.0).reshape(layers * RANKS, ff_pad)
    wide = max(ff_pad, width)
    both = jnp.concatenate(
        [
            jnp.pad(jnp.concatenate(vectors), ((0, 0), (0, wide - width))),
            jnp.pad(bias, ((0, 0), (0, wide - ff_pad))),
        ]
    )
    tokens_grad = lax.ppermute(tokens_grad, AXES, back)

    def sum_along(v, axis):
        step = 1
        while step < lax.axis_size(axis):
            v = v + flip(v, axis, step)
            step *= 2
        return v

    both = sum_along(sum_along(both, "c"), "x")
    both, grads[0][0] = tie((both, grads[0][0]))
    both = sum_along(both, "hi")
    mine_last, theirs_last = waiting
    mine_last, both, tokens_grad, homes = tie((mine_last, both, tokens_grad, homes))
    last = scatter_rows(halve_rows(mine_last, theirs_last))
    both = sum_along(both, "seq")
    grads[0][2] = last
    homes[0] = home_of([grads[0][0], grads[0][1], last[:, : 3 * part]])
    results = [[None] * layers for _ in range(4)]
    for l in range(layers):
        owned = grads[l][2]
        results[1][l] = plain_order(owned[:, 3 * part :].reshape(held, width))
        for i in (2, 3):
            home = homes[l][:, :, (i - 2) * ff_pad : (i - 2) * ff_pad + ff_part]
            results[i][l] = home.transpose(1, 0, 2).reshape(held, ff)
        qkv_grad = homes[l][:, :, 2 * ff_pad :]
        qkv_grad = qkv_grad.reshape(RANKS, held, 3, blocks, chunk).transpose(1, 2, 3, 0, 4)
        results[0][l] = qkv_grad.reshape(held, 3 * width)
    results = [jnp.stack(v).astype(f32) for v in results]

    vector = both[: layers * kinds, :width].reshape(layers, kinds, blocks, seqs, RANKS, held)
    for axis, index in ((2, "hi"), (2, "seq")):
        vector = pick(vector, lax.axis_index(index), axis)
    vector = pick(vector, rank, 2).swapaxes(1, 2)
    bias = both[layers * kinds :, :ff_part].reshape(layers, ff)
    return (
        plain_order(output),
        plain_order(tokens_grad),
        *results,
        bias,
        vector[:, :, :2],
        vector[:, :, 2:],
    )


def solution(mesh):
    sizes = mesh.shape
    devices = mesh.devices.reshape(sizes["img"] // RANKS, 2, 2, sizes["seq"])
    fine = Mesh(devices, AXES)
    row = P(AXES, None)
    param = P(None, AXES, None)
    in_specs = (row, row, P(AXES[:3], None), param, param, param, param, P(), param, param)
    out_specs = (row, row, param, param, param, param, P(), param, param)
    return jax.shard_map(
        body, mesh=fine, in_specs=in_specs, out_specs=out_specs, check_vma=False
    )
```

```python
import functools
import math

import jax
import jax.numpy as jnp
from jax import lax
from jax.experimental import pallas as pl
from jax.experimental.pallas import tpu as pltpu
from jax.sharding import Mesh
from jax.sharding import PartitionSpec as P

HEADS = 16
RANKS = 4
CHUNKS = 1
EPSILON = 1e-06
NEGATIVE = -1e30
ROOT = math.sqrt(2.0 / math.pi)
AXES = ("hi", "x", "c", "seq")
SWAP = ((0, 1), (1, 0))
bf16, f32 = jnp.bfloat16, jnp.float32
VMEM = pl.BlockSpec(memory_space=pltpu.VMEM)


def mm(left, right):
    return jnp.dot(left, right, preferred_element_type=f32)


def mm_last(left, right):
    dims = (((1,), (1,)), ((), ()))
    return lax.dot_general(left, right, dims, preferred_element_type=f32)


def mm_first(left, right):
    dims = (((0,), (0,)), ((), ()))
    return lax.dot_general(left, right, dims, preferred_element_type=f32)


def shape(dims, kind):
    return jax.ShapeDtypeStruct(tuple(dims), kind)


def params(mib):
    return pltpu.CompilerParams(vmem_limit_bytes=mib * 2**20)


def cost(flops, moved, exps=0):
    share = 0.1
    return pl.CostEstimate(
        flops=int(share * flops), bytes_accessed=int(share * moved), transcendentals=int(share * exps)
    )


def const(dims):
    return pl.BlockSpec(tuple(dims), lambda i: (0,) * len(dims))


def columns(weight):
    array, width, place = weight
    return pl.BlockSpec((array.shape[0], width), lambda i: (0, place))


def split(half, block, width):
    n = half // block
    own = pl.BlockSpec((block, width), lambda i: (jnp.minimum(i, n - 1), 0))
    rec = pl.BlockSpec((block, width), lambda i: (jnp.maximum(i - n, 0), 0))
    strip = pl.BlockSpec((block, width), lambda i: (i, 0))
    return n, own, rec, strip


def either(own_work, rec_work):
    step, half = pl.program_id(0), pl.num_programs(0) // 2
    pl.when(step < half)(own_work)
    pl.when(step >= half)(rec_work)


def project_kernel(own_ref, rec_ref, w_ref, shift_ref, out_ref):
    width = out_ref.shape[1]

    def work(ref):
        out_ref[...] = (mm(ref[...], w_ref[:, :width]) + shift_ref[...]).astype(bf16)

    either(lambda: work(own_ref), lambda: work(rec_ref))


def project(own, rec, weight, shift):
    half, depth = own.shape
    width = shift.shape[0]
    n, own_spec, rec_spec, _ = split(half, min(half, 256), depth)
    return pl.pallas_call(
        project_kernel,
        grid=(2 * n,),
        in_specs=[own_spec, rec_spec, columns(weight), const((1, width))],
        out_specs=pl.BlockSpec((half // n, width), lambda i: (i, 0)),
        out_shape=shape((2 * half, width), bf16),
        compiler_params=params(24),
        cost_estimate=cost(4 * half * depth * width, 2 * depth * (2 * half + width)),
    )(own, rec, weight[0], shift[None])


def attend_kernel(heads, dim, offset, count, *refs):
    qid_ref, kid_ref, q_ref, wo_ref = refs[:4]
    kv_refs = refs[4 : 4 + count]
    o_ref, total_ref, own_ref, rec_ref = refs[4 + count :]
    factor = dim**-0.5 * math.log2(math.e)
    width = heads * dim
    same = qid_ref[...] == kid_ref[...]

    def scores(h):
        lo = h * dim
        q = q_ref[:, lo : lo + dim]
        k = jnp.concatenate([ref[:, offset + lo : offset + lo + dim] for ref in kv_refs])
        return jnp.where(same, mm_last(q, k), NEGATIVE)

    keys = sum(ref.shape[0] for ref in kv_refs)
    ones = jnp.ones((keys, 8), bf16)
    outs, totals = [], []
    following = scores(0)
    for h in range(heads):
        at = offset + width + h * dim
        v = jnp.concatenate([ref[:, at : at + dim] for ref in kv_refs])
        s = following
        if h < heads - 1:
            following = scores(h + 1)
        top = jnp.max(s, axis=1, keepdims=True)
        p = jnp.exp2((s - top) * factor).astype(bf16)
        o = mm(p, jnp.concatenate([v, ones], axis=1))
        total = o[:, dim : dim + 1]
        outs.append(o[:, :dim] * (1.0 / total))
        totals.append(top * factor + jnp.log2(total))
    o_ref[...] = jnp.concatenate(outs, axis=1).astype(bf16)
    total_ref[...] = jnp.concatenate(totals + totals, axis=1)

    def own_work():
        own_ref[...] = mm(o_ref[...], wo_ref[...])

    def rec_work():
        rec_ref[...] = mm(o_ref[...], wo_ref[...]).astype(bf16)

    either(own_work, rec_work)


def attend(qkv, kvs, offset, query_ids, key_ids, out_full, heads, dim):
    rows, width, wide = qkv.shape[0], heads * dim, out_full.shape[1]
    keys = sum(kv.shape[0] for kv in kvs)
    n, own_spec, rec_spec, _ = split(rows // 2, min(rows // 2, 512 * 1024 // keys), wide)
    block = rows // (2 * n)
    return pl.pallas_call(
        functools.partial(attend_kernel, heads, dim, offset, len(kvs)),
        grid=(2 * n,),
        in_specs=[
            pl.BlockSpec((block, 1), lambda i: (i, 0)),
            const((1, keys)),
            pl.BlockSpec((block, qkv.shape[1]), lambda i: (i, 0)),
            const(out_full.shape),
        ]
        + [const(kv.shape) for kv in kvs],
        out_specs=[
            pl.BlockSpec((block, width), lambda i: (i, 0)),
            pl.BlockSpec((block, 2 * heads), lambda i: (i, 0)),
            own_spec,
            rec_spec,
        ],
        out_shape=[
            shape((rows, width), bf16),
            shape((rows, 2 * heads), f32),
            shape((rows // 2, wide), f32),
            shape((rows // 2, wide), bf16),
        ],
        compiler_params=params(44),
        cost_estimate=cost(10 * rows * keys * width, 16 * rows * width, heads * rows * keys),
    )(query_ids[:, None], key_ids[None, :], qkv, out_full, *kvs)


def attend_back_kernel(heads, dim, offset, count, first, last, *refs):
    qid_ref, kid_ref, q_ref, total_ref, wo_ref, own_ref, rec_ref = refs[:7]
    kv_refs = refs[7 : 7 + count]
    rest = refs[7 + count :]
    if not first:
        before_ref, rest = rest[0], rest[1:]
    dq_ref, dkv_ref, do_ref, acc_ref = rest
    step = pl.program_id(0)
    scale = dim**-0.5
    factor = scale * math.log2(math.e)
    width = heads * dim

    @pl.when(step == 0)
    def _():
        acc_ref[...] = jnp.zeros_like(acc_ref) if first else before_ref[...]

    def own_work():
        do_ref[...] = mm_last(own_ref[...], wo_ref[...]).astype(bf16)

    def rec_work():
        do_ref[...] = mm_last(rec_ref[...], wo_ref[...]).astype(bf16)

    either(own_work, rec_work)
    same = kid_ref[...] == qid_ref[...]
    dqs = []
    for h in range(heads):
        lo = h * dim
        at = offset + width + lo
        q = q_ref[:, lo : lo + dim]
        do = do_ref[:, lo : lo + dim]
        k = jnp.concatenate([ref[:, offset + lo : offset + lo + dim] for ref in kv_refs])
        v = jnp.concatenate([ref[:, at : at + dim] for ref in kv_refs])
        s = jnp.where(same, mm_last(k, q), NEGATIVE)
        p = jnp.exp2(s * factor - total_ref[h : h + 1, :])
        dp = mm_last(v, do)
        delta = jnp.sum(p * dp, axis=0, keepdims=True)
        ds = (p * (dp - delta)).astype(bf16)
        acc_ref[heads + h] += mm(p.astype(bf16), do)
        acc_ref[h] += mm(ds, q)
        dqs.append(mm_first(ds, k) * scale)
    dq_ref[...] = jnp.concatenate(dqs, axis=1).astype(bf16)

    @pl.when(step == pl.num_programs(0) - 1)
    def _():
        if last:
            parts = [acc_ref[h] * scale for h in range(heads)]
            parts += [acc_ref[heads + h] for h in range(heads)]
            dkv_ref[...] = jnp.concatenate(parts, axis=1).astype(bf16)
        else:
            dkv_ref[...] = acc_ref[...]


def attend_back(
    qkv, kvs, offset, query_ids, key_ids, totals, out_full, own, rec, before, last, heads, dim
):
    rows, width, wide = qkv.shape[0], heads * dim, out_full.shape[1]
    keys = sum(kv.shape[0] for kv in kvs)
    sums = (2 * heads, keys, dim)
    extra = [] if before is None else [before]
    n, own_spec, rec_spec, _ = split(rows // 2, min(rows // 2, 512 * 1024 // keys), wide)
    block = rows // (2 * n)
    done = shape((keys, 2 * width), bf16) if last else shape(sums, f32)
    return pl.pallas_call(
        functools.partial(attend_back_kernel, heads, dim, offset, len(kvs), before is None, last),
        grid=(2 * n,),
        in_specs=[
            pl.BlockSpec((1, block), lambda i: (0, i)),
            const((keys, 1)),
            pl.BlockSpec((block, qkv.shape[1]), lambda i: (i, 0)),
            pl.BlockSpec((2 * heads, block), lambda i: (0, i)),
            const(out_full.shape),
            own_spec,
            rec_spec,
        ]
        + [const(v.shape) for v in list(kvs) + extra],
        out_specs=[pl.BlockSpec((block, width), lambda i: (i, 0)), const(done.shape)],
        out_shape=[shape((rows, width), bf16), done],
        scratch_shapes=[pltpu.VMEM((block, width), bf16), pltpu.VMEM(sums, f32)],
        compiler_params=params(52),
        cost_estimate=cost(24 * rows * keys * width, 30 * rows * width, heads * rows * keys),
    )(query_ids[None, :], key_ids[:, None], qkv, totals.T, out_full, own, rec, *kvs, *extra)


def join_kernel(dq_ref, dkv_ref, w_ref, dqkv_ref, own_ref, rec_ref, sum_ref):
    @pl.when(pl.program_id(0) == 0)
    def _():
        sum_ref[...] = jnp.zeros_like(sum_ref)

    dqkv = jnp.concatenate([dq_ref[...], dkv_ref[...]], axis=1)
    dqkv_ref[...] = dqkv
    sum_ref[...] += jnp.sum(dqkv.astype(f32), axis=0, keepdims=True)
    width = dqkv.shape[1]

    def own_work():
        own_ref[...] = mm_last(dqkv_ref[...], w_ref[:, :width])

    def rec_work():
        rec_ref[...] = mm_last(dqkv_ref[...], w_ref[:, :width]).astype(bf16)

    either(own_work, rec_work)


def join(dq, dkv, chunk, weight):
    rows, width, wide = dq.shape[0], dq.shape[1] + dkv.shape[1], weight[0].shape[0]
    n, own_spec, rec_spec, _ = split(rows // 2, min(rows // 2, 256), wide)
    block, at = rows // (2 * n), 2 * n * chunk
    return pl.pallas_call(
        join_kernel,
        grid=(2 * n,),
        in_specs=[
            pl.BlockSpec((block, dq.shape[1]), lambda i: (i, 0)),
            pl.BlockSpec((block, dkv.shape[1]), lambda i: (at + i, 0)),
            columns(weight),
        ],
        out_specs=[pl.BlockSpec((block, width), lambda i: (i, 0)), own_spec, rec_spec, const((1, width))],
        out_shape=[
            shape((rows, width), bf16),
            shape((rows // 2, wide), f32),
            shape((rows // 2, wide), bf16),
            shape((1, width), f32),
        ],
        compiler_params=params(24),
        cost_estimate=cost(2 * rows * width * wide, 4 * wide * (rows + width)),
    )(dq, dkv, weight[0])


def hidden_kernel(own_ref, rec_ref, up_ref, down_ref, shift_ref, slope_ref, act_ref, po_ref, pr_ref):
    def work(ref, out_ref):
        e = mm(ref[...], up_ref[...]) + shift_ref[...]
        square = e * e
        h = 0.5 * jnp.tanh(e * (square * (ROOT * 0.044715) + ROOT)) + 0.5
        g = e * h
        slope = h + g * (1.0 - h) * (square * (6 * ROOT * 0.044715) + 2 * ROOT)
        g = g.astype(bf16)
        act_ref[...] = g
        slope_ref[...] = slope.astype(bf16)
        out_ref[...] = mm_last(g, down_ref[...]).astype(out_ref.dtype)

    either(lambda: work(own_ref, po_ref), lambda: work(rec_ref, pr_ref))


def tile_of(size):
    return 384 if size % 384 == 0 else 128


def hidden(own, rec, up, down, shift):
    half, wide = own.shape
    ff = up[1]
    n, own_spec, rec_spec, _ = split(half, min(half, 256), wide)
    strip = pl.BlockSpec((half // n, ff), lambda i: (i, 0))
    return pl.pallas_call(
        hidden_kernel,
        grid=(2 * n,),
        in_specs=[own_spec, rec_spec, columns(up), columns(down), const((1, ff))],
        out_specs=[strip, strip, own_spec, rec_spec],
        out_shape=[
            shape((2 * half, ff), bf16),
            shape((2 * half, ff), bf16),
            shape((half, wide), f32),
            shape((half, wide), bf16),
        ],
        compiler_params=params(30),
        cost_estimate=cost(8 * half * wide * ff, 4 * wide * ff + 20 * half * wide, 2 * half * ff),
    )(own, rec, up[0], down[0], shift[None])


def hidden_back_kernel(own_ref, rec_ref, slope_ref, up_ref, down_ref, de_ref, sum_ref, po_ref, pr_ref):
    @pl.when(pl.program_id(0) == 0)
    def _():
        sum_ref[...] = jnp.zeros_like(sum_ref)

    def work(ref, out_ref):
        de = (mm(ref[...], down_ref[...]) * slope_ref[...].astype(f32)).astype(bf16)
        de_ref[...] = de
        sum_ref[...] += jnp.sum(de.astype(f32), axis=0, keepdims=True)
        out_ref[...] = mm_last(de, up_ref[...]).astype(out_ref.dtype)

    either(lambda: work(own_ref, po_ref), lambda: work(rec_ref, pr_ref))


def hidden_back(own, rec, slope, up, down):
    half, wide = own.shape
    ff = up[1]
    n, own_spec, rec_spec, _ = split(half, min(half, 256), wide)
    strip = pl.BlockSpec((half // n, ff), lambda i: (i, 0))
    return pl.pallas_call(
        hidden_back_kernel,
        grid=(2 * n,),
        in_specs=[own_spec, rec_spec, strip, columns(up), columns(down)],
        out_specs=[strip, const((1, ff)), own_spec, rec_spec],
        out_shape=[
            shape((2 * half, ff), bf16),
            shape((1, ff), f32),
            shape((half, wide), f32),
            shape((half, wide), bf16),
        ],
        compiler_params=params(30),
        cost_estimate=cost(8 * half * wide * ff, 4 * wide * ff + 16 * half * wide),
    )(own, rec, slope, up[0], down[0])


def outer_kernel(lefts, rights, beside, bit_ref, *refs):
    left_refs, right_refs = refs[:lefts], refs[lefts : lefts + rights]
    rest = refs[lefts + rights :]
    if beside:
        beside_ref, rest = rest[0], rest[1:]
    mine_ref, theirs_ref = rest
    turned = right_refs[0].shape[0]
    cuts = [ref.shape[0] for ref in left_refs]
    total, at = None, 0
    for ref, size in zip(left_refs, cuts):
        low = at % turned
        right = right_refs[at // turned]
        part = mm_first(ref[...], right[low : low + size, :])
        total = part if total is None else total + part
        at += size
    out = total.astype(bf16)
    if beside:
        out = jnp.concatenate([out, beside_ref[...]], axis=1)
    half = out.shape[0] // 2

    @pl.when(bit_ref[0] == 0)
    def _():
        mine_ref[...], theirs_ref[...] = out[:half], out[half:]

    @pl.when(bit_ref[0] == 1)
    def _():
        mine_ref[...], theirs_ref[...] = out[half:], out[:half]


def outer(lefts, rights, bit, beside=None):
    depth, width = lefts[0].shape[1], rights[0].shape[1]
    rows = sum(v.shape[0] for v in lefts)
    extra = [] if beside is None else [beside]
    out = shape((depth // 2, width + sum(v.shape[1] for v in extra)), bf16)
    return pl.pallas_call(
        functools.partial(outer_kernel, len(lefts), len(rights), len(extra)),
        in_specs=[pl.BlockSpec(memory_space=pltpu.SMEM)]
        + [VMEM] * (len(lefts) + len(rights) + len(extra)),
        out_specs=[VMEM] * 2,
        out_shape=[out] * 2,
        compiler_params=params(30),
        cost_estimate=cost(2 * rows * depth * width, 2 * rows * (depth + width) + 2 * depth * width),
    )(bit, *lefts, *rights, *extra)


def outer_out_kernel(count, o_ref, *refs):
    out_ref = refs[count]
    total, at = None, 0
    for ref in refs[:count]:
        part = mm_first(o_ref[at : at + ref.shape[0], :], ref[...])
        total = part if total is None else total + part
        at += ref.shape[0]
    out_ref[...] = total.astype(bf16)


def outer_out(attended, rights):
    depth, width, rows = attended.shape[1], rights[0].shape[1], attended.shape[0]
    return pl.pallas_call(
        functools.partial(outer_out_kernel, len(rights)),
        in_specs=[VMEM] * (1 + len(rights)),
        out_specs=VMEM,
        out_shape=shape((depth, width), bf16),
        compiler_params=params(24),
        cost_estimate=cost(2 * rows * depth * width, 2 * rows * (depth + width) + 2 * depth * width),
    )(attended, *rights)


def spread(v):
    centred = v - jnp.mean(v, axis=-1, keepdims=True)
    scale = lax.rsqrt(jnp.mean(centred * centred, axis=-1, keepdims=True) + EPSILON)
    return centred * scale, scale


def norm_kernel(rows_of, v_ref, q_ref, come_ref, small_ref, next_ref, u_ref, m_ref):
    shift, gain, offset = rows_of
    u = v_ref[...] + (q_ref[...].astype(f32) + come_ref[...].astype(f32) + small_ref[shift : shift + 1, :])
    u_ref[...] = u
    n = spread(u)[0] * next_ref[gain : gain + 1, :] + next_ref[offset : offset + 1, :]
    m_ref[...] = n.astype(bf16)


def add_norm(v, q, come, small, following, rows_of):
    rows, width = v.shape
    block = pl.BlockSpec((min(rows, 256), width), lambda i: (i, 0))
    return pl.pallas_call(
        functools.partial(norm_kernel, rows_of),
        grid=(rows // min(rows, 256),),
        in_specs=[block] * 3 + [const(small.shape)] * 2,
        out_specs=[block] * 2,
        out_shape=[shape(v.shape, f32), shape(v.shape, bf16)],
        compiler_params=params(16),
        cost_estimate=cost(12 * v.size, 14 * v.size),
    )(v, q, come, small, following)


def norm_back_kernel(gain, v_ref, q_ref, come_ref, grad_ref, small_ref, out_ref, round_ref, sum_ref):
    @pl.when(pl.program_id(0) == 0)
    def _():
        sum_ref[...] = jnp.zeros_like(sum_ref)

    t = q_ref[...].astype(f32) + come_ref[...].astype(f32)
    n, scale = spread(v_ref[...])
    w = t * small_ref[gain : gain + 1, :]
    mean_w = jnp.mean(w, axis=-1, keepdims=True)
    mean_wn = jnp.mean(w * n, axis=-1, keepdims=True)
    out = grad_ref[...] + scale * (w - mean_w - n * mean_wn)
    out_ref[...] = out
    rounded = out.astype(bf16)
    round_ref[...] = rounded
    sum_ref[0:1, :] += jnp.sum(t * n, axis=0, keepdims=True)
    sum_ref[1:2, :] += jnp.sum(t, axis=0, keepdims=True)
    sum_ref[2:3, :] += jnp.sum(rounded.astype(f32), axis=0, keepdims=True)


def norm_back(v, q, come, grad, small, gain):
    rows, width = v.shape
    block = pl.BlockSpec((min(rows, 256), width), lambda i: (i, 0))
    return pl.pallas_call(
        functools.partial(norm_back_kernel, gain),
        grid=(rows // min(rows, 256),),
        in_specs=[block] * 4 + [const(small.shape)],
        out_specs=[block] * 2 + [const((8, width))],
        out_shape=[shape(v.shape, f32), shape(v.shape, bf16), shape((8, width), f32)],
        compiler_params=params(20),
        cost_estimate=cost(24 * v.size, 18 * v.size),
    )(v, q, come, grad, small)


def tie(values):
    return lax.optimization_barrier(values)


def pick(array, index, axis=0):
    return lax.dynamic_index_in_dim(array, index, axis, keepdims=False)


def swap_x(v):
    return lax.ppermute(v, "x", SWAP)


def swap_c(v):
    return lax.ppermute(v, "c", SWAP)


def in_order(axis, own, other):
    first = lax.axis_index(axis) == 0
    return jnp.where(first, own, other), jnp.where(first, other, own)


def exchange(blocks):
    xi, ci = lax.axis_index("x"), lax.axis_index("c")
    blocks = blocks.reshape((2, 2) + blocks.shape[1:])
    both = jnp.stack(in_order("x", pick(blocks, xi), swap_x(pick(blocks, 1 - xi))))
    out = in_order("c", pick(both, ci, 1), swap_c(pick(both, 1 - ci, 1)))
    return jnp.stack(out, axis=1).reshape((RANKS,) + blocks.shape[2:])


def flip(v, axis, step):
    size = lax.axis_size(axis)
    return lax.ppermute(v, axis, [(i, i ^ step) for i in range(size)])


def gather_rows(payload):
    return lax.all_gather(payload, ("hi", "seq"), axis=0, tiled=True)


def halve_rows(mine, theirs):
    step = lax.axis_size("hi") // 2
    place = lax.axis_index("hi")
    terms = (mine.astype(f32) + flip(theirs, "hi", step).astype(f32)).astype(bf16)
    step //= 2
    while step:
        halves = terms.reshape((2, -1) + terms.shape[1:])
        bit = (place // step) % 2
        come = flip(pick(halves, 1 - bit), "hi", step)
        terms = (pick(halves, bit).astype(f32) + come.astype(f32)).astype(bf16)
        step //= 2
    return terms


def scatter_rows(terms):
    return lax.psum_scatter(terms, "seq", scatter_dimension=0, tiled=True)


def body(
    tokens,
    cotangent,
    image_lengths,
    qkv_weight,
    out_weight,
    up_weight,
    down_weight,
    up_bias,
    norm_scale,
    shifts,
):
    rows, width = tokens.shape
    layers, held = qkv_weight.shape[0], qkv_weight.shape[1]
    blocks, seqs = lax.axis_size("hi"), lax.axis_size("seq")
    ways = seqs // RANKS
    shards = blocks * seqs
    chunk = seqs * held
    heads = HEADS // RANKS
    dim = width // HEADS
    part = width // RANKS
    ff = up_weight.shape[2]
    ff_part = ff // RANKS
    ff_pad = -(-ff_part // 128) * 128
    xi, ci = lax.axis_index("x"), lax.axis_index("c")
    rank = 2 * xi + ci

    spot = jnp.arange(width, dtype=jnp.int32)
    natural = ((spot // (RANKS * held * seqs) * RANKS + spot // held % RANKS) * seqs) * held
    natural = natural + spot // (RANKS * held) % seqs * held + spot % held
    turn_matrix = (spot[:, None] == natural[None, :]).astype(bf16)

    def mixed_order(v):
        return mm(v, turn_matrix).astype(bf16)

    def plain_order(v):
        return mm_last(v, turn_matrix)

    def mine(v):
        return pick(v.reshape(blocks, seqs, RANKS, held), rank, 2).reshape(part)

    def placed(v):
        v = v.reshape(blocks, seqs, 1, held)
        spots = (jnp.arange(RANKS) == rank)[None, None, :, None]
        return jnp.where(spots, v, 0.0).reshape(width)

    there, spots = [], (0, 3, 1, 2)
    for b in range(blocks):
        for r in range(RANKS):
            for s in range(seqs):
                target = (b * RANKS + s % RANKS) * seqs + spots[r] * ways + s // RANKS
                there.append(((b * RANKS + r) * seqs + s, target))
    back = [(target, source) for source, target in there]

    def rank_columns(piece):
        piece = piece.reshape(held, 3, blocks, RANKS, chunk)
        return piece.transpose(3, 0, 1, 2, 4).reshape(RANKS, held, 3 * part)

    def ff_columns(piece):
        piece = piece.reshape(held, RANKS, ff_part).transpose(1, 0, 2)
        return jnp.pad(piece, ((0, 0), (0, 0), (0, ff_pad - ff_part)))

    def out_rows(l):
        return mixed_order(out_weight[l]).reshape(held * RANKS, part)

    kinds = norm_scale.shape[2] + shifts.shape[2]
    smalls = jnp.concatenate([norm_scale, shifts], axis=2)
    smalls = smalls.transpose(1, 0, 2).reshape(1, held, layers * kinds)
    smalls = jnp.broadcast_to(smalls, (RANKS, held, layers * kinds))

    qkv_fulls, out_fulls, up_fulls, down_fulls = [], [], [], []
    came = exchange(jnp.concatenate([rank_columns(qkv_weight[0]), smalls], axis=2))
    came = came.reshape(RANKS * held, -1)
    payload = jnp.concatenate([came[:, : 3 * part], out_rows(0), came[:, 3 * part :]], axis=1)
    first = gather_rows(payload)
    def ff_pieces(weights):
        return [ff_columns(piece) for piece in weights]

    def pieces_of(weights):
        return [v for i, w in enumerate(weights) for v in (map(ff_columns, w) if i % 2 == 0 else [rank_columns(w)])]

    def payloads_of(weights, l):
        sent = exchange(jnp.concatenate(pieces_of(weights), axis=2)).reshape(RANKS * held, -1)
        payloads, at = [], 0
        for i in range(len(weights)):
            if i % 2 == 0:
                payloads.append(sent[:, at : at + 2 * ff_pad])
                at += 2 * ff_pad
            else:
                l += 1
                columns = sent[:, at : at + 3 * part]
                payloads.append(jnp.concatenate([columns, out_rows(l)], axis=1))
                at += 3 * part
        return payloads

    order = []
    for l in range(layers):
        order += [(up_weight[l], down_weight[l])] + [qkv_weight[i] for i in range(l + 1, min(l + 2, layers))]
    arrived = lax.ppermute(tokens, AXES, there)
    soon, _ = tie((order[:2], payload))
    soon, arrived = tie((soon, arrived))
    soon = payloads_of(soon, 0)
    own = mixed_order(arrived)
    soon, first, starts = tie((soon, first, in_order("x", own, swap_x(own))))
    gathered = [gather_rows(v) for v in soon]

    unit = jnp.eye(layers * kinds, dtype=bf16)
    small_full = mm_last(unit, first[:, width:]).reshape(layers, kinds, width)
    qkv_fulls.append((first, first.shape[1], 0))
    out_fulls.append(first[:, 3 * part : width].reshape(part, width))
    up_shift = pick(up_bias.reshape(layers, RANKS, ff_part), rank, 1).astype(f32)
    up_shift = jnp.pad(up_shift, ((0, 0), (0, ff_pad - ff_part)))

    xs = [(0, 1)] if CHUNKS == 1 else [(0,), (1,)]
    span = 4 * rows // CHUNKS
    lengths = lax.ppermute(image_lengths, AXES, there)
    finish = jnp.cumsum(lengths[0])
    base = jnp.arange(rows, dtype=jnp.int32)
    local = [
        jnp.concatenate([base + (2 * x + c) * rows for c in (ci, 1 - ci) for x in chunk_xs])
        for chunk_xs in xs
    ]
    group = RANKS * rows
    turn = lax.axis_index("seq") % ways

    def ids_of(pos):
        return jnp.sum((pos[:, None] >= finish[None, :]).astype(jnp.int32), axis=1)

    query_ids = [ids_of(v + turn * group) for v in local]
    key_ids = ids_of(jnp.concatenate([v + w * group for v in local for w in range(ways)]))
    seq_groups = [[j * ways + w for w in range(ways)] for j in range(seqs // ways)]

    def keys_of(qkv):
        if ways == 1:
            return qkv, part
        kv = lax.all_gather(
            qkv[:, part:], "seq", axis=0, tiled=True, axis_index_groups=seq_groups
        )
        return kv, 0

    def chunks_of(v):
        own = mixed_order(v)
        pair = in_order("x", own, swap_x(own))
        return list(pair) if CHUNKS == 2 else [jnp.concatenate(pair)]

    def at_x(chunks, index):
        if CHUNKS == 2:
            return jnp.where(index == 0, chunks[0], chunks[1])
        return pick(chunks[0].reshape((2, rows) + chunks[0].shape[1:]), index)

    def core_sum(own, other):
        return (own + swap_c(other).astype(f32)).astype(bf16)

    def last_sum(qs):
        return at_x(qs, xi), swap_x(at_x(qs, 1 - xi))

    GAIN1, GAIN2, OFF1, QB, VB, OB, OFF2, DB = range(8)
    starts = list(starts) if CHUNKS == 2 else [jnp.concatenate(starts)]
    current = [v.astype(f32) for v in starts]
    normed = [
        (spread(v)[0] * small_full[0, GAIN1] + small_full[0, OFF1]).astype(bf16) for v in current
    ]
    saved = []
    output = None
    for l in range(layers):
        if l > 0:
            full = gathered[2 * l - 1]
            qkv_fulls.append((full, width, 0))
            out_fulls.append(full[:, 3 * part :].reshape(part, width))
        up_fulls.append((gathered[2 * l], ff_pad, 0))
        down_fulls.append((gathered[2 * l], ff_pad, 1))
        small = small_full[l]
        attn_in = [(v, swap_c(v)) for v in normed]
        shift = jnp.concatenate([mine(small[QB]), jnp.zeros((part,), f32), mine(small[VB])])
        qkv = [project(own, rec, qkv_fulls[l], shift) for own, rec in attn_in]
        kvs = [keys_of(v) for v in qkv]
        offset, kvs = kvs[0][1], [v[0] for v in kvs]
        attended, totals, after, normed = [], [], [], []
        for j in range(CHUNKS):
            o, total, own, other = attend(
                qkv[j], kvs, offset, query_ids[j], key_ids, out_fulls[l], heads, dim
            )
            attended.append(o)
            totals.append(total)
            q = core_sum(own, other)
            if l == layers - 1 and j == 0:
                q, cotangent = tie((q, cotangent))
                arrived = lax.ppermute(cotangent, AXES, there)
            if l == 0 and j == 0:
                q, rest = tie((q, order[2:]))
            come = swap_x(q)
            if l == 0 and j == 0:
                come, rest = tie((come, payloads_of(rest, 1)))
                gathered += [gather_rows(v) for v in rest]
            if l == layers - 1 and j == 0:
                come, arrived = tie((come, arrived))
            u, m = add_norm(current[j], q, come, small, small, (OB, GAIN2, OFF2))
            after.append(u)
            normed.append(m)
        mlp_in = [(v, swap_c(v)) for v in normed]
        if l == layers - 1:
            rounded = chunks_of(arrived)
        slopes, acts, qs, following, normed = [], [], [], [], []
        for j in range(CHUNKS):
            slope, act, own, other = hidden(*mlp_in[j], up_fulls[l], down_fulls[l], up_shift[l])
            slopes.append(slope)
            acts.append(act)
            q = core_sum(own, other)
            qs.append(q)
            if l < layers - 1:
                u, m = add_norm(
                    after[j], q, swap_x(q), small, small_full[l + 1], (DB, GAIN1, OFF1)
                )
                following.append(u)
                normed.append(m)
        saved.append((current, attn_in, qkv, kvs, attended, totals, after, mlp_in, slopes, acts))
        current = following
        if l == layers - 1:
            output = (qs, after, small[DB])

    grads = [None] * layers
    vectors = [None] * layers
    biases = [None] * layers
    grad = [v.astype(f32) for v in rounded]
    d_sum = 0.5 * sum(jnp.sum(v, axis=0) for v in grad)
    tokens_grad = None
    top_bit = (lax.axis_index("hi") // (blocks // 2)).astype(jnp.int32)[None]

    def home_of(pieces):
        return exchange(jnp.concatenate(pieces, axis=1).reshape(RANKS, held, -1))


    waiting, homes = None, {}
    for l in reversed(range(layers)):
        (current, attn_in, qkv, kvs, attended, totals, after, mlp_in, slopes, acts) = saved[l]
        small = small_full[l]
        last_layer = waiting is None
        down_in = [(v, swap_c(v)) for v in rounded]
        down_terms = outer([v for pair in down_in for v in pair], acts, top_bit)
        down_in, down_terms = tie((down_in, down_terms))
        des, qs, bias = [], [], 0.0
        for j in range(CHUNKS):
            de, sums, own, other = hidden_back(*down_in[j], slopes[j], up_fulls[l], down_fulls[l])
            des.append(de)
            bias = bias + sums[0]
            qs.append(core_sum(own, other))
        biases[l] = bias
        if last_layer:
            qs, des = tie((qs, des))
        else:
            waiting = halve_rows(*waiting)
            qs, des, waiting = tie((qs, des, waiting))
            waiting = scatter_rows(waiting)
        comes = [swap_x(q) for q in qs]
        up_terms = outer([v for pair in mlp_in for v in pair], des, top_bit)
        down_terms = halve_rows(*down_terms)
        if last_layer:
            comes, down_terms, up_terms, output = tie((comes, down_terms, up_terms, output))
            q, come = last_sum(output[0])
            output = at_x(output[1], xi) + (q.astype(f32) + come.astype(f32) + output[2])
            output = output.astype(bf16)
        else:
            comes, down_terms, up_terms, grads[l + 1][2], output = tie(
                (comes, down_terms, up_terms, waiting, output)
            )
            output = lax.ppermute(output, AXES, back)
        if l > 0:
            down_owned = scatter_rows(down_terms)
        rounded, mid, sums = [], [], 0.0
        for j in range(CHUNKS):
            g, r, s = norm_back(after[j], qs[j], comes[j], grad[j], small, GAIN2)
            mid.append(g)
            rounded.append(r)
            sums = sums + 0.5 * s
        gain_two_sum, off_two_sum, o_sum = sums[0], sums[1], sums[2]
        out_in = [(v, swap_c(v)) for v in rounded]
        acc, dqs = None, []
        for j in range(CHUNKS):
            dq, acc = attend_back(
                qkv[j], kvs, 0 if ways > 1 else part, query_ids[j], key_ids, totals[j],
                out_fulls[l], *out_in[j], acc, j == CHUNKS - 1, heads, dim,
            )
            dqs.append(dq)
        if ways > 1:
            acc = acc.reshape(CHUNKS, ways, span, 2 * part).swapaxes(0, 1)
            acc = lax.psum_scatter(
                acc.reshape(ways * CHUNKS * span, 2 * part),
                "seq",
                scatter_dimension=0,
                tiled=True,
                axis_index_groups=seq_groups,
            )
        if not last_layer:
            dqs, acc, output, down_terms = tie((dqs, acc, output, down_terms))
        dqkvs, qs, sums_qkv = [], [], 0.0
        for j in range(CHUNKS):
            dqkv, own, other, s = join(dqs[j], acc, j, qkv_fulls[l])
            dqkvs.append(dqkv)
            sums_qkv = sums_qkv + s[0]
            qs.append(core_sum(own, other))
        up_terms = halve_rows(*up_terms)
        if last_layer:
            qs, dqkvs, out_in, up_terms, down_owned, output = tie(
                (qs, dqkvs, out_in, up_terms, down_owned, output)
            )
        else:
            down_owned = scatter_rows(down_terms)
            qs, dqkvs, out_in, up_terms = tie((qs, dqkvs, out_in, up_terms))
        up_owned = scatter_rows(up_terms)
        if l > 0:
            comes = [swap_x(q) for q in qs]
        else:
            q, comes = last_sum(qs)
        out_terms = outer_out(
            jnp.concatenate(attended) if CHUNKS > 1 else attended[0],
            [v for pair in out_in for v in pair],
        ).reshape(width, part)
        waiting = outer([v for pair in attn_in for v in pair], dqkvs, top_bit, out_terms)
        if not last_layer:
            grads[l + 1], waiting = tie((grads[l + 1], waiting))
            homes[l + 1] = home_of([grads[l + 1][0], grads[l + 1][1], grads[l + 1][2][:, : 3 * part]])
        if l > 0:
            comes, waiting, up_owned = tie((comes, waiting, up_owned))
        else:
            comes, waiting, down_owned = tie((comes, waiting, down_owned))
        d_next = None
        if l > 0:
            grad, rounded, sums = [], [], 0.0
            for j in range(CHUNKS):
                g, r, s = norm_back(current[j], qs[j], comes[j], mid[j], small, GAIN1)
                grad.append(g)
                rounded.append(r)
                sums = sums + 0.5 * s
            d_next = sums[2]
        else:
            g, r, sums = norm_back(at_x(current, xi), q, comes, at_x(mid, xi), small, GAIN1)
            tokens_grad = r
        vectors[l] = jnp.stack(
            [
                sums[0],
                gain_two_sum,
                sums[1],
                placed(sums_qkv[:part]),
                placed(sums_qkv[2 * part :]),
                o_sum,
                off_two_sum,
                d_sum,
            ]
        )
        d_sum = d_next
        grads[l] = [up_owned, down_owned, None]

    spots = (jnp.arange(RANKS) == rank)[None, :, None]
    bias = jnp.where(spots, jnp.stack(biases)[:, None, :], 0.0).reshape(layers * RANKS, ff_pad)
    wide = max(ff_pad, width)
    both = jnp.concatenate(
        [
            jnp.pad(jnp.concatenate(vectors), ((0, 0), (0, wide - width))),
            jnp.pad(bias, ((0, 0), (0, wide - ff_pad))),
        ]
    )
    tokens_grad = lax.ppermute(tokens_grad, AXES, back)

    def sum_along(v, axis):
        step = 1
        while step < lax.axis_size(axis):
            v = v + flip(v, axis, step)
            step *= 2
        return v

    both = sum_along(sum_along(both, "c"), "x")
    both, grads[0][0] = tie((both, grads[0][0]))
    both = sum_along(both, "hi")
    mine_last, theirs_last = waiting
    mine_last, both, tokens_grad, homes = tie((mine_last, both, tokens_grad, homes))
    last = scatter_rows(halve_rows(mine_last, theirs_last))
    both = sum_along(both, "seq")
    grads[0][2] = last
    homes[0] = home_of([grads[0][0], grads[0][1], last[:, : 3 * part]])
    results = [[None] * layers for _ in range(4)]
    for l in range(layers):
        owned = grads[l][2]
        results[1][l] = plain_order(owned[:, 3 * part :].reshape(held, width))
        for i in (2, 3):
            home = homes[l][:, :, (i - 2) * ff_pad : (i - 2) * ff_pad + ff_part]
            results[i][l] = home.transpose(1, 0, 2).reshape(held, ff)
        qkv_grad = homes[l][:, :, 2 * ff_pad :]
        qkv_grad = qkv_grad.reshape(RANKS, held, 3, blocks, chunk).transpose(1, 2, 3, 0, 4)
        results[0][l] = qkv_grad.reshape(held, 3 * width)
    results = [jnp.stack(v).astype(f32) for v in results]

    vector = both[: layers * kinds, :width].reshape(layers, kinds, blocks, seqs, RANKS, held)
    for axis, index in ((2, "hi"), (2, "seq")):
        vector = pick(vector, lax.axis_index(index), axis)
    vector = pick(vector, rank, 2).swapaxes(1, 2)
    bias = both[layers * kinds :, :ff_part].reshape(layers, ff)
    return (
        plain_order(output),
        plain_order(tokens_grad),
        *results,
        bias,
        vector[:, :, :2],
        vector[:, :, 2:],
    )


def solution(mesh):
    sizes = mesh.shape
    devices = mesh.devices.reshape(sizes["img"] // RANKS, 2, 2, sizes["seq"])
    fine = Mesh(devices, AXES)
    row = P(AXES, None)
    param = P(None, AXES, None)
    in_specs = (row, row, P(AXES[:3], None), param, param, param, param, P(), param, param)
    out_specs = (row, row, param, param, param, param, P(), param, param)
    return jax.shard_map(
        body, mesh=fine, in_specs=in_specs, out_specs=out_specs, check_vma=False
    )
```

```python
import functools
import math

import jax
import jax.numpy as jnp
from jax import lax
from jax.experimental import pallas as pl
from jax.experimental.pallas import tpu as pltpu
from jax.sharding import Mesh
from jax.sharding import PartitionSpec as P

HEADS = 16
RANKS = 4
CHUNKS = 1
EPSILON = 1e-06
NEGATIVE = -1e30
ROOT = math.sqrt(2.0 / math.pi)
AXES = ("hi", "x", "c", "seq")
SWAP = ((0, 1), (1, 0))
bf16, f32 = jnp.bfloat16, jnp.float32
VMEM = pl.BlockSpec(memory_space=pltpu.VMEM)


def mm(left, right):
    return jnp.dot(left, right, preferred_element_type=f32)


def mm_last(left, right):
    dims = (((1,), (1,)), ((), ()))
    return lax.dot_general(left, right, dims, preferred_element_type=f32)


def mm_first(left, right):
    dims = (((0,), (0,)), ((), ()))
    return lax.dot_general(left, right, dims, preferred_element_type=f32)


def shape(dims, kind):
    return jax.ShapeDtypeStruct(tuple(dims), kind)


def params(mib):
    return pltpu.CompilerParams(vmem_limit_bytes=mib * 2**20)


def cost(flops, moved, exps=0):
    share = 0.1
    return pl.CostEstimate(
        flops=int(share * flops), bytes_accessed=int(share * moved), transcendentals=int(share * exps)
    )


def const(dims):
    return pl.BlockSpec(tuple(dims), lambda i: (0,) * len(dims))


def columns(weight):
    array, width, place = weight
    return pl.BlockSpec((array.shape[0], width), lambda i: (0, place))


def split(half, block, width):
    n = half // block
    own = pl.BlockSpec((block, width), lambda i: (jnp.minimum(i, n - 1), 0))
    rec = pl.BlockSpec((block, width), lambda i: (jnp.maximum(i - n, 0), 0))
    strip = pl.BlockSpec((block, width), lambda i: (i, 0))
    return n, own, rec, strip


def either(own_work, rec_work):
    step, half = pl.program_id(0), pl.num_programs(0) // 2
    pl.when(step < half)(own_work)
    pl.when(step >= half)(rec_work)


def project_kernel(own_ref, rec_ref, w_ref, shift_ref, out_ref):
    width = out_ref.shape[1]

    def work(ref):
        out_ref[...] = (mm(ref[...], w_ref[:, :width]) + shift_ref[...]).astype(bf16)

    either(lambda: work(own_ref), lambda: work(rec_ref))


def project(own, rec, weight, shift):
    half, depth = own.shape
    width = shift.shape[0]
    n, own_spec, rec_spec, _ = split(half, min(half, 256), depth)
    return pl.pallas_call(
        project_kernel,
        grid=(2 * n,),
        in_specs=[own_spec, rec_spec, columns(weight), const((1, width))],
        out_specs=pl.BlockSpec((half // n, width), lambda i: (i, 0)),
        out_shape=shape((2 * half, width), bf16),
        compiler_params=params(24),
        cost_estimate=cost(4 * half * depth * width, 2 * depth * (2 * half + width)),
    )(own, rec, weight[0], shift[None])


def attend_kernel(heads, dim, offset, count, *refs):
    qid_ref, kid_ref, q_ref, wo_ref = refs[:4]
    kv_refs = refs[4 : 4 + count]
    o_ref, total_ref, own_ref, rec_ref = refs[4 + count :]
    factor = dim**-0.5 * math.log2(math.e)
    width = heads * dim
    same = qid_ref[...] == kid_ref[...]

    def scores(h):
        lo = h * dim
        q = q_ref[:, lo : lo + dim]
        k = jnp.concatenate([ref[:, offset + lo : offset + lo + dim] for ref in kv_refs])
        return jnp.where(same, mm_last(q, k), NEGATIVE)

    keys = sum(ref.shape[0] for ref in kv_refs)
    ones = jnp.ones((keys, 8), bf16)
    outs, totals = [], []
    following = scores(0)
    for h in range(heads):
        at = offset + width + h * dim
        v = jnp.concatenate([ref[:, at : at + dim] for ref in kv_refs])
        s = following
        if h < heads - 1:
            following = scores(h + 1)
        top = jnp.max(s, axis=1, keepdims=True)
        p = jnp.exp2((s - top) * factor).astype(bf16)
        o = mm(p, jnp.concatenate([v, ones], axis=1))
        total = o[:, dim : dim + 1]
        outs.append(o[:, :dim] * (1.0 / total))
        totals.append(top * factor + jnp.log2(total))
    o_ref[...] = jnp.concatenate(outs, axis=1).astype(bf16)
    total_ref[...] = jnp.concatenate(totals + totals, axis=1)

    def own_work():
        own_ref[...] = mm(o_ref[...], wo_ref[...])

    def rec_work():
        rec_ref[...] = mm(o_ref[...], wo_ref[...]).astype(bf16)

    either(own_work, rec_work)


def attend(qkv, kvs, offset, query_ids, key_ids, out_full, heads, dim):
    rows, width, wide = qkv.shape[0], heads * dim, out_full.shape[1]
    keys = sum(kv.shape[0] for kv in kvs)
    n, own_spec, rec_spec, _ = split(rows // 2, min(rows // 2, 512 * 1024 // keys), wide)
    block = rows // (2 * n)
    return pl.pallas_call(
        functools.partial(attend_kernel, heads, dim, offset, len(kvs)),
        grid=(2 * n,),
        in_specs=[
            pl.BlockSpec((block, 1), lambda i: (i, 0)),
            const((1, keys)),
            pl.BlockSpec((block, qkv.shape[1]), lambda i: (i, 0)),
            const(out_full.shape),
        ]
        + [const(kv.shape) for kv in kvs],
        out_specs=[
            pl.BlockSpec((block, width), lambda i: (i, 0)),
            pl.BlockSpec((block, 2 * heads), lambda i: (i, 0)),
            own_spec,
            rec_spec,
        ],
        out_shape=[
            shape((rows, width), bf16),
            shape((rows, 2 * heads), f32),
            shape((rows // 2, wide), f32),
            shape((rows // 2, wide), bf16),
        ],
        compiler_params=params(44),
        cost_estimate=cost(10 * rows * keys * width, 16 * rows * width, heads * rows * keys),
    )(query_ids[:, None], key_ids[None, :], qkv, out_full, *kvs)


def attend_back_kernel(heads, dim, offset, count, first, last, *refs):
    qid_ref, kid_ref, q_ref, total_ref, wo_ref, own_ref, rec_ref = refs[:7]
    kv_refs = refs[7 : 7 + count]
    rest = refs[7 + count :]
    if not first:
        before_ref, rest = rest[0], rest[1:]
    dq_ref, dkv_ref, do_ref, acc_ref = rest
    step = pl.program_id(0)
    scale = dim**-0.5
    factor = scale * math.log2(math.e)
    width = heads * dim

    @pl.when(step == 0)
    def _():
        acc_ref[...] = jnp.zeros_like(acc_ref) if first else before_ref[...]

    def own_work():
        do_ref[...] = mm_last(own_ref[...], wo_ref[...]).astype(bf16)

    def rec_work():
        do_ref[...] = mm_last(rec_ref[...], wo_ref[...]).astype(bf16)

    either(own_work, rec_work)
    same = kid_ref[...] == qid_ref[...]
    dqs = []
    for h in range(heads):
        lo = h * dim
        at = offset + width + lo
        q = q_ref[:, lo : lo + dim]
        do = do_ref[:, lo : lo + dim]
        k = jnp.concatenate([ref[:, offset + lo : offset + lo + dim] for ref in kv_refs])
        v = jnp.concatenate([ref[:, at : at + dim] for ref in kv_refs])
        s = jnp.where(same, mm_last(k, q), NEGATIVE)
        p = jnp.exp2(s * factor - total_ref[h : h + 1, :])
        dp = mm_last(v, do)
        delta = jnp.sum(p * dp, axis=0, keepdims=True)
        ds = (p * (dp - delta)).astype(bf16)
        acc_ref[heads + h] += mm(p.astype(bf16), do)
        acc_ref[h] += mm(ds, q)
        dqs.append(mm_first(ds, k) * scale)
    dq_ref[...] = jnp.concatenate(dqs, axis=1).astype(bf16)

    @pl.when(step == pl.num_programs(0) - 1)
    def _():
        if last:
            parts = [acc_ref[h] * scale for h in range(heads)]
            parts += [acc_ref[heads + h] for h in range(heads)]
            dkv_ref[...] = jnp.concatenate(parts, axis=1).astype(bf16)
        else:
            dkv_ref[...] = acc_ref[...]


def attend_back(
    qkv, kvs, offset, query_ids, key_ids, totals, out_full, own, rec, before, last, heads, dim
):
    rows, width, wide = qkv.shape[0], heads * dim, out_full.shape[1]
    keys = sum(kv.shape[0] for kv in kvs)
    sums = (2 * heads, keys, dim)
    extra = [] if before is None else [before]
    n, own_spec, rec_spec, _ = split(rows // 2, min(rows // 2, 512 * 1024 // keys), wide)
    block = rows // (2 * n)
    done = shape((keys, 2 * width), bf16) if last else shape(sums, f32)
    return pl.pallas_call(
        functools.partial(attend_back_kernel, heads, dim, offset, len(kvs), before is None, last),
        grid=(2 * n,),
        in_specs=[
            pl.BlockSpec((1, block), lambda i: (0, i)),
            const((keys, 1)),
            pl.BlockSpec((block, qkv.shape[1]), lambda i: (i, 0)),
            pl.BlockSpec((2 * heads, block), lambda i: (0, i)),
            const(out_full.shape),
            own_spec,
            rec_spec,
        ]
        + [const(v.shape) for v in list(kvs) + extra],
        out_specs=[pl.BlockSpec((block, width), lambda i: (i, 0)), const(done.shape)],
        out_shape=[shape((rows, width), bf16), done],
        scratch_shapes=[pltpu.VMEM((block, width), bf16), pltpu.VMEM(sums, f32)],
        compiler_params=params(52),
        cost_estimate=cost(24 * rows * keys * width, 30 * rows * width, heads * rows * keys),
    )(query_ids[None, :], key_ids[:, None], qkv, totals.T, out_full, own, rec, *kvs, *extra)


def join_kernel(dq_ref, dkv_ref, w_ref, dqkv_ref, own_ref, rec_ref, sum_ref):
    @pl.when(pl.program_id(0) == 0)
    def _():
        sum_ref[...] = jnp.zeros_like(sum_ref)

    dqkv = jnp.concatenate([dq_ref[...], dkv_ref[...]], axis=1)
    dqkv_ref[...] = dqkv
    sum_ref[...] += jnp.sum(dqkv.astype(f32), axis=0, keepdims=True)
    width = dqkv.shape[1]

    def own_work():
        own_ref[...] = mm_last(dqkv_ref[...], w_ref[:, :width])

    def rec_work():
        rec_ref[...] = mm_last(dqkv_ref[...], w_ref[:, :width]).astype(bf16)

    either(own_work, rec_work)


def join(dq, dkv, chunk, weight):
    rows, width, wide = dq.shape[0], dq.shape[1] + dkv.shape[1], weight[0].shape[0]
    n, own_spec, rec_spec, _ = split(rows // 2, min(rows // 2, 256), wide)
    block, at = rows // (2 * n), 2 * n * chunk
    return pl.pallas_call(
        join_kernel,
        grid=(2 * n,),
        in_specs=[
            pl.BlockSpec((block, dq.shape[1]), lambda i: (i, 0)),
            pl.BlockSpec((block, dkv.shape[1]), lambda i: (at + i, 0)),
            columns(weight),
        ],
        out_specs=[pl.BlockSpec((block, width), lambda i: (i, 0)), own_spec, rec_spec, const((1, width))],
        out_shape=[
            shape((rows, width), bf16),
            shape((rows // 2, wide), f32),
            shape((rows // 2, wide), bf16),
            shape((1, width), f32),
        ],
        compiler_params=params(24),
        cost_estimate=cost(2 * rows * width * wide, 4 * wide * (rows + width)),
    )(dq, dkv, weight[0])


def hidden_kernel(own_ref, rec_ref, up_ref, down_ref, shift_ref, slope_ref, act_ref, po_ref, pr_ref):
    def work(ref, out_ref):
        e = mm(ref[...], up_ref[...]) + shift_ref[...]
        square = e * e
        h = 0.5 * jnp.tanh(e * (square * (ROOT * 0.044715) + ROOT)) + 0.5
        g = e * h
        slope = h + g * (1.0 - h) * (square * (6 * ROOT * 0.044715) + 2 * ROOT)
        g = g.astype(bf16)
        act_ref[...] = g
        slope_ref[...] = slope.astype(bf16)
        out_ref[...] = mm_last(g, down_ref[...]).astype(out_ref.dtype)

    either(lambda: work(own_ref, po_ref), lambda: work(rec_ref, pr_ref))


def tile_of(size):
    return 384 if size % 384 == 0 else 128


def hidden(own, rec, up, down, shift):
    half, wide = own.shape
    ff = up[1]
    n, own_spec, rec_spec, _ = split(half, min(half, 256), wide)
    strip = pl.BlockSpec((half // n, ff), lambda i: (i, 0))
    return pl.pallas_call(
        hidden_kernel,
        grid=(2 * n,),
        in_specs=[own_spec, rec_spec, columns(up), columns(down), const((1, ff))],
        out_specs=[strip, strip, own_spec, rec_spec],
        out_shape=[
            shape((2 * half, ff), bf16),
            shape((2 * half, ff), bf16),
            shape((half, wide), f32),
            shape((half, wide), bf16),
        ],
        compiler_params=params(30),
        cost_estimate=cost(8 * half * wide * ff, 4 * wide * ff + 20 * half * wide, 2 * half * ff),
    )(own, rec, up[0], down[0], shift[None])


def hidden_back_kernel(own_ref, rec_ref, slope_ref, up_ref, down_ref, de_ref, sum_ref, po_ref, pr_ref):
    @pl.when(pl.program_id(0) == 0)
    def _():
        sum_ref[...] = jnp.zeros_like(sum_ref)

    def work(ref, out_ref):
        de = (mm(ref[...], down_ref[...]) * slope_ref[...].astype(f32)).astype(bf16)
        de_ref[...] = de
        sum_ref[...] += jnp.sum(de.astype(f32), axis=0, keepdims=True)
        out_ref[...] = mm_last(de, up_ref[...]).astype(out_ref.dtype)

    either(lambda: work(own_ref, po_ref), lambda: work(rec_ref, pr_ref))


def hidden_back(own, rec, slope, up, down):
    half, wide = own.shape
    ff = up[1]
    n, own_spec, rec_spec, _ = split(half, min(half, 256), wide)
    strip = pl.BlockSpec((half // n, ff), lambda i: (i, 0))
    return pl.pallas_call(
        hidden_back_kernel,
        grid=(2 * n,),
        in_specs=[own_spec, rec_spec, strip, columns(up), columns(down)],
        out_specs=[strip, const((1, ff)), own_spec, rec_spec],
        out_shape=[
            shape((2 * half, ff), bf16),
            shape((1, ff), f32),
            shape((half, wide), f32),
            shape((half, wide), bf16),
        ],
        compiler_params=params(30),
        cost_estimate=cost(8 * half * wide * ff, 4 * wide * ff + 16 * half * wide),
    )(own, rec, slope, up[0], down[0])


def outer_kernel(lefts, rights, beside, bit_ref, *refs):
    left_refs, right_refs = refs[:lefts], refs[lefts : lefts + rights]
    rest = refs[lefts + rights :]
    if beside:
        beside_ref, rest = rest[0], rest[1:]
    mine_ref, theirs_ref = rest
    turned = right_refs[0].shape[0]
    cuts = [ref.shape[0] for ref in left_refs]
    total, at = None, 0
    for ref, size in zip(left_refs, cuts):
        low = at % turned
        right = right_refs[at // turned]
        part = mm_first(ref[...], right[low : low + size, :])
        total = part if total is None else total + part
        at += size
    out = total.astype(bf16)
    if beside:
        out = jnp.concatenate([out, beside_ref[...]], axis=1)
    half = out.shape[0] // 2

    @pl.when(bit_ref[0] == 0)
    def _():
        mine_ref[...], theirs_ref[...] = out[:half], out[half:]

    @pl.when(bit_ref[0] == 1)
    def _():
        mine_ref[...], theirs_ref[...] = out[half:], out[:half]


def outer(lefts, rights, bit, beside=None):
    depth, width = lefts[0].shape[1], rights[0].shape[1]
    rows = sum(v.shape[0] for v in lefts)
    extra = [] if beside is None else [beside]
    out = shape((depth // 2, width + sum(v.shape[1] for v in extra)), bf16)
    return pl.pallas_call(
        functools.partial(outer_kernel, len(lefts), len(rights), len(extra)),
        in_specs=[pl.BlockSpec(memory_space=pltpu.SMEM)]
        + [VMEM] * (len(lefts) + len(rights) + len(extra)),
        out_specs=[VMEM] * 2,
        out_shape=[out] * 2,
        compiler_params=params(30),
        cost_estimate=cost(2 * rows * depth * width, 2 * rows * (depth + width) + 2 * depth * width),
    )(bit, *lefts, *rights, *extra)


def outer_out_kernel(count, o_ref, *refs):
    out_ref = refs[count]
    total, at = None, 0
    for ref in refs[:count]:
        part = mm_first(o_ref[at : at + ref.shape[0], :], ref[...])
        total = part if total is None else total + part
        at += ref.shape[0]
    out_ref[...] = total.astype(bf16)


def outer_out(attended, rights):
    depth, width, rows = attended.shape[1], rights[0].shape[1], attended.shape[0]
    return pl.pallas_call(
        functools.partial(outer_out_kernel, len(rights)),
        in_specs=[VMEM] * (1 + len(rights)),
        out_specs=VMEM,
        out_shape=shape((depth, width), bf16),
        compiler_params=params(24),
        cost_estimate=cost(2 * rows * depth * width, 2 * rows * (depth + width) + 2 * depth * width),
    )(attended, *rights)


def spread(v):
    centred = v - jnp.mean(v, axis=-1, keepdims=True)
    scale = lax.rsqrt(jnp.mean(centred * centred, axis=-1, keepdims=True) + EPSILON)
    return centred * scale, scale


def norm_kernel(rows_of, v_ref, q_ref, come_ref, small_ref, next_ref, u_ref, m_ref):
    shift, gain, offset = rows_of
    u = v_ref[...] + (q_ref[...].astype(f32) + come_ref[...].astype(f32) + small_ref[shift : shift + 1, :])
    u_ref[...] = u
    n = spread(u)[0] * next_ref[gain : gain + 1, :] + next_ref[offset : offset + 1, :]
    m_ref[...] = n.astype(bf16)


def add_norm(v, q, come, small, following, rows_of):
    rows, width = v.shape
    block = pl.BlockSpec((min(rows, 256), width), lambda i: (i, 0))
    return pl.pallas_call(
        functools.partial(norm_kernel, rows_of),
        grid=(rows // min(rows, 256),),
        in_specs=[block] * 3 + [const(small.shape)] * 2,
        out_specs=[block] * 2,
        out_shape=[shape(v.shape, f32), shape(v.shape, bf16)],
        compiler_params=params(16),
        cost_estimate=cost(12 * v.size, 14 * v.size),
    )(v, q, come, small, following)


def norm_back_kernel(gain, v_ref, q_ref, come_ref, grad_ref, small_ref, out_ref, round_ref, sum_ref):
    @pl.when(pl.program_id(0) == 0)
    def _():
        sum_ref[...] = jnp.zeros_like(sum_ref)

    t = q_ref[...].astype(f32) + come_ref[...].astype(f32)
    n, scale = spread(v_ref[...])
    w = t * small_ref[gain : gain + 1, :]
    mean_w = jnp.mean(w, axis=-1, keepdims=True)
    mean_wn = jnp.mean(w * n, axis=-1, keepdims=True)
    out = grad_ref[...] + scale * (w - mean_w - n * mean_wn)
    out_ref[...] = out
    rounded = out.astype(bf16)
    round_ref[...] = rounded
    sum_ref[0:1, :] += jnp.sum(t * n, axis=0, keepdims=True)
    sum_ref[1:2, :] += jnp.sum(t, axis=0, keepdims=True)
    sum_ref[2:3, :] += jnp.sum(rounded.astype(f32), axis=0, keepdims=True)


def norm_back(v, q, come, grad, small, gain):
    rows, width = v.shape
    block = pl.BlockSpec((min(rows, 256), width), lambda i: (i, 0))
    return pl.pallas_call(
        functools.partial(norm_back_kernel, gain),
        grid=(rows // min(rows, 256),),
        in_specs=[block] * 4 + [const(small.shape)],
        out_specs=[block] * 2 + [const((8, width))],
        out_shape=[shape(v.shape, f32), shape(v.shape, bf16), shape((8, width), f32)],
        compiler_params=params(20),
        cost_estimate=cost(24 * v.size, 18 * v.size),
    )(v, q, come, grad, small)


def tie(values):
    return lax.optimization_barrier(values)


def pick(array, index, axis=0):
    return lax.dynamic_index_in_dim(array, index, axis, keepdims=False)


def swap_x(v):
    return lax.ppermute(v, "x", SWAP)


def swap_c(v):
    return lax.ppermute(v, "c", SWAP)


def in_order(axis, own, other):
    first = lax.axis_index(axis) == 0
    return jnp.where(first, own, other), jnp.where(first, other, own)


def exchange(blocks):
    xi, ci = lax.axis_index("x"), lax.axis_index("c")
    blocks = blocks.reshape((2, 2) + blocks.shape[1:])
    both = jnp.stack(in_order("x", pick(blocks, xi), swap_x(pick(blocks, 1 - xi))))
    out = in_order("c", pick(both, ci, 1), swap_c(pick(both, 1 - ci, 1)))
    return jnp.stack(out, axis=1).reshape((RANKS,) + blocks.shape[2:])


def flip(v, axis, step):
    size = lax.axis_size(axis)
    return lax.ppermute(v, axis, [(i, i ^ step) for i in range(size)])


def gather_rows(payload):
    return lax.all_gather(payload, ("hi", "seq"), axis=0, tiled=True)


def halve_rows(mine, theirs):
    step = lax.axis_size("hi") // 2
    place = lax.axis_index("hi")
    terms = (mine.astype(f32) + flip(theirs, "hi", step).astype(f32)).astype(bf16)
    step //= 2
    while step:
        halves = terms.reshape((2, -1) + terms.shape[1:])
        bit = (place // step) % 2
        come = flip(pick(halves, 1 - bit), "hi", step)
        terms = (pick(halves, bit).astype(f32) + come.astype(f32)).astype(bf16)
        step //= 2
    return terms


def scatter_rows(terms):
    return lax.psum_scatter(terms, "seq", scatter_dimension=0, tiled=True)


def body(
    tokens,
    cotangent,
    image_lengths,
    qkv_weight,
    out_weight,
    up_weight,
    down_weight,
    up_bias,
    norm_scale,
    shifts,
):
    rows, width = tokens.shape
    layers, held = qkv_weight.shape[0], qkv_weight.shape[1]
    blocks, seqs = lax.axis_size("hi"), lax.axis_size("seq")
    ways = seqs // RANKS
    shards = blocks * seqs
    chunk = seqs * held
    heads = HEADS // RANKS
    dim = width // HEADS
    part = width // RANKS
    ff = up_weight.shape[2]
    ff_part = ff // RANKS
    ff_pad = -(-ff_part // 128) * 128
    xi, ci = lax.axis_index("x"), lax.axis_index("c")
    rank = 2 * xi + ci

    spot = jnp.arange(width, dtype=jnp.int32)
    natural = ((spot // (RANKS * held * seqs) * RANKS + spot // held % RANKS) * seqs) * held
    natural = natural + spot // (RANKS * held) % seqs * held + spot % held
    turn_matrix = (spot[:, None] == natural[None, :]).astype(bf16)

    def mixed_order(v):
        return mm(v, turn_matrix).astype(bf16)

    def plain_order(v):
        return mm_last(v, turn_matrix)

    def mine(v):
        return pick(v.reshape(blocks, seqs, RANKS, held), rank, 2).reshape(part)

    def placed(v):
        v = v.reshape(blocks, seqs, 1, held)
        spots = (jnp.arange(RANKS) == rank)[None, None, :, None]
        return jnp.where(spots, v, 0.0).reshape(width)

    there, spots = [], (0, 3, 1, 2)
    for b in range(blocks):
        for r in range(RANKS):
            for s in range(seqs):
                target = (b * RANKS + s % RANKS) * seqs + spots[r] * ways + s // RANKS
                there.append(((b * RANKS + r) * seqs + s, target))
    back = [(target, source) for source, target in there]

    def rank_columns(piece):
        piece = piece.reshape(held, 3, blocks, RANKS, chunk)
        return piece.transpose(3, 0, 1, 2, 4).reshape(RANKS, held, 3 * part)

    def ff_columns(piece):
        piece = piece.reshape(held, RANKS, ff_part).transpose(1, 0, 2)
        return jnp.pad(piece, ((0, 0), (0, 0), (0, ff_pad - ff_part)))

    def out_rows(l):
        return mixed_order(out_weight[l]).reshape(held * RANKS, part)

    kinds = norm_scale.shape[2] + shifts.shape[2]
    smalls = jnp.concatenate([norm_scale, shifts], axis=2)
    smalls = smalls.transpose(1, 0, 2).reshape(1, held, layers * kinds)
    smalls = jnp.broadcast_to(smalls, (RANKS, held, layers * kinds))

    qkv_fulls, out_fulls, up_fulls, down_fulls = [], [], [], []
    came = exchange(jnp.concatenate([rank_columns(qkv_weight[0]), smalls], axis=2))
    came = came.reshape(RANKS * held, -1)
    payload = jnp.concatenate([came[:, : 3 * part], out_rows(0), came[:, 3 * part :]], axis=1)
    first = gather_rows(payload)
    def ff_pieces(weights):
        return [ff_columns(piece) for piece in weights]

    def pieces_of(weights):
        return [v for i, w in enumerate(weights) for v in (map(ff_columns, w) if i % 2 == 0 else [rank_columns(w)])]

    def payloads_of(weights, l):
        sent = exchange(jnp.concatenate(pieces_of(weights), axis=2)).reshape(RANKS * held, -1)
        payloads, at = [], 0
        for i in range(len(weights)):
            if i % 2 == 0:
                payloads.append(sent[:, at : at + 2 * ff_pad])
                at += 2 * ff_pad
            else:
                l += 1
                columns = sent[:, at : at + 3 * part]
                payloads.append(jnp.concatenate([columns, out_rows(l)], axis=1))
                at += 3 * part
        return payloads

    order = []
    for l in range(layers):
        order += [(up_weight[l], down_weight[l])] + [qkv_weight[i] for i in range(l + 1, min(l + 2, layers))]
    arrived = lax.ppermute(tokens, AXES, there)
    soon, _ = tie((order[:2], payload))
    soon, arrived = tie((soon, arrived))
    soon = payloads_of(soon, 0)
    own = mixed_order(arrived)
    soon, first, starts = tie((soon, first, in_order("x", own, swap_x(own))))
    gathered = [gather_rows(v) for v in soon]

    unit = jnp.eye(layers * kinds, dtype=bf16)
    small_full = mm_last(unit, first[:, width:]).reshape(layers, kinds, width)
    qkv_fulls.append((first, first.shape[1], 0))
    out_fulls.append(first[:, 3 * part : width].reshape(part, width))
    up_shift = pick(up_bias.reshape(layers, RANKS, ff_part), rank, 1).astype(f32)
    up_shift = jnp.pad(up_shift, ((0, 0), (0, ff_pad - ff_part)))

    xs = [(0, 1)] if CHUNKS == 1 else [(0,), (1,)]
    span = 4 * rows // CHUNKS
    lengths = lax.ppermute(image_lengths, AXES, there)
    finish = jnp.cumsum(lengths[0])
    base = jnp.arange(rows, dtype=jnp.int32)
    local = [
        jnp.concatenate([base + (2 * x + c) * rows for c in (ci, 1 - ci) for x in chunk_xs])
        for chunk_xs in xs
    ]
    group = RANKS * rows
    turn = lax.axis_index("seq") % ways

    def ids_of(pos):
        return jnp.sum((pos[:, None] >= finish[None, :]).astype(jnp.int32), axis=1)

    query_ids = [ids_of(v + turn * group) for v in local]
    key_ids = ids_of(jnp.concatenate([v + w * group for v in local for w in range(ways)]))
    seq_groups = [[j * ways + w for w in range(ways)] for j in range(seqs // ways)]

    def keys_of(qkv):
        if ways == 1:
            return qkv, part
        kv = lax.all_gather(
            qkv[:, part:], "seq", axis=0, tiled=True, axis_index_groups=seq_groups
        )
        return kv, 0

    def chunks_of(v):
        own = mixed_order(v)
        pair = in_order("x", own, swap_x(own))
        return list(pair) if CHUNKS == 2 else [jnp.concatenate(pair)]

    def at_x(chunks, index):
        if CHUNKS == 2:
            return jnp.where(index == 0, chunks[0], chunks[1])
        return pick(chunks[0].reshape((2, rows) + chunks[0].shape[1:]), index)

    def core_sum(own, other):
        return (own + swap_c(other).astype(f32)).astype(bf16)

    def last_sum(qs):
        return at_x(qs, xi), swap_x(at_x(qs, 1 - xi))

    GAIN1, GAIN2, OFF1, QB, VB, OB, OFF2, DB = range(8)
    starts = list(starts) if CHUNKS == 2 else [jnp.concatenate(starts)]
    current = [v.astype(f32) for v in starts]
    normed = [
        (spread(v)[0] * small_full[0, GAIN1] + small_full[0, OFF1]).astype(bf16) for v in current
    ]
    saved = []
    output = None
    for l in range(layers):
        if l > 0:
            full = gathered[2 * l - 1]
            qkv_fulls.append((full, width, 0))
            out_fulls.append(full[:, 3 * part :].reshape(part, width))
        up_fulls.append((gathered[2 * l], ff_pad, 0))
        down_fulls.append((gathered[2 * l], ff_pad, 1))
        small = small_full[l]
        attn_in = [(v, swap_c(v)) for v in normed]
        if l == layers - 1:
            attn_in, cotangent = tie((attn_in, cotangent))
            arrived = lax.ppermute(cotangent, AXES, there)
        shift = jnp.concatenate([mine(small[QB]), jnp.zeros((part,), f32), mine(small[VB])])
        qkv = [project(own, rec, qkv_fulls[l], shift) for own, rec in attn_in]
        kvs = [keys_of(v) for v in qkv]
        offset, kvs = kvs[0][1], [v[0] for v in kvs]
        attended, totals, after, normed = [], [], [], []
        for j in range(CHUNKS):
            o, total, own, other = attend(
                qkv[j], kvs, offset, query_ids[j], key_ids, out_fulls[l], heads, dim
            )
            if l == layers - 1 and j == 0:
                o, total, own, other, arrived = tie((o, total, own, other, arrived))
            attended.append(o)
            totals.append(total)
            q = core_sum(own, other)
            if l == 0 and j == 0:
                q, rest = tie((q, order[2:]))
            come = swap_x(q)
            if l == 0 and j == 0:
                come, rest = tie((come, payloads_of(rest, 1)))
                gathered += [gather_rows(v) for v in rest]
            if l == layers - 1 and j == 0:
                come, arrived = tie((come, arrived))
            u, m = add_norm(current[j], q, come, small, small, (OB, GAIN2, OFF2))
            after.append(u)
            normed.append(m)
        mlp_in = [(v, swap_c(v)) for v in normed]
        if l == layers - 1:
            rounded = chunks_of(arrived)
        slopes, acts, qs, following, normed = [], [], [], [], []
        for j in range(CHUNKS):
            slope, act, own, other = hidden(*mlp_in[j], up_fulls[l], down_fulls[l], up_shift[l])
            slopes.append(slope)
            acts.append(act)
            q = core_sum(own, other)
            qs.append(q)
            if l < layers - 1:
                u, m = add_norm(
                    after[j], q, swap_x(q), small, small_full[l + 1], (DB, GAIN1, OFF1)
                )
                following.append(u)
                normed.append(m)
        saved.append((current, attn_in, qkv, kvs, attended, totals, after, mlp_in, slopes, acts))
        current = following
        if l == layers - 1:
            output = (qs, after, small[DB])

    grads = [None] * layers
    vectors = [None] * layers
    biases = [None] * layers
    grad = [v.astype(f32) for v in rounded]
    d_sum = 0.5 * sum(jnp.sum(v, axis=0) for v in grad)
    tokens_grad = None
    top_bit = (lax.axis_index("hi") // (blocks // 2)).astype(jnp.int32)[None]

    def home_of(pieces):
        return exchange(jnp.concatenate(pieces, axis=1).reshape(RANKS, held, -1))


    waiting, homes = None, {}
    for l in reversed(range(layers)):
        (current, attn_in, qkv, kvs, attended, totals, after, mlp_in, slopes, acts) = saved[l]
        small = small_full[l]
        last_layer = waiting is None
        down_in = [(v, swap_c(v)) for v in rounded]
        down_terms = outer([v for pair in down_in for v in pair], acts, top_bit)
        down_in, down_terms = tie((down_in, down_terms))
        des, qs, bias = [], [], 0.0
        for j in range(CHUNKS):
            de, sums, own, other = hidden_back(*down_in[j], slopes[j], up_fulls[l], down_fulls[l])
            des.append(de)
            bias = bias + sums[0]
            qs.append(core_sum(own, other))
        biases[l] = bias
        if last_layer:
            qs, des = tie((qs, des))
        else:
            waiting = halve_rows(*waiting)
            qs, des, waiting = tie((qs, des, waiting))
            waiting = scatter_rows(waiting)
        comes = [swap_x(q) for q in qs]
        up_terms = outer([v for pair in mlp_in for v in pair], des, top_bit)
        down_terms = halve_rows(*down_terms)
        if last_layer:
            comes, down_terms, up_terms, output = tie((comes, down_terms, up_terms, output))
            q, come = last_sum(output[0])
            output = at_x(output[1], xi) + (q.astype(f32) + come.astype(f32) + output[2])
            output = output.astype(bf16)
        else:
            comes, down_terms, up_terms, grads[l + 1][2], output = tie(
                (comes, down_terms, up_terms, waiting, output)
            )
            output = lax.ppermute(output, AXES, back)
        if l > 0:
            down_owned = scatter_rows(down_terms)
        rounded, mid, sums = [], [], 0.0
        for j in range(CHUNKS):
            g, r, s = norm_back(after[j], qs[j], comes[j], grad[j], small, GAIN2)
            mid.append(g)
            rounded.append(r)
            sums = sums + 0.5 * s
        gain_two_sum, off_two_sum, o_sum = sums[0], sums[1], sums[2]
        out_in = [(v, swap_c(v)) for v in rounded]
        acc, dqs = None, []
        for j in range(CHUNKS):
            dq, acc = attend_back(
                qkv[j], kvs, 0 if ways > 1 else part, query_ids[j], key_ids, totals[j],
                out_fulls[l], *out_in[j], acc, j == CHUNKS - 1, heads, dim,
            )
            dqs.append(dq)
        if ways > 1:
            acc = acc.reshape(CHUNKS, ways, span, 2 * part).swapaxes(0, 1)
            acc = lax.psum_scatter(
                acc.reshape(ways * CHUNKS * span, 2 * part),
                "seq",
                scatter_dimension=0,
                tiled=True,
                axis_index_groups=seq_groups,
            )
        if not last_layer:
            dqs, acc, output, down_terms = tie((dqs, acc, output, down_terms))
        dqkvs, qs, sums_qkv = [], [], 0.0
        for j in range(CHUNKS):
            dqkv, own, other, s = join(dqs[j], acc, j, qkv_fulls[l])
            dqkvs.append(dqkv)
            sums_qkv = sums_qkv + s[0]
            qs.append(core_sum(own, other))
        up_terms = halve_rows(*up_terms)
        if last_layer:
            qs, dqkvs, out_in, up_terms, down_owned, output = tie(
                (qs, dqkvs, out_in, up_terms, down_owned, output)
            )
        else:
            down_owned = scatter_rows(down_terms)
            qs, dqkvs, out_in, up_terms = tie((qs, dqkvs, out_in, up_terms))
        up_owned = scatter_rows(up_terms)
        if l > 0:
            comes = [swap_x(q) for q in qs]
        else:
            q, comes = last_sum(qs)
        out_terms = outer_out(
            jnp.concatenate(attended) if CHUNKS > 1 else attended[0],
            [v for pair in out_in for v in pair],
        ).reshape(width, part)
        waiting = outer([v for pair in attn_in for v in pair], dqkvs, top_bit, out_terms)
        if not last_layer:
            grads[l + 1], waiting = tie((grads[l + 1], waiting))
            homes[l + 1] = home_of([grads[l + 1][0], grads[l + 1][1], grads[l + 1][2][:, : 3 * part]])
        if l > 0:
            comes, waiting, up_owned = tie((comes, waiting, up_owned))
        else:
            comes, waiting, down_owned = tie((comes, waiting, down_owned))
        d_next = None
        if l > 0:
            grad, rounded, sums = [], [], 0.0
            for j in range(CHUNKS):
                g, r, s = norm_back(current[j], qs[j], comes[j], mid[j], small, GAIN1)
                grad.append(g)
                rounded.append(r)
                sums = sums + 0.5 * s
            d_next = sums[2]
        else:
            g, r, sums = norm_back(at_x(current, xi), q, comes, at_x(mid, xi), small, GAIN1)
            tokens_grad = r
        vectors[l] = jnp.stack(
            [
                sums[0],
                gain_two_sum,
                sums[1],
                placed(sums_qkv[:part]),
                placed(sums_qkv[2 * part :]),
                o_sum,
                off_two_sum,
                d_sum,
            ]
        )
        d_sum = d_next
        grads[l] = [up_owned, down_owned, None]

    spots = (jnp.arange(RANKS) == rank)[None, :, None]
    bias = jnp.where(spots, jnp.stack(biases)[:, None, :], 0.0).reshape(layers * RANKS, ff_pad)
    wide = max(ff_pad, width)
    both = jnp.concatenate(
        [
            jnp.pad(jnp.concatenate(vectors), ((0, 0), (0, wide - width))),
            jnp.pad(bias, ((0, 0), (0, wide - ff_pad))),
        ]
    )
    tokens_grad = lax.ppermute(tokens_grad, AXES, back)

    def sum_along(v, axis):
        step = 1
        while step < lax.axis_size(axis):
            v = v + flip(v, axis, step)
            step *= 2
        return v

    both = sum_along(sum_along(both, "c"), "x")
    both, grads[0][0] = tie((both, grads[0][0]))
    both = sum_along(both, "hi")
    mine_last, theirs_last = waiting
    mine_last, both, tokens_grad, homes = tie((mine_last, both, tokens_grad, homes))
    last = scatter_rows(halve_rows(mine_last, theirs_last))
    both = sum_along(both, "seq")
    grads[0][2] = last
    homes[0] = home_of([grads[0][0], grads[0][1], last[:, : 3 * part]])
    results = [[None] * layers for _ in range(4)]
    for l in range(layers):
        owned = grads[l][2]
        results[1][l] = plain_order(owned[:, 3 * part :].reshape(held, width))
        for i in (2, 3):
            home = homes[l][:, :, (i - 2) * ff_pad : (i - 2) * ff_pad + ff_part]
            results[i][l] = home.transpose(1, 0, 2).reshape(held, ff)
        qkv_grad = homes[l][:, :, 2 * ff_pad :]
        qkv_grad = qkv_grad.reshape(RANKS, held, 3, blocks, chunk).transpose(1, 2, 3, 0, 4)
        results[0][l] = qkv_grad.reshape(held, 3 * width)
    results = [jnp.stack(v).astype(f32) for v in results]

    vector = both[: layers * kinds, :width].reshape(layers, kinds, blocks, seqs, RANKS, held)
    for axis, index in ((2, "hi"), (2, "seq")):
        vector = pick(vector, lax.axis_index(index), axis)
    vector = pick(vector, rank, 2).swapaxes(1, 2)
    bias = both[layers * kinds :, :ff_part].reshape(layers, ff)
    return (
        plain_order(output),
        plain_order(tokens_grad),
        *results,
        bias,
        vector[:, :, :2],
        vector[:, :, 2:],
    )


def solution(mesh):
    sizes = mesh.shape
    devices = mesh.devices.reshape(sizes["img"] // RANKS, 2, 2, sizes["seq"])
    fine = Mesh(devices, AXES)
    row = P(AXES, None)
    param = P(None, AXES, None)
    in_specs = (row, row, P(AXES[:3], None), param, param, param, param, P(), param, param)
    out_specs = (row, row, param, param, param, param, P(), param, param)
    return jax.shard_map(
        body, mesh=fine, in_specs=in_specs, out_specs=out_specs, check_vma=False
    )
```

```python
import functools
import math

import jax
import jax.numpy as jnp
from jax import lax
from jax.experimental import pallas as pl
from jax.experimental.pallas import tpu as pltpu
from jax.sharding import Mesh
from jax.sharding import PartitionSpec as P

HEADS = 16
RANKS = 4
CHUNKS = 1
EPSILON = 1e-06
NEGATIVE = -1e30
ROOT = math.sqrt(2.0 / math.pi)
AXES = ("hi", "x", "c", "seq")
SWAP = ((0, 1), (1, 0))
bf16, f32 = jnp.bfloat16, jnp.float32
VMEM = pl.BlockSpec(memory_space=pltpu.VMEM)


def mm(left, right):
    return jnp.dot(left, right, preferred_element_type=f32)


def mm_last(left, right):
    dims = (((1,), (1,)), ((), ()))
    return lax.dot_general(left, right, dims, preferred_element_type=f32)


def mm_first(left, right):
    dims = (((0,), (0,)), ((), ()))
    return lax.dot_general(left, right, dims, preferred_element_type=f32)


def shape(dims, kind):
    return jax.ShapeDtypeStruct(tuple(dims), kind)


def params(mib):
    return pltpu.CompilerParams(vmem_limit_bytes=mib * 2**20)


def cost(flops, moved, exps=0):
    share = 0.14
    return pl.CostEstimate(
        flops=int(share * flops), bytes_accessed=int(share * moved), transcendentals=int(share * exps)
    )


def const(dims):
    return pl.BlockSpec(tuple(dims), lambda i: (0,) * len(dims))


def columns(weight):
    array, width, place = weight
    return pl.BlockSpec((array.shape[0], width), lambda i: (0, place))


def split(half, block, width):
    n = half // block
    own = pl.BlockSpec((block, width), lambda i: (jnp.minimum(i, n - 1), 0))
    rec = pl.BlockSpec((block, width), lambda i: (jnp.maximum(i - n, 0), 0))
    strip = pl.BlockSpec((block, width), lambda i: (i, 0))
    return n, own, rec, strip


def either(own_work, rec_work):
    step, half = pl.program_id(0), pl.num_programs(0) // 2
    pl.when(step < half)(own_work)
    pl.when(step >= half)(rec_work)


def project_kernel(own_ref, rec_ref, w_ref, shift_ref, out_ref):
    width = out_ref.shape[1]

    def work(ref):
        out_ref[...] = (mm(ref[...], w_ref[:, :width]) + shift_ref[...]).astype(bf16)

    either(lambda: work(own_ref), lambda: work(rec_ref))


def project(own, rec, weight, shift):
    half, depth = own.shape
    width = shift.shape[0]
    n, own_spec, rec_spec, _ = split(half, min(half, 256), depth)
    return pl.pallas_call(
        project_kernel,
        grid=(2 * n,),
        in_specs=[own_spec, rec_spec, columns(weight), const((1, width))],
        out_specs=pl.BlockSpec((half // n, width), lambda i: (i, 0)),
        out_shape=shape((2 * half, width), bf16),
        compiler_params=params(24),
        cost_estimate=cost(4 * half * depth * width, 2 * depth * (2 * half + width)),
    )(own, rec, weight[0], shift[None])


def attend_kernel(heads, dim, offset, count, *refs):
    qid_ref, kid_ref, q_ref, wo_ref = refs[:4]
    kv_refs = refs[4 : 4 + count]
    o_ref, total_ref, own_ref, rec_ref = refs[4 + count :]
    factor = dim**-0.5 * math.log2(math.e)
    width = heads * dim
    same = qid_ref[...] == kid_ref[...]

    def scores(h):
        lo = h * dim
        q = q_ref[:, lo : lo + dim]
        k = jnp.concatenate([ref[:, offset + lo : offset + lo + dim] for ref in kv_refs])
        return jnp.where(same, mm_last(q, k), NEGATIVE)

    keys = sum(ref.shape[0] for ref in kv_refs)
    ones = jnp.ones((keys, 8), bf16)
    outs, totals = [], []
    following = scores(0)
    for h in range(heads):
        at = offset + width + h * dim
        v = jnp.concatenate([ref[:, at : at + dim] for ref in kv_refs])
        s = following
        if h < heads - 1:
            following = scores(h + 1)
        top = jnp.max(s, axis=1, keepdims=True)
        p = jnp.exp2((s - top) * factor).astype(bf16)
        o = mm(p, jnp.concatenate([v, ones], axis=1))
        total = o[:, dim : dim + 1]
        outs.append(o[:, :dim] * (1.0 / total))
        totals.append(top * factor + jnp.log2(total))
    o_ref[...] = jnp.concatenate(outs, axis=1).astype(bf16)
    total_ref[...] = jnp.concatenate(totals + totals, axis=1)

    def own_work():
        own_ref[...] = mm(o_ref[...], wo_ref[...])

    def rec_work():
        rec_ref[...] = mm(o_ref[...], wo_ref[...]).astype(bf16)

    either(own_work, rec_work)


def attend(qkv, kvs, offset, query_ids, key_ids, out_full, heads, dim):
    rows, width, wide = qkv.shape[0], heads * dim, out_full.shape[1]
    keys = sum(kv.shape[0] for kv in kvs)
    n, own_spec, rec_spec, _ = split(rows // 2, min(rows // 2, 512 * 1024 // keys), wide)
    block = rows // (2 * n)
    return pl.pallas_call(
        functools.partial(attend_kernel, heads, dim, offset, len(kvs)),
        grid=(2 * n,),
        in_specs=[
            pl.BlockSpec((block, 1), lambda i: (i, 0)),
            const((1, keys)),
            pl.BlockSpec((block, qkv.shape[1]), lambda i: (i, 0)),
            const(out_full.shape),
        ]
        + [const(kv.shape) for kv in kvs],
        out_specs=[
            pl.BlockSpec((block, width), lambda i: (i, 0)),
            pl.BlockSpec((block, 2 * heads), lambda i: (i, 0)),
            own_spec,
            rec_spec,
        ],
        out_shape=[
            shape((rows, width), bf16),
            shape((rows, 2 * heads), f32),
            shape((rows // 2, wide), f32),
            shape((rows // 2, wide), bf16),
        ],
        compiler_params=params(44),
        cost_estimate=cost(10 * rows * keys * width, 16 * rows * width, heads * rows * keys),
    )(query_ids[:, None], key_ids[None, :], qkv, out_full, *kvs)


def attend_back_kernel(heads, dim, offset, count, first, last, *refs):
    qid_ref, kid_ref, q_ref, total_ref, wo_ref, own_ref, rec_ref = refs[:7]
    kv_refs = refs[7 : 7 + count]
    rest = refs[7 + count :]
    if not first:
        before_ref, rest = rest[0], rest[1:]
    dq_ref, dkv_ref, do_ref, acc_ref = rest
    step = pl.program_id(0)
    scale = dim**-0.5
    factor = scale * math.log2(math.e)
    width = heads * dim

    @pl.when(step == 0)
    def _():
        acc_ref[...] = jnp.zeros_like(acc_ref) if first else before_ref[...]

    def own_work():
        do_ref[...] = mm_last(own_ref[...], wo_ref[...]).astype(bf16)

    def rec_work():
        do_ref[...] = mm_last(rec_ref[...], wo_ref[...]).astype(bf16)

    either(own_work, rec_work)
    same = kid_ref[...] == qid_ref[...]
    dqs = []
    for h in range(heads):
        lo = h * dim
        at = offset + width + lo
        q = q_ref[:, lo : lo + dim]
        do = do_ref[:, lo : lo + dim]
        k = jnp.concatenate([ref[:, offset + lo : offset + lo + dim] for ref in kv_refs])
        v = jnp.concatenate([ref[:, at : at + dim] for ref in kv_refs])
        s = jnp.where(same, mm_last(k, q), NEGATIVE)
        p = jnp.exp2(s * factor - total_ref[h : h + 1, :])
        dp = mm_last(v, do)
        delta = jnp.sum(p * dp, axis=0, keepdims=True)
        ds = (p * (dp - delta)).astype(bf16)
        acc_ref[heads + h] += mm(p.astype(bf16), do)
        acc_ref[h] += mm(ds, q)
        dqs.append(mm_first(ds, k) * scale)
    dq_ref[...] = jnp.concatenate(dqs, axis=1).astype(bf16)

    @pl.when(step == pl.num_programs(0) - 1)
    def _():
        if last:
            parts = [acc_ref[h] * scale for h in range(heads)]
            parts += [acc_ref[heads + h] for h in range(heads)]
            dkv_ref[...] = jnp.concatenate(parts, axis=1).astype(bf16)
        else:
            dkv_ref[...] = acc_ref[...]


def attend_back(
    qkv, kvs, offset, query_ids, key_ids, totals, out_full, own, rec, before, last, heads, dim
):
    rows, width, wide = qkv.shape[0], heads * dim, out_full.shape[1]
    keys = sum(kv.shape[0] for kv in kvs)
    sums = (2 * heads, keys, dim)
    extra = [] if before is None else [before]
    n, own_spec, rec_spec, _ = split(rows // 2, min(rows // 2, 512 * 1024 // keys), wide)
    block = rows // (2 * n)
    done = shape((keys, 2 * width), bf16) if last else shape(sums, f32)
    return pl.pallas_call(
        functools.partial(attend_back_kernel, heads, dim, offset, len(kvs), before is None, last),
        grid=(2 * n,),
        in_specs=[
            pl.BlockSpec((1, block), lambda i: (0, i)),
            const((keys, 1)),
            pl.BlockSpec((block, qkv.shape[1]), lambda i: (i, 0)),
            pl.BlockSpec((2 * heads, block), lambda i: (0, i)),
            const(out_full.shape),
            own_spec,
            rec_spec,
        ]
        + [const(v.shape) for v in list(kvs) + extra],
        out_specs=[pl.BlockSpec((block, width), lambda i: (i, 0)), const(done.shape)],
        out_shape=[shape((rows, width), bf16), done],
        scratch_shapes=[pltpu.VMEM((block, width), bf16), pltpu.VMEM(sums, f32)],
        compiler_params=params(52),
        cost_estimate=cost(24 * rows * keys * width, 30 * rows * width, heads * rows * keys),
    )(query_ids[None, :], key_ids[:, None], qkv, totals.T, out_full, own, rec, *kvs, *extra)


def join_kernel(dq_ref, dkv_ref, w_ref, dqkv_ref, own_ref, rec_ref, sum_ref):
    @pl.when(pl.program_id(0) == 0)
    def _():
        sum_ref[...] = jnp.zeros_like(sum_ref)

    dqkv = jnp.concatenate([dq_ref[...], dkv_ref[...]], axis=1)
    dqkv_ref[...] = dqkv
    sum_ref[...] += jnp.sum(dqkv.astype(f32), axis=0, keepdims=True)
    width = dqkv.shape[1]

    def own_work():
        own_ref[...] = mm_last(dqkv_ref[...], w_ref[:, :width])

    def rec_work():
        rec_ref[...] = mm_last(dqkv_ref[...], w_ref[:, :width]).astype(bf16)

    either(own_work, rec_work)


def join(dq, dkv, chunk, weight):
    rows, width, wide = dq.shape[0], dq.shape[1] + dkv.shape[1], weight[0].shape[0]
    n, own_spec, rec_spec, _ = split(rows // 2, min(rows // 2, 256), wide)
    block, at = rows // (2 * n), 2 * n * chunk
    return pl.pallas_call(
        join_kernel,
        grid=(2 * n,),
        in_specs=[
            pl.BlockSpec((block, dq.shape[1]), lambda i: (i, 0)),
            pl.BlockSpec((block, dkv.shape[1]), lambda i: (at + i, 0)),
            columns(weight),
        ],
        out_specs=[pl.BlockSpec((block, width), lambda i: (i, 0)), own_spec, rec_spec, const((1, width))],
        out_shape=[
            shape((rows, width), bf16),
            shape((rows // 2, wide), f32),
            shape((rows // 2, wide), bf16),
            shape((1, width), f32),
        ],
        compiler_params=params(24),
        cost_estimate=cost(2 * rows * width * wide, 4 * wide * (rows + width)),
    )(dq, dkv, weight[0])


def hidden_kernel(own_ref, rec_ref, up_ref, down_ref, shift_ref, slope_ref, act_ref, po_ref, pr_ref):
    def work(ref, out_ref):
        e = mm(ref[...], up_ref[...]) + shift_ref[...]
        square = e * e
        h = 0.5 * jnp.tanh(e * (square * (ROOT * 0.044715) + ROOT)) + 0.5
        g = e * h
        slope = h + g * (1.0 - h) * (square * (6 * ROOT * 0.044715) + 2 * ROOT)
        g = g.astype(bf16)
        act_ref[...] = g
        slope_ref[...] = slope.astype(bf16)
        out_ref[...] = mm_last(g, down_ref[...]).astype(out_ref.dtype)

    either(lambda: work(own_ref, po_ref), lambda: work(rec_ref, pr_ref))


def tile_of(size):
    return 384 if size % 384 == 0 else 128


def hidden(own, rec, up, down, shift):
    half, wide = own.shape
    ff = up[1]
    n, own_spec, rec_spec, _ = split(half, min(half, 256), wide)
    strip = pl.BlockSpec((half // n, ff), lambda i: (i, 0))
    return pl.pallas_call(
        hidden_kernel,
        grid=(2 * n,),
        in_specs=[own_spec, rec_spec, columns(up), columns(down), const((1, ff))],
        out_specs=[strip, strip, own_spec, rec_spec],
        out_shape=[
            shape((2 * half, ff), bf16),
            shape((2 * half, ff), bf16),
            shape((half, wide), f32),
            shape((half, wide), bf16),
        ],
        compiler_params=params(30),
        cost_estimate=cost(8 * half * wide * ff, 4 * wide * ff + 20 * half * wide, 2 * half * ff),
    )(own, rec, up[0], down[0], shift[None])


def hidden_back_kernel(own_ref, rec_ref, slope_ref, up_ref, down_ref, de_ref, sum_ref, po_ref, pr_ref):
    @pl.when(pl.program_id(0) == 0)
    def _():
        sum_ref[...] = jnp.zeros_like(sum_ref)

    def work(ref, out_ref):
        de = (mm(ref[...], down_ref[...]) * slope_ref[...].astype(f32)).astype(bf16)
        de_ref[...] = de
        sum_ref[...] += jnp.sum(de.astype(f32), axis=0, keepdims=True)
        out_ref[...] = mm_last(de, up_ref[...]).astype(out_ref.dtype)

    either(lambda: work(own_ref, po_ref), lambda: work(rec_ref, pr_ref))


def hidden_back(own, rec, slope, up, down):
    half, wide = own.shape
    ff = up[1]
    n, own_spec, rec_spec, _ = split(half, min(half, 256), wide)
    strip = pl.BlockSpec((half // n, ff), lambda i: (i, 0))
    return pl.pallas_call(
        hidden_back_kernel,
        grid=(2 * n,),
        in_specs=[own_spec, rec_spec, strip, columns(up), columns(down)],
        out_specs=[strip, const((1, ff)), own_spec, rec_spec],
        out_shape=[
            shape((2 * half, ff), bf16),
            shape((1, ff), f32),
            shape((half, wide), f32),
            shape((half, wide), bf16),
        ],
        compiler_params=params(30),
        cost_estimate=cost(8 * half * wide * ff, 4 * wide * ff + 16 * half * wide),
    )(own, rec, slope, up[0], down[0])


def outer_kernel(lefts, rights, beside, bit_ref, *refs):
    left_refs, right_refs = refs[:lefts], refs[lefts : lefts + rights]
    rest = refs[lefts + rights :]
    if beside:
        beside_ref, rest = rest[0], rest[1:]
    mine_ref, theirs_ref = rest
    turned = right_refs[0].shape[0]
    cuts = [ref.shape[0] for ref in left_refs]
    total, at = None, 0
    for ref, size in zip(left_refs, cuts):
        low = at % turned
        right = right_refs[at // turned]
        part = mm_first(ref[...], right[low : low + size, :])
        total = part if total is None else total + part
        at += size
    out = total.astype(bf16)
    if beside:
        out = jnp.concatenate([out, beside_ref[...]], axis=1)
    half = out.shape[0] // 2

    @pl.when(bit_ref[0] == 0)
    def _():
        mine_ref[...], theirs_ref[...] = out[:half], out[half:]

    @pl.when(bit_ref[0] == 1)
    def _():
        mine_ref[...], theirs_ref[...] = out[half:], out[:half]


def outer(lefts, rights, bit, beside=None):
    depth, width = lefts[0].shape[1], rights[0].shape[1]
    rows = sum(v.shape[0] for v in lefts)
    extra = [] if beside is None else [beside]
    out = shape((depth // 2, width + sum(v.shape[1] for v in extra)), bf16)
    return pl.pallas_call(
        functools.partial(outer_kernel, len(lefts), len(rights), len(extra)),
        in_specs=[pl.BlockSpec(memory_space=pltpu.SMEM)]
        + [VMEM] * (len(lefts) + len(rights) + len(extra)),
        out_specs=[VMEM] * 2,
        out_shape=[out] * 2,
        compiler_params=params(30),
        cost_estimate=cost(2 * rows * depth * width, 2 * rows * (depth + width) + 2 * depth * width),
    )(bit, *lefts, *rights, *extra)


def outer_out_kernel(count, o_ref, *refs):
    out_ref = refs[count]
    total, at = None, 0
    for ref in refs[:count]:
        part = mm_first(o_ref[at : at + ref.shape[0], :], ref[...])
        total = part if total is None else total + part
        at += ref.shape[0]
    out_ref[...] = total.astype(bf16)


def outer_out(attended, rights):
    depth, width, rows = attended.shape[1], rights[0].shape[1], attended.shape[0]
    return pl.pallas_call(
        functools.partial(outer_out_kernel, len(rights)),
        in_specs=[VMEM] * (1 + len(rights)),
        out_specs=VMEM,
        out_shape=shape((depth, width), bf16),
        compiler_params=params(24),
        cost_estimate=cost(2 * rows * depth * width, 2 * rows * (depth + width) + 2 * depth * width),
    )(attended, *rights)


def spread(v):
    centred = v - jnp.mean(v, axis=-1, keepdims=True)
    scale = lax.rsqrt(jnp.mean(centred * centred, axis=-1, keepdims=True) + EPSILON)
    return centred * scale, scale


def norm_kernel(rows_of, v_ref, q_ref, come_ref, small_ref, next_ref, u_ref, m_ref):
    shift, gain, offset = rows_of
    u = v_ref[...] + (q_ref[...].astype(f32) + come_ref[...].astype(f32) + small_ref[shift : shift + 1, :])
    u_ref[...] = u
    n = spread(u)[0] * next_ref[gain : gain + 1, :] + next_ref[offset : offset + 1, :]
    m_ref[...] = n.astype(bf16)


def add_norm(v, q, come, small, following, rows_of):
    rows, width = v.shape
    block = pl.BlockSpec((min(rows, 256), width), lambda i: (i, 0))
    return pl.pallas_call(
        functools.partial(norm_kernel, rows_of),
        grid=(rows // min(rows, 256),),
        in_specs=[block] * 3 + [const(small.shape)] * 2,
        out_specs=[block] * 2,
        out_shape=[shape(v.shape, f32), shape(v.shape, bf16)],
        compiler_params=params(16),
        cost_estimate=cost(12 * v.size, 14 * v.size),
    )(v, q, come, small, following)


def norm_back_kernel(gain, v_ref, q_ref, come_ref, grad_ref, small_ref, out_ref, round_ref, sum_ref):
    @pl.when(pl.program_id(0) == 0)
    def _():
        sum_ref[...] = jnp.zeros_like(sum_ref)

    t = q_ref[...].astype(f32) + come_ref[...].astype(f32)
    n, scale = spread(v_ref[...])
    w = t * small_ref[gain : gain + 1, :]
    mean_w = jnp.mean(w, axis=-1, keepdims=True)
    mean_wn = jnp.mean(w * n, axis=-1, keepdims=True)
    out = grad_ref[...] + scale * (w - mean_w - n * mean_wn)
    out_ref[...] = out
    rounded = out.astype(bf16)
    round_ref[...] = rounded
    sum_ref[0:1, :] += jnp.sum(t * n, axis=0, keepdims=True)
    sum_ref[1:2, :] += jnp.sum(t, axis=0, keepdims=True)
    sum_ref[2:3, :] += jnp.sum(rounded.astype(f32), axis=0, keepdims=True)


def norm_back(v, q, come, grad, small, gain):
    rows, width = v.shape
    block = pl.BlockSpec((min(rows, 256), width), lambda i: (i, 0))
    return pl.pallas_call(
        functools.partial(norm_back_kernel, gain),
        grid=(rows // min(rows, 256),),
        in_specs=[block] * 4 + [const(small.shape)],
        out_specs=[block] * 2 + [const((8, width))],
        out_shape=[shape(v.shape, f32), shape(v.shape, bf16), shape((8, width), f32)],
        compiler_params=params(20),
        cost_estimate=cost(24 * v.size, 18 * v.size),
    )(v, q, come, grad, small)


def tie(values):
    return lax.optimization_barrier(values)


def pick(array, index, axis=0):
    return lax.dynamic_index_in_dim(array, index, axis, keepdims=False)


def swap_x(v):
    return lax.ppermute(v, "x", SWAP)


def swap_c(v):
    return lax.ppermute(v, "c", SWAP)


def in_order(axis, own, other):
    first = lax.axis_index(axis) == 0
    return jnp.where(first, own, other), jnp.where(first, other, own)


def exchange(blocks):
    xi, ci = lax.axis_index("x"), lax.axis_index("c")
    blocks = blocks.reshape((2, 2) + blocks.shape[1:])
    both = jnp.stack(in_order("x", pick(blocks, xi), swap_x(pick(blocks, 1 - xi))))
    out = in_order("c", pick(both, ci, 1), swap_c(pick(both, 1 - ci, 1)))
    return jnp.stack(out, axis=1).reshape((RANKS,) + blocks.shape[2:])


def flip(v, axis, step):
    size = lax.axis_size(axis)
    return lax.ppermute(v, axis, [(i, i ^ step) for i in range(size)])


def gather_rows(payload):
    return lax.all_gather(payload, ("hi", "seq"), axis=0, tiled=True)


def halve_rows(mine, theirs):
    step = lax.axis_size("hi") // 2
    place = lax.axis_index("hi")
    terms = (mine.astype(f32) + flip(theirs, "hi", step).astype(f32)).astype(bf16)
    step //= 2
    while step:
        halves = terms.reshape((2, -1) + terms.shape[1:])
        bit = (place // step) % 2
        come = flip(pick(halves, 1 - bit), "hi", step)
        terms = (pick(halves, bit).astype(f32) + come.astype(f32)).astype(bf16)
        step //= 2
    return terms


def scatter_rows(terms):
    return lax.psum_scatter(terms, "seq", scatter_dimension=0, tiled=True)


def body(
    tokens,
    cotangent,
    image_lengths,
    qkv_weight,
    out_weight,
    up_weight,
    down_weight,
    up_bias,
    norm_scale,
    shifts,
):
    rows, width = tokens.shape
    layers, held = qkv_weight.shape[0], qkv_weight.shape[1]
    blocks, seqs = lax.axis_size("hi"), lax.axis_size("seq")
    ways = seqs // RANKS
    shards = blocks * seqs
    chunk = seqs * held
    heads = HEADS // RANKS
    dim = width // HEADS
    part = width // RANKS
    ff = up_weight.shape[2]
    ff_part = ff // RANKS
    ff_pad = -(-ff_part // 128) * 128
    xi, ci = lax.axis_index("x"), lax.axis_index("c")
    rank = 2 * xi + ci

    spot = jnp.arange(width, dtype=jnp.int32)
    natural = ((spot // (RANKS * held * seqs) * RANKS + spot // held % RANKS) * seqs) * held
    natural = natural + spot // (RANKS * held) % seqs * held + spot % held
    turn_matrix = (spot[:, None] == natural[None, :]).astype(bf16)

    def mixed_order(v):
        return mm(v, turn_matrix).astype(bf16)

    def plain_order(v):
        return mm_last(v, turn_matrix)

    def mine(v):
        return pick(v.reshape(blocks, seqs, RANKS, held), rank, 2).reshape(part)

    def placed(v):
        v = v.reshape(blocks, seqs, 1, held)
        spots = (jnp.arange(RANKS) == rank)[None, None, :, None]
        return jnp.where(spots, v, 0.0).reshape(width)

    there, spots = [], (0, 3, 1, 2)
    for b in range(blocks):
        for r in range(RANKS):
            for s in range(seqs):
                target = (b * RANKS + s % RANKS) * seqs + spots[r] * ways + s // RANKS
                there.append(((b * RANKS + r) * seqs + s, target))
    back = [(target, source) for source, target in there]

    def rank_columns(piece):
        piece = piece.reshape(held, 3, blocks, RANKS, chunk)
        return piece.transpose(3, 0, 1, 2, 4).reshape(RANKS, held, 3 * part)

    def ff_columns(piece):
        piece = piece.reshape(held, RANKS, ff_part).transpose(1, 0, 2)
        return jnp.pad(piece, ((0, 0), (0, 0), (0, ff_pad - ff_part)))

    def out_rows(l):
        return mixed_order(out_weight[l]).reshape(held * RANKS, part)

    kinds = norm_scale.shape[2] + shifts.shape[2]
    smalls = jnp.concatenate([norm_scale, shifts], axis=2)
    smalls = smalls.transpose(1, 0, 2).reshape(1, held, layers * kinds)
    smalls = jnp.broadcast_to(smalls, (RANKS, held, layers * kinds))

    qkv_fulls, out_fulls, up_fulls, down_fulls = [], [], [], []
    came = exchange(jnp.concatenate([rank_columns(qkv_weight[0]), smalls], axis=2))
    came = came.reshape(RANKS * held, -1)
    payload = jnp.concatenate([came[:, : 3 * part], out_rows(0), came[:, 3 * part :]], axis=1)
    first = gather_rows(payload)
    def ff_pieces(weights):
        return [ff_columns(piece) for piece in weights]

    def pieces_of(weights):
        return [v for i, w in enumerate(weights) for v in (map(ff_columns, w) if i % 2 == 0 else [rank_columns(w)])]

    def payloads_of(weights, l):
        sent = exchange(jnp.concatenate(pieces_of(weights), axis=2)).reshape(RANKS * held, -1)
        payloads, at = [], 0
        for i in range(len(weights)):
            if i % 2 == 0:
                payloads.append(sent[:, at : at + 2 * ff_pad])
                at += 2 * ff_pad
            else:
                l += 1
                columns = sent[:, at : at + 3 * part]
                payloads.append(jnp.concatenate([columns, out_rows(l)], axis=1))
                at += 3 * part
        return payloads

    order = []
    for l in range(layers):
        order += [(up_weight[l], down_weight[l])] + [qkv_weight[i] for i in range(l + 1, min(l + 2, layers))]
    arrived = lax.ppermute(tokens, AXES, there)
    soon, _ = tie((order[:2], payload))
    soon, arrived = tie((soon, arrived))
    soon = payloads_of(soon, 0)
    own = mixed_order(arrived)
    soon, first, starts = tie((soon, first, in_order("x", own, swap_x(own))))
    gathered = [gather_rows(v) for v in soon]

    unit = jnp.eye(layers * kinds, dtype=bf16)
    small_full = mm_last(unit, first[:, width:]).reshape(layers, kinds, width)
    qkv_fulls.append((first, first.shape[1], 0))
    out_fulls.append(first[:, 3 * part : width].reshape(part, width))
    up_shift = pick(up_bias.reshape(layers, RANKS, ff_part), rank, 1).astype(f32)
    up_shift = jnp.pad(up_shift, ((0, 0), (0, ff_pad - ff_part)))

    xs = [(0, 1)] if CHUNKS == 1 else [(0,), (1,)]
    span = 4 * rows // CHUNKS
    lengths = lax.ppermute(image_lengths, AXES, there)
    finish = jnp.cumsum(lengths[0])
    base = jnp.arange(rows, dtype=jnp.int32)
    local = [
        jnp.concatenate([base + (2 * x + c) * rows for c in (ci, 1 - ci) for x in chunk_xs])
        for chunk_xs in xs
    ]
    group = RANKS * rows
    turn = lax.axis_index("seq") % ways

    def ids_of(pos):
        return jnp.sum((pos[:, None] >= finish[None, :]).astype(jnp.int32), axis=1)

    query_ids = [ids_of(v + turn * group) for v in local]
    key_ids = ids_of(jnp.concatenate([v + w * group for v in local for w in range(ways)]))
    seq_groups = [[j * ways + w for w in range(ways)] for j in range(seqs // ways)]

    def keys_of(qkv):
        if ways == 1:
            return qkv, part
        kv = lax.all_gather(
            qkv[:, part:], "seq", axis=0, tiled=True, axis_index_groups=seq_groups
        )
        return kv, 0

    def chunks_of(v):
        own = mixed_order(v)
        pair = in_order("x", own, swap_x(own))
        return list(pair) if CHUNKS == 2 else [jnp.concatenate(pair)]

    def at_x(chunks, index):
        if CHUNKS == 2:
            return jnp.where(index == 0, chunks[0], chunks[1])
        return pick(chunks[0].reshape((2, rows) + chunks[0].shape[1:]), index)

    def core_sum(own, other):
        return (own + swap_c(other).astype(f32)).astype(bf16)

    def last_sum(qs):
        return at_x(qs, xi), swap_x(at_x(qs, 1 - xi))

    GAIN1, GAIN2, OFF1, QB, VB, OB, OFF2, DB = range(8)
    starts = list(starts) if CHUNKS == 2 else [jnp.concatenate(starts)]
    current = [v.astype(f32) for v in starts]
    normed = [
        (spread(v)[0] * small_full[0, GAIN1] + small_full[0, OFF1]).astype(bf16) for v in current
    ]
    saved = []
    output = None
    for l in range(layers):
        if l > 0:
            full = gathered[2 * l - 1]
            qkv_fulls.append((full, width, 0))
            out_fulls.append(full[:, 3 * part :].reshape(part, width))
        up_fulls.append((gathered[2 * l], ff_pad, 0))
        down_fulls.append((gathered[2 * l], ff_pad, 1))
        small = small_full[l]
        attn_in = [(v, swap_c(v)) for v in normed]
        if l == layers - 1:
            attn_in, cotangent = tie((attn_in, cotangent))
            arrived = lax.ppermute(cotangent, AXES, there)
        shift = jnp.concatenate([mine(small[QB]), jnp.zeros((part,), f32), mine(small[VB])])
        qkv = [project(own, rec, qkv_fulls[l], shift) for own, rec in attn_in]
        kvs = [keys_of(v) for v in qkv]
        offset, kvs = kvs[0][1], [v[0] for v in kvs]
        attended, totals, after, normed = [], [], [], []
        for j in range(CHUNKS):
            o, total, own, other = attend(
                qkv[j], kvs, offset, query_ids[j], key_ids, out_fulls[l], heads, dim
            )
            if l == layers - 1 and j == 0:
                o, total, own, other, arrived = tie((o, total, own, other, arrived))
            attended.append(o)
            totals.append(total)
            q = core_sum(own, other)
            if l == 0 and j == 0:
                q, rest = tie((q, order[2:]))
            come = swap_x(q)
            if l == 0 and j == 0:
                come, rest = tie((come, payloads_of(rest, 1)))
                gathered += [gather_rows(v) for v in rest]
            if l == layers - 1 and j == 0:
                come, arrived = tie((come, arrived))
            u, m = add_norm(current[j], q, come, small, small, (OB, GAIN2, OFF2))
            after.append(u)
            normed.append(m)
        mlp_in = [(v, swap_c(v)) for v in normed]
        if l == layers - 1:
            rounded = chunks_of(arrived)
        slopes, acts, qs, following, normed = [], [], [], [], []
        for j in range(CHUNKS):
            slope, act, own, other = hidden(*mlp_in[j], up_fulls[l], down_fulls[l], up_shift[l])
            slopes.append(slope)
            acts.append(act)
            q = core_sum(own, other)
            qs.append(q)
            if l < layers - 1:
                u, m = add_norm(
                    after[j], q, swap_x(q), small, small_full[l + 1], (DB, GAIN1, OFF1)
                )
                following.append(u)
                normed.append(m)
        saved.append((current, attn_in, qkv, kvs, attended, totals, after, mlp_in, slopes, acts))
        current = following
        if l == layers - 1:
            output = (qs, after, small[DB])

    grads = [None] * layers
    vectors = [None] * layers
    biases = [None] * layers
    grad = [v.astype(f32) for v in rounded]
    d_sum = 0.5 * sum(jnp.sum(v, axis=0) for v in grad)
    tokens_grad = None
    top_bit = (lax.axis_index("hi") // (blocks // 2)).astype(jnp.int32)[None]

    def home_of(pieces):
        return exchange(jnp.concatenate(pieces, axis=1).reshape(RANKS, held, -1))


    waiting, homes = None, {}
    for l in reversed(range(layers)):
        (current, attn_in, qkv, kvs, attended, totals, after, mlp_in, slopes, acts) = saved[l]
        small = small_full[l]
        last_layer = waiting is None
        down_in = [(v, swap_c(v)) for v in rounded]
        down_terms = outer([v for pair in down_in for v in pair], acts, top_bit)
        down_in, down_terms = tie((down_in, down_terms))
        des, qs, bias = [], [], 0.0
        for j in range(CHUNKS):
            de, sums, own, other = hidden_back(*down_in[j], slopes[j], up_fulls[l], down_fulls[l])
            des.append(de)
            bias = bias + sums[0]
            qs.append(core_sum(own, other))
        biases[l] = bias
        if last_layer:
            qs, des = tie((qs, des))
        else:
            waiting = halve_rows(*waiting)
            qs, des, waiting = tie((qs, des, waiting))
            waiting = scatter_rows(waiting)
        comes = [swap_x(q) for q in qs]
        up_terms = outer([v for pair in mlp_in for v in pair], des, top_bit)
        down_terms = halve_rows(*down_terms)
        if last_layer:
            comes, down_terms, up_terms, output = tie((comes, down_terms, up_terms, output))
            q, come = last_sum(output[0])
            output = at_x(output[1], xi) + (q.astype(f32) + come.astype(f32) + output[2])
            output = output.astype(bf16)
        else:
            comes, down_terms, up_terms, grads[l + 1][2], output = tie(
                (comes, down_terms, up_terms, waiting, output)
            )
            output = lax.ppermute(output, AXES, back)
        if l > 0:
            down_owned = scatter_rows(down_terms)
        rounded, mid, sums = [], [], 0.0
        for j in range(CHUNKS):
            g, r, s = norm_back(after[j], qs[j], comes[j], grad[j], small, GAIN2)
            mid.append(g)
            rounded.append(r)
            sums = sums + 0.5 * s
        gain_two_sum, off_two_sum, o_sum = sums[0], sums[1], sums[2]
        out_in = [(v, swap_c(v)) for v in rounded]
        acc, dqs = None, []
        for j in range(CHUNKS):
            dq, acc = attend_back(
                qkv[j], kvs, 0 if ways > 1 else part, query_ids[j], key_ids, totals[j],
                out_fulls[l], *out_in[j], acc, j == CHUNKS - 1, heads, dim,
            )
            dqs.append(dq)
        if ways > 1:
            acc = acc.reshape(CHUNKS, ways, span, 2 * part).swapaxes(0, 1)
            acc = lax.psum_scatter(
                acc.reshape(ways * CHUNKS * span, 2 * part),
                "seq",
                scatter_dimension=0,
                tiled=True,
                axis_index_groups=seq_groups,
            )
        if not last_layer:
            dqs, acc, output, down_terms = tie((dqs, acc, output, down_terms))
        dqkvs, qs, sums_qkv = [], [], 0.0
        for j in range(CHUNKS):
            dqkv, own, other, s = join(dqs[j], acc, j, qkv_fulls[l])
            dqkvs.append(dqkv)
            sums_qkv = sums_qkv + s[0]
            qs.append(core_sum(own, other))
        up_terms = halve_rows(*up_terms)
        if last_layer:
            qs, dqkvs, out_in, up_terms, down_owned, output = tie(
                (qs, dqkvs, out_in, up_terms, down_owned, output)
            )
        else:
            down_owned = scatter_rows(down_terms)
            qs, dqkvs, out_in, up_terms = tie((qs, dqkvs, out_in, up_terms))
        up_owned = scatter_rows(up_terms)
        if l > 0:
            comes = [swap_x(q) for q in qs]
        else:
            q, comes = last_sum(qs)
        out_terms = outer_out(
            jnp.concatenate(attended) if CHUNKS > 1 else attended[0],
            [v for pair in out_in for v in pair],
        ).reshape(width, part)
        waiting = outer([v for pair in attn_in for v in pair], dqkvs, top_bit, out_terms)
        if not last_layer:
            grads[l + 1], waiting = tie((grads[l + 1], waiting))
            homes[l + 1] = home_of([grads[l + 1][0], grads[l + 1][1], grads[l + 1][2][:, : 3 * part]])
        if l > 0:
            comes, waiting, up_owned = tie((comes, waiting, up_owned))
        else:
            comes, waiting, down_owned = tie((comes, waiting, down_owned))
        d_next = None
        if l > 0:
            grad, rounded, sums = [], [], 0.0
            for j in range(CHUNKS):
                g, r, s = norm_back(current[j], qs[j], comes[j], mid[j], small, GAIN1)
                grad.append(g)
                rounded.append(r)
                sums = sums + 0.5 * s
            d_next = sums[2]
        else:
            g, r, sums = norm_back(at_x(current, xi), q, comes, at_x(mid, xi), small, GAIN1)
            tokens_grad = r
        vectors[l] = jnp.stack(
            [
                sums[0],
                gain_two_sum,
                sums[1],
                placed(sums_qkv[:part]),
                placed(sums_qkv[2 * part :]),
                o_sum,
                off_two_sum,
                d_sum,
            ]
        )
        d_sum = d_next
        grads[l] = [up_owned, down_owned, None]

    spots = (jnp.arange(RANKS) == rank)[None, :, None]
    bias = jnp.where(spots, jnp.stack(biases)[:, None, :], 0.0).reshape(layers * RANKS, ff_pad)
    wide = max(ff_pad, width)
    both = jnp.concatenate(
        [
            jnp.pad(jnp.concatenate(vectors), ((0, 0), (0, wide - width))),
            jnp.pad(bias, ((0, 0), (0, wide - ff_pad))),
        ]
    )
    tokens_grad = lax.ppermute(tokens_grad, AXES, back)

    def sum_along(v, axis):
        step = 1
        while step < lax.axis_size(axis):
            v = v + flip(v, axis, step)
            step *= 2
        return v

    both = sum_along(sum_along(both, "c"), "x")
    both, grads[0][0] = tie((both, grads[0][0]))
    both = sum_along(both, "hi")
    mine_last, theirs_last = waiting
    mine_last, both, tokens_grad, homes = tie((mine_last, both, tokens_grad, homes))
    last = scatter_rows(halve_rows(mine_last, theirs_last))
    both = sum_along(both, "seq")
    grads[0][2] = last
    homes[0] = home_of([grads[0][0], grads[0][1], last[:, : 3 * part]])
    results = [[None] * layers for _ in range(4)]
    for l in range(layers):
        owned = grads[l][2]
        results[1][l] = plain_order(owned[:, 3 * part :].reshape(held, width))
        for i in (2, 3):
            home = homes[l][:, :, (i - 2) * ff_pad : (i - 2) * ff_pad + ff_part]
            results[i][l] = home.transpose(1, 0, 2).reshape(held, ff)
        qkv_grad = homes[l][:, :, 2 * ff_pad :]
        qkv_grad = qkv_grad.reshape(RANKS, held, 3, blocks, chunk).transpose(1, 2, 3, 0, 4)
        results[0][l] = qkv_grad.reshape(held, 3 * width)
    results = [jnp.stack(v).astype(f32) for v in results]

    vector = both[: layers * kinds, :width].reshape(layers, kinds, blocks, seqs, RANKS, held)
    for axis, index in ((2, "hi"), (2, "seq")):
        vector = pick(vector, lax.axis_index(index), axis)
    vector = pick(vector, rank, 2).swapaxes(1, 2)
    bias = both[layers * kinds :, :ff_part].reshape(layers, ff)
    return (
        plain_order(output),
        plain_order(tokens_grad),
        *results,
        bias,
        vector[:, :, :2],
        vector[:, :, 2:],
    )


def solution(mesh):
    sizes = mesh.shape
    devices = mesh.devices.reshape(sizes["img"] // RANKS, 2, 2, sizes["seq"])
    fine = Mesh(devices, AXES)
    row = P(AXES, None)
    param = P(None, AXES, None)
    in_specs = (row, row, P(AXES[:3], None), param, param, param, param, P(), param, param)
    out_specs = (row, row, param, param, param, param, P(), param, param)
    return jax.shard_map(
        body, mesh=fine, in_specs=in_specs, out_specs=out_specs, check_vma=False
    )
```
